256 devices in a mesh: batch: 8 (over z_lo, y), seq: 32 (over x, z_hi, core).
Axes of the slice: x: 4, y: 4, z: 8 (z_hi: 4, z_lo: 2; z = z_hi * 2 + z_lo), core: 2. Of those that a mesh axis runs over, the one named last changes fastest.
Arguments:
- history: bfloat16 [8, 4096, 1024], P('batch', 'seq'), may hold values from -6 to 6
- candidates: bfloat16 [8, 1024, 1024], P('batch', 'seq'), may hold values from -6 to 6
- event_times: int32 [8, 4096], P('batch', 'seq'), may hold values from 0 to 8382465, as said below
- request_times: int32 [8, 1024], P('batch', 'seq'), may hold values from 8382466 to 8448000, as said below
- w_proj: bfloat16 [1024, 4096], P(None, 'batch'), may hold values from -0.1875 to 0.1875
- w_out: bfloat16 [1024, 1024], P('batch'), may hold values from -0.1875 to 0.1875
- bias_steps: float32 [24, 8], replicated, may hold values from -1 to 1
Outputs:
- history_out: bfloat16 [8, 4096, 1024], P('batch', 'seq')
- cand_out: bfloat16 [8, 1024, 1024], P('batch', 'seq')
The draws below stay inside these ranges and needn't reach their ends.
Inputs may be any that keep to these rules, and one draw needn't show every extreme that they name: `event_times`: Non-decreasing along each user's history; each user's first event is at time 0 and its last at 8382465. `request_times`: every candidate's time is later than all events of its user's history, by 1 to 65535.
All inputs are finite; a program needn't handle non-finite values.
Results may differ from the reference program's by a relative error of at most 0.012.
Values may be sent and summed in bfloat16 or wider, within the bound.
No kernel may reach another device: no remote copies, remote signals or barrier semaphores. Data moves between devices by JAX's collectives and lax.ppermute only.
A program may use at most 128 MiB of HBM per device.

```python
import math
import jax
import jax.numpy as jnp
from jax import lax

D = 1024
HEADS = 8
HEAD_DIM = 128
BUCKETS = 12
USERS = 8
HISTORY = 4096
CANDS = 1024


def clock_helper(key):
    gaps = jax.random.randint(key, (USERS, HISTORY), 0, 2048, dtype=jnp.int32)
    places = jnp.arange(HISTORY, dtype=jnp.int32)[None, :]
    gaps = jnp.where(places > 0, gaps, 0)
    stamps = jnp.cumsum(gaps, axis=1).astype(jnp.int32)
    final_time = jnp.int32(2047) * jnp.int32(HISTORY - 1)
    return jnp.where(places == HISTORY - 1, final_time, stamps).astype(jnp.int32)


def draw_event_times(key, part):
    return clock_helper(key)


def draw_request_times(key, part):
    stamps = clock_helper(key)
    key = jax.random.fold_in(key, 7)
    latest = stamps[:, -1:]
    extra = jax.random.randint(key, (USERS, CANDS), 1, 65536, dtype=jnp.int32)
    slots = jnp.arange(CANDS, dtype=jnp.int32)[None, :]
    extra = jnp.where(slots == 0, jnp.int32(65535), extra)
    extra = jnp.where(slots == 1, jnp.int32(1), extra)
    return (latest + extra).astype(jnp.int32)


def block_scale(rng, dims, cuts, low, top_value):
    level = 1.0
    for position, shards_of in cuts:
        draws = jax.random.uniform(jax.random.fold_in(jax.random.fold_in(rng, 6), position), (shards_of,), jnp.float32, low / len(cuts), top_value / len(cuts))
        level = level * jnp.repeat(jnp.exp(draws), dims[position] // shards_of).reshape((-1,) + (1,) * (len(dims) - 1 - position))
    return level


def normal_values(key, shape, scale, most, pieces=(), kind=jnp.bfloat16):
    array = scale * jax.random.normal(key, shape, jnp.float32)
    if pieces:
        array = array * block_scale(key, shape, pieces, -0.22, 0.18)
    return jnp.clip(array, -most, most).astype(kind)


def setup_inputs(seed: int = 0) -> dict:
    seeds = jax.random.split(jax.random.key(seed), 8)
    return {
        "history": normal_values(seeds[0], (USERS, HISTORY, D), 1.0, 6.0, ((0, 8), (1, 32))),
        "candidates": normal_values(seeds[1], (USERS, CANDS, D), 1.0, 6.0, ((0, 8), (1, 32))),
        "event_times": draw_event_times(jax.random.fold_in(seeds[7], 71), 0),
        "request_times": draw_request_times(jax.random.fold_in(seeds[7], 71), 0),
        "w_proj": normal_values(seeds[4], (D, 4 * HEADS * HEAD_DIM), D ** -0.5, 0.1875, ((1, 8),)),
        "w_out": normal_values(seeds[5], (HEADS * HEAD_DIM, D), (HEADS * HEAD_DIM) ** -0.5, 0.1875, ((0, 8),)),
        "bias_steps": normal_values(seeds[6], (2 * BUCKETS, HEADS), 0.25, 1.0, (), jnp.float32),
    }


def layer_norm(tensor):
    center = lax.optimization_barrier(jnp.mean(tensor, axis=-1, keepdims=True))
    shifted = tensor - center
    spread = lax.optimization_barrier(jnp.mean(shifted * shifted, axis=-1, keepdims=True))
    return shifted * lax.rsqrt(spread + 1e-06)

def pair_bias(query_pos, query_time, key_pos, key_time, bias_steps):
    levels = bias_steps.shape[0] // 2
    steps = bias_steps.astype(jnp.float32)
    time_gap = query_time[:, None] - key_time[None, :]
    place_gap = query_pos[:, None] - key_pos[None, :]
    total = jnp.zeros((steps.shape[1], time_gap.shape[0], time_gap.shape[1]), jnp.float32)
    for level in range(levels):
        time_mark = time_gap >= jnp.int32(4 ** level)
        place_mark = place_gap >= jnp.int32(2 ** level)
        total = total + jnp.where(time_mark[None], steps[level][:, None, None], jnp.float32(0.0))
        total = total + jnp.where(place_mark[None], steps[levels + level][:, None, None], jnp.float32(0.0))
    return total

def attend(queries, keys, values, query_pos, query_time, key_pos, key_time, bias_steps):
    heads = bias_steps.shape[1]
    head_dim = queries.shape[1] // heads
    query_heads = queries.reshape(queries.shape[0], heads, head_dim).astype(jnp.float32)
    key_heads = keys.reshape(keys.shape[0], heads, head_dim).astype(jnp.float32)
    value_heads = values.reshape(values.shape[0], heads, head_dim).astype(jnp.float32)
    scores = jnp.einsum('rhd,khd->hrk', query_heads, key_heads) * head_dim ** (-0.5)
    scores = scores + pair_bias(query_pos, query_time, key_pos, key_time, bias_steps)
    allowed = key_pos[None, :] <= query_pos[:, None]
    weights = jnp.where(allowed[None], jax.nn.silu(scores), 0.0).astype(jnp.bfloat16)
    weights = lax.optimization_barrier(weights).astype(jnp.float32)
    mixed = jnp.einsum('hrk,khd->rhd', weights, value_heads)
    return mixed.reshape(queries.shape[0], heads * head_dim)

def own_term(queries, keys, values, heads):
    head_dim = queries.shape[1] // heads
    query_heads = queries.reshape(queries.shape[0], heads, head_dim).astype(jnp.float32)
    key_heads = keys.reshape(keys.shape[0], heads, head_dim).astype(jnp.float32)
    value_heads = values.reshape(values.shape[0], heads, head_dim).astype(jnp.float32)
    dots = lax.optimization_barrier(jnp.sum(query_heads * key_heads, axis=-1)) * head_dim ** (-0.5)
    weights = lax.optimization_barrier(jax.nn.silu(dots).astype(jnp.bfloat16)).astype(jnp.float32)
    return (weights[:, :, None] * value_heads).reshape(queries.shape[0], heads * head_dim)

def user_layer(hist, cand, etimes, rtimes, w_proj, w_out, bias_steps):
    length = hist.shape[0]
    count = cand.shape[0]
    heads = bias_steps.shape[1]
    width = w_out.shape[0]
    all_rows = jnp.concatenate([hist, cand], axis=0)
    normed = layer_norm(all_rows.astype(jnp.float32)).astype(jnp.bfloat16)
    mixed = jax.nn.silu(jnp.dot(normed, w_proj, preferred_element_type=jnp.float32)).astype(jnp.bfloat16)
    gate = mixed[:, :width]
    values = mixed[:, width:2 * width]
    queries = mixed[:, 2 * width:3 * width]
    keys = mixed[:, 3 * width:]
    query_pos = jnp.concatenate([jnp.arange(length, dtype=jnp.int32), jnp.full((count,), length, jnp.int32)])
    query_time = jnp.concatenate([etimes, rtimes]).astype(jnp.int32)
    key_all_pos = jnp.arange(length, dtype=jnp.int32)
    query_block = math.gcd(length + count, 512)
    key_block = math.gcd(length, 512)

    def one_block(block_index):
        first = block_index * query_block
        block_queries = lax.dynamic_slice_in_dim(queries, first, query_block)
        block_pos = lax.dynamic_slice_in_dim(query_pos, first, query_block)
        block_time = lax.dynamic_slice_in_dim(query_time, first, query_block)

        def key_step(running, key_index):
            key_first = key_index * key_block
            block_keys = lax.dynamic_slice_in_dim(keys, key_first, key_block)
            block_values = lax.dynamic_slice_in_dim(values, key_first, key_block)
            block_key_pos = lax.dynamic_slice_in_dim(key_all_pos, key_first, key_block)
            block_key_time = lax.dynamic_slice_in_dim(etimes, key_first, key_block)
            part = attend(block_queries, block_keys, block_values, block_pos, block_time, block_key_pos, block_key_time, bias_steps)
            return (running + part, None)
        running, _ = lax.scan(key_step, jnp.zeros((query_block, width), jnp.float32), jnp.arange(length // key_block, dtype=jnp.int32))
        return running
    sums = lax.map(one_block, jnp.arange((length + count) // query_block, dtype=jnp.int32))
    sums = sums.reshape(length + count, width)
    own = own_term(queries[length:], keys[length:], values[length:], heads)
    attended = jnp.concatenate([sums[:length], sums[length:] + own], axis=0).astype(jnp.bfloat16)
    gated = (layer_norm(attended.astype(jnp.float32)) * gate.astype(jnp.float32)).astype(jnp.bfloat16)
    result = all_rows.astype(jnp.float32) + jnp.dot(gated, w_out, preferred_element_type=jnp.float32)
    result = result.astype(jnp.bfloat16)
    return (result[:length], result[length:])

def reference(history, candidates, event_times, request_times, w_proj, w_out, bias_steps):

    def one_user(items):
        hist, cand, etimes, rtimes = items
        return user_layer(hist, cand, etimes, rtimes, w_proj, w_out, bias_steps)
    history_out, cand_out = lax.map(one_user, (history, candidates, event_times, request_times))
    return (history_out, cand_out)
```

```python
import functools

import jax
import jax.numpy as jnp
from jax import lax
from jax.experimental import pallas as pl
from jax.experimental.pallas import tpu as pltpu
from jax.sharding import PartitionSpec as P

F32, BF16, I32 = jnp.float32, jnp.bfloat16, jnp.int32
ZL, NY, NX, ZH, NC = 2, 4, 4, 4, 2
NB, NS = ZL * NY, NX * ZH * NC
OFF = (0, -1, 1, 2)
HEADS, HD, D = 8, 128, 1024
HIST, CAND = 128, 32
ROWS = HIST + CAND
NP = ZH * NC
QH, QC = NP * HIST, NP * CAND
QROWS = QH + QC
KEYS = NP * HIST
LENGTH = NS * HIST
LEVELS = 12
MASKED = -1e30
VM = pl.BlockSpec(memory_space=pltpu.VMEM)
SM = pl.BlockSpec(memory_space=pltpu.SMEM)


def params(mib):
    return pltpu.CompilerParams(vmem_limit_bytes=mib << 20)


def seq_perm(dx=0, dz=0, flip=False):
    pairs = []
    for s in range(NS):
        x, z, c = s // (ZH * NC), s // NC % ZH, s % NC
        t = ((x + dx) % NX * ZH + (z + dz) % ZH) * NC + (c ^ int(flip))
        pairs.append((s, t))
    return pairs


def shift(array, dx=0, dz=0, flip=False):
    return lax.ppermute(array, "seq", seq_perm(dx, dz, flip))


def source_perm(dzl=0, dy=0):
    pairs = []
    for b in range(NB):
        zl, y = b // NY, b % NY
        t = (zl + dzl) % ZL * NY + (y + dy) % NY
        for s in range(NS):
            if y % 2 == s // NC % ZH // 2:
                pairs.append((b * NS + s, t * NS + s))
    return pairs


def from_sources(array, dzl=0, dy=0):
    return lax.ppermute(array, ("batch", "seq"), source_perm(dzl, dy))


def norm_kernel(hist_ref, cand_ref, out_ref):
    for ref, first, count in ((hist_ref, 0, HIST), (cand_ref, HIST, CAND)):
        rows = ref[0].astype(F32)
        rows = rows - jnp.mean(rows, axis=-1, keepdims=True)
        spread = jnp.mean(rows * rows, axis=-1, keepdims=True)
        out_ref[first : first + count, :] = (rows * lax.rsqrt(spread + 1e-6)).astype(BF16)


def norm_rows(hist, cand):
    return pl.pallas_call(
        norm_kernel,
        out_shape=jax.ShapeDtypeStruct((ROWS, D), BF16),
        in_specs=[VM, VM],
        out_specs=VM,
        cost_estimate=pl.CostEstimate(flops=8 * ROWS * D, bytes_accessed=4 * ROWS * D, transcendentals=0),
        name="norm_rows",
    )(hist, cand)


def bias_kernel(gap_ref, flat_ref, value_ref, kpos_ref, later_ref, tq_ref, tk_ref, ttab_ref, ptab_ref, hist_ref, cand_ref, col_ref):
    m = pl.program_id(0)
    g = pl.program_id(1)

    @pl.when((m == 0) & (g == 0))
    def _():
        for i in range(QROWS // 128):
            col_ref[i * 128 : (i + 1) * 128, :] = jnp.transpose(jnp.broadcast_to(tq_ref[i : i + 1, :], (128, 128)))

    ttab = jnp.broadcast_to(ttab_ref[0:1, :], (128, 128))
    ptab = jnp.broadcast_to(ptab_ref[0:1, :], (128, 128))
    row = lax.broadcasted_iota(I32, (128, 128), 0)
    lane = lax.broadcasted_iota(I32, (128, 128), 1)

    def time_tile(first, j):
        gap = col_ref[pl.ds(first, 128), :] - tk_ref[0, j : j + 1, :]
        return jnp.take_along_axis(ttab, lax.clz(gap), axis=1)

    for i in range(QC // 128):
        for j in range(4):
            kpos = kpos_ref[m * NP + g * 4 + j]
            gap = (LENGTH - kpos) - lax.broadcasted_iota(I32, (8, 128), 1)
            place = jnp.take_along_axis(ptab[0:8], lax.clz(gap), axis=1)
            cand_ref[i * 128 : (i + 1) * 128, j * 128 : (j + 1) * 128] = time_tile(QH + i * 128, j) + place[0:1, :]

    @pl.when(later_ref[m] == 0)
    def _():
        def hist_block(i, carry):
            first = pl.multiple_of(i * 128, 128)
            at = (i * NX + m) * NP + g * 4
            for j in range(4):
                hist_ref[pl.ds(first, 128), j * 128 : (j + 1) * 128] = time_tile(first, j) + value_ref[at + j]
            for j in range(4):

                @pl.when(flat_ref[at + j] == 0)
                def _():
                    gap = gap_ref[at + j] + row - lane
                    place = jnp.take_along_axis(ptab, lax.clz(gap), axis=1)
                    tile = hist_ref[pl.ds(first, 128), j * 128 : (j + 1) * 128] + place
                    hist_ref[pl.ds(first, 128), j * 128 : (j + 1) * 128] = jnp.where(gap >= 0, tile, MASKED)

            return carry

        lax.fori_loop(0, NP, hist_block, 0)


def make_bias(gap, flat, value, kpos, later, tq, tk, ttab, ptab):
    return pl.pallas_call(
        bias_kernel,
        grid=(NX, 2),
        out_shape=[
            jax.ShapeDtypeStruct((NX, QH, KEYS), F32),
            jax.ShapeDtypeStruct((NX, QC, KEYS), F32),
        ],
        in_specs=[SM] * 5
        + [
            pl.BlockSpec((16, 128), lambda m, g: (0, 0)),
            pl.BlockSpec((1, 4, 128), lambda m, g: (m * 2 + g, 0, 0)),
            pl.BlockSpec((8, 128), lambda m, g: (0, 0)),
            pl.BlockSpec((8, 128), lambda m, g: (0, 0)),
        ],
        out_specs=[
            pl.BlockSpec((None, QH, 512), lambda m, g: (m, 0, g)),
            pl.BlockSpec((None, QC, 512), lambda m, g: (m, 0, g)),
        ],
        scratch_shapes=[pltpu.VMEM((QROWS, 128), I32)],
        compiler_params=params(32),
        cost_estimate=pl.CostEstimate(flops=20 * QROWS * LENGTH, bytes_accessed=4 * QROWS * LENGTH, transcendentals=0),
        name="make_bias",
    )(gap, flat, value, kpos, later, tq, tk, ttab, ptab)


def half_silu(half):
    return half + half * jnp.tanh(half)


def project_kernel(x_ref, n0, n1, n2, n3a, n3b, s0, s1, s2, s3a, s3b, w0, w1, w2, w3a, w3b, q_ref, kv_ref, own_ref, *rest):
    gates, (rows, weights) = rest[:NP], rest[NP:]
    for place, piece in enumerate(((n0,), (n1,), (n2,), (n3a, n3b), (s0,), (s1,), (s2,), (s3a, s3b))):
        if len(piece) == 1:
            rows[place * HIST : (place + 1) * HIST, :] = piece[0][:HIST, :]
            rows[QH + place * CAND : QH + (place + 1) * CAND, :] = piece[0][HIST:, :]
        else:
            half = ROWS // 2
            rows[place * HIST : place * HIST + half, :] = piece[0][...]
            rows[place * HIST + half : (place + 1) * HIST, :] = piece[1][: HIST - half, :]
            rows[QH + place * CAND : QH + (place + 1) * CAND, :] = piece[1][HIST - half :, :]
    depth = D // NX
    for m, part in enumerate((w0, w1, w2)):
        at = pl.multiple_of(x_ref[m] * depth, depth)
        for kind in range(4):
            weights[pl.ds(at, depth), kind * HD : (kind + 1) * HD] = part[kind]
    at = pl.multiple_of(x_ref[3] * depth, depth)
    for kind in range(4):
        weights[pl.ds(at, depth), kind * HD : (kind + 1) * HD] = (w3a, w3b)[kind // 2][kind % 2]
    mixed = jnp.dot(rows[...], weights[:, 2 * HD :], preferred_element_type=F32)
    mixed = half_silu(0.5 * mixed)
    queries, keys = mixed[:, :HD], mixed[:, HD:]
    q_ref[...] = (queries * (0.5 * HD**-0.5)).astype(BF16)
    kv_ref[:, :HD] = keys[:QH].astype(BF16)
    dots = jnp.sum(queries[QH:].astype(BF16).astype(F32) * keys[QH:].astype(BF16).astype(F32), axis=-1, keepdims=True)
    own = half_silu(dots * (0.5 * HD**-0.5)).astype(BF16).astype(F32)
    mixed = jnp.dot(rows[...], weights[:, : 2 * HD], preferred_element_type=F32)
    mixed = half_silu(0.5 * mixed).astype(BF16)
    kv_ref[:, HD:] = mixed[:QH, HD:]
    own_ref[...] = own * mixed[QH:, HD:].astype(F32)
    for place, gate in enumerate(gates):
        gate[:HIST, :] = mixed[place * HIST : (place + 1) * HIST, :HD]
        gate[HIST:, :] = mixed[QH + place * CAND : QH + (place + 1) * CAND, :HD]


def project(x_of, pieces, parts):
    return pl.pallas_call(
        project_kernel,
        out_shape=[
            jax.ShapeDtypeStruct((QROWS, HD), BF16),
            jax.ShapeDtypeStruct((KEYS, 2 * HD), BF16),
            jax.ShapeDtypeStruct((QC, HD), F32),
        ]
        + [jax.ShapeDtypeStruct((ROWS, HD), BF16)] * NP,
        in_specs=[SM] + [VM] * 15,
        out_specs=[VM] * (3 + NP),
        scratch_shapes=[pltpu.VMEM((QROWS, D), BF16), pltpu.VMEM((D, 4 * HD), BF16)],
        compiler_params=params(48),
        cost_estimate=pl.CostEstimate(flops=2 * QROWS * D * 4 * HD, bytes_accessed=6 << 20, transcendentals=QROWS * 4 * HD),
        name="project",
    )(x_of, *pieces, *parts)


def attend_kernel(flag_ref, q_ref, kv_ref, hist_ref, cand_ref, sums_in, sums_ref, *, fresh, block):
    g = pl.program_id(0)

    @pl.when(g == 0)
    def _():
        if fresh:
            sums_ref[:QH, :] = jnp.zeros((QH, HD), F32)
            sums_ref[QH:, :] = sums_in[...]
        else:
            sums_ref[...] = sums_in[...]

    def step(first, count, bias_ref):
        half = lax.dot_general(
            q_ref[first : first + count, :], kv_ref[:, :HD], (((1,), (1,)), ((), ())), preferred_element_type=F32
        )
        weights = half_silu(half + bias_ref[...]).astype(BF16)
        sums_ref[first : first + count, :] += jnp.dot(weights, kv_ref[:, HD:], preferred_element_type=F32)

    step(QH, QC, cand_ref)

    @pl.when(flag_ref[0] == 0)
    def _():
        step(0, QH, hist_ref)


def attend(flag, q, kv, hist_bias, cand_bias, sums, m, first, fresh):
    keys, block = kv.shape[0], 256
    return pl.pallas_call(
        functools.partial(attend_kernel, fresh=fresh, block=block),
        grid_spec=pltpu.PrefetchScalarGridSpec(
            num_scalar_prefetch=1,
            grid=(keys // block,),
            in_specs=[
                pl.BlockSpec((QROWS, HD), lambda g, flag: (0, 0)),
                pl.BlockSpec((block, 2 * HD), lambda g, flag: (g, 0)),
                pl.BlockSpec((None, QH, block), lambda g, flag: (m, 0, jnp.where(flag[0] == 0, first // block + g, 0))),
                pl.BlockSpec((None, QC, block), lambda g, flag: (m, 0, first // block + g)),
                pl.BlockSpec((QC if fresh else QROWS, HD), lambda g, flag: (0, 0)),
            ],
            out_specs=pl.BlockSpec((QROWS, HD), lambda g, flag: (0, 0)),
        ),
        out_shape=jax.ShapeDtypeStruct((QROWS, HD), F32),
        compiler_params=params(40),
        cost_estimate=pl.CostEstimate(
            flops=4 * QROWS * keys * HD, bytes_accessed=4 * QROWS * keys, transcendentals=QROWS * keys
        ),
        name="attend",
    )(flag, q, kv, hist_bias, cand_bias, sums)


def split_kernel(sums_ref, *outs):
    for place, out in enumerate(outs):
        out[:HIST, :] = sums_ref[place * HIST : (place + 1) * HIST, :].astype(BF16)
        out[HIST:, :] = sums_ref[QH + place * CAND : QH + (place + 1) * CAND, :].astype(BF16)


def split_sums(sums):
    return pl.pallas_call(
        split_kernel,
        out_shape=[jax.ShapeDtypeStruct((ROWS, HD), BF16)] * NP,
        in_specs=[VM],
        out_specs=[VM] * NP,
        cost_estimate=pl.CostEstimate(flops=QROWS * HD, bytes_accessed=6 * QROWS * HD, transcendentals=0),
        name="split_sums",
    )(sums)


def finish_kernel(z_ref, core_ref, hist_ref, cand_ref, w_ref, *rest):
    atts, gates, (hist_out, cand_out) = rest[:NP], rest[NP : 2 * NP], rest[2 * NP :]
    parts = [att[...].astype(F32) for att in atts]
    center = sum(jnp.sum(part, axis=-1, keepdims=True) for part in parts) * (1.0 / D)
    parts = [part - center for part in parts]
    spread = sum(jnp.sum(part * part, axis=-1, keepdims=True) for part in parts) * (1.0 / D)
    scale = lax.rsqrt(spread + 1e-6)
    parts = [(part * scale * gate[...].astype(F32)).astype(BF16) for part, gate in zip(parts, gates)]
    total = jnp.zeros((ROWS, D), F32)
    for r in range(ZH):
        mine, other = parts[r], parts[ZH + r]
        first = core_ref[0] == 0
        pair = jnp.concatenate([jnp.where(first, mine, other), jnp.where(first, other, mine)], axis=1)
        at = pl.multiple_of(z_ref[r] * (2 * HD), 2 * HD)
        total = total + jnp.dot(pair, w_ref[pl.ds(at, 2 * HD), :], preferred_element_type=F32)
    hist_out[0] = (hist_ref[0].astype(F32) + total[:HIST]).astype(BF16)
    cand_out[0] = (cand_ref[0].astype(F32) + total[HIST:]).astype(BF16)


def finish(z_from, core, hist, cand, w_out, atts, gates):
    return pl.pallas_call(
        finish_kernel,
        out_shape=[
            jax.ShapeDtypeStruct((1, HIST, D), BF16),
            jax.ShapeDtypeStruct((1, CAND, D), BF16),
        ],
        in_specs=[SM, SM] + [VM] * (3 + 2 * NP),
        out_specs=[VM, VM],
        compiler_params=params(32),
        cost_estimate=pl.CostEstimate(flops=2 * ROWS * D * D, bytes_accessed=4 << 20, transcendentals=0),
        name="finish",
    )(z_from, core, hist, cand, w_out, *atts, *gates)


def gather_weights(w_proj, x, z, core, batch):
    depth = D // NX
    z_lo, y = batch // NY, batch % NY
    head = NC * z + core
    mine = lax.dynamic_slice(w_proj, (x * depth, head % 4 * HD), (depth, HD))
    other = from_sources(mine, dzl=1)
    pair = jnp.stack([mine, other])
    up, down, across = from_sources(pair, dy=1), from_sources(pair, dy=-1), from_sources(pair, dy=2)
    is_source = y % 2 == z // 2
    halves = []
    for f in range(2):
        source = jnp.where(y // 2 == f, pair, across)
        sink = jnp.where((y - 1) % NY // 2 == f, up, down)
        halves.append(jnp.where(is_source, source, sink))
    low = [jnp.where(z_lo == 0, half[0], half[1]) for half in halves]
    high = [jnp.where(z_lo == 0, half[1], half[0]) for half in halves]
    return jnp.stack(low + high)


def body(history, candidates, event_times, request_times, w_proj, w_out, bias_steps):
    seq, batch = lax.axis_index("seq"), lax.axis_index("batch")
    x, z, core = seq // (ZH * NC), seq // NC % ZH, seq % NC
    head = NC * z + core
    zs = jnp.stack([(z + off) % ZH for off in OFF])
    back = jnp.stack([(z - off) % ZH for off in OFF])
    xs = jnp.stack([(x + off) % NX for off in OFF])

    n0 = norm_rows(history, candidates)
    n1, n2 = shift(n0, dz=1), shift(n0, dz=-1)
    half = ROWS // 2
    n3a, n3b = shift(n1[:half], dz=1), shift(n2[half:], dz=-1)
    own = [n0, n1, n2, n3a, n3b]
    pieces = own + [shift(piece, flip=True) for piece in own]

    w0 = gather_weights(w_proj, x, z, core, batch)
    w1, w2 = shift(w0, dx=1), shift(w0, dx=-1)
    w3a, w3b = shift(w1[:2], dx=1), shift(w2[2:], dx=-1)
    w_full = lax.all_gather(w_out, "batch", axis=0, tiled=True)

    t0 = jnp.concatenate([event_times, request_times], axis=1)
    t4 = jnp.concatenate([t0, shift(t0, dz=1), shift(t0, dz=-1), shift(t0, dz=2)], axis=0)
    t8 = jnp.concatenate([t4, shift(t4, flip=True)], axis=0)
    k0 = t8[:, :HIST]
    tk = jnp.stack([k0, shift(k0, dx=1), shift(k0, dx=-1), shift(k0, dx=2)])
    tq = jnp.concatenate([k0, t8[:, HIST:].reshape(QC // 128, 128), jnp.zeros((6, 128), I32)], axis=0)

    places = (zs[None, :] * NC + jnp.stack([core, 1 - core])[:, None]).reshape(NP)
    qpos = (x * NP + places) * HIST
    kpos = (xs[:, None] * NP + places[None, :]) * HIST
    gap = qpos[:, None, None] - kpos[None]
    steps = 0.5 * lax.dynamic_slice(bias_steps, (0, head), (2 * LEVELS, 1))[:, 0]
    bits = 32 - jnp.arange(128, dtype=I32)
    level = jnp.arange(LEVELS, dtype=I32)
    ttab = jnp.sum(jnp.where(bits[None, :] >= 2 * level[:, None] + 1, steps[:LEVELS, None], 0.0), axis=0)
    ptab = jnp.sum(jnp.where(bits[None, :] >= level[:, None] + 1, steps[LEVELS:, None], 0.0), axis=0)
    low, top = gap - (HIST - 1), gap + (HIST - 1)
    marks = 2**level
    flat = (low >= 1) & ~jnp.any((low[..., None] < marks) & (top[..., None] >= marks), axis=-1)
    value = jnp.sum(jnp.where(low[..., None] >= marks, steps[LEVELS:], 0.0), axis=-1)
    value = jnp.where(flat, value, 0.0)
    later = (xs > x).astype(I32)
    hist_bias, cand_bias = make_bias(
        gap.reshape(-1),
        flat.astype(I32).reshape(-1),
        value.reshape(-1),
        kpos.reshape(-1),
        later,
        tq,
        tk.reshape(NX * 2, 4, 128),
        jnp.broadcast_to(ttab, (8, 128)),
        jnp.broadcast_to(ptab, (8, 128)),
    )

    q, kv0, sums, *gates = project(xs, pieces, [w0, w1, w2, w3a, w3b])
    kv1, kv2 = shift(kv0, dx=1), shift(kv0, dx=-1)
    part = KEYS // 2
    kv3a, kv3b = shift(kv1[:part], dx=1), shift(kv2[part:], dx=-1)
    chunks = [(kv0, 0, 0), (kv1, 1, 0), (kv2, 2, 0), (kv3a, 3, 0), (kv3b, 3, part)]
    for kv, m, first in chunks:
        sums = attend(later[m : m + 1], q, kv, hist_bias, cand_bias, sums, m, first, m == 0)

    def send_back(arrays):
        out = []
        for place, array in enumerate(arrays):
            flip, r = place // ZH, place % ZH
            out.append(array if place == 0 else shift(array, dz=OFF[r], flip=bool(flip)))
        return out

    gates = send_back(gates)
    atts = send_back(split_sums(sums))
    return tuple(finish(back, core[None], history, candidates, w_full, atts, gates))


def solution(mesh):
    in_specs = (
        P("batch", "seq", None),
        P("batch", "seq", None),
        P("batch", "seq"),
        P("batch", "seq"),
        P(None, "batch"),
        P("batch", None),
        P(),
    )
    out_specs = (P("batch", "seq", None), P("batch", "seq", None))
    return jax.shard_map(body, mesh=mesh, in_specs=in_specs, out_specs=out_specs, check_vma=False)
```

```python
import functools

import jax
import jax.numpy as jnp
from jax import lax
from jax.experimental import pallas as pl
from jax.experimental.pallas import tpu as pltpu
from jax.sharding import PartitionSpec as P

F32, BF16, I32 = jnp.float32, jnp.bfloat16, jnp.int32
ZL, NY, NX, ZH, NC = 2, 4, 4, 4, 2
NB, NS = ZL * NY, NX * ZH * NC
OFF = (0, -1, 1, 2)
HEADS, HD, D = 8, 128, 1024
HIST, CAND = 128, 32
ROWS = HIST + CAND
NP = ZH * NC
QH, QC = NP * HIST, NP * CAND
QROWS = QH + QC
KEYS = NP * HIST
LENGTH = NS * HIST
LEVELS = 12
MASKED = -1e30
SAME_X = [[x * NP + p for p in range(NP)] for x in range(NX)]
VM = pl.BlockSpec(memory_space=pltpu.VMEM)
SM = pl.BlockSpec(memory_space=pltpu.SMEM)


def params(mib):
    return pltpu.CompilerParams(vmem_limit_bytes=mib << 20)


def seq_perm(dx=0, dz=0, flip=False):
    pairs = []
    for s in range(NS):
        x, z, c = s // (ZH * NC), s // NC % ZH, s % NC
        t = ((x + dx) % NX * ZH + (z + dz) % ZH) * NC + (c ^ int(flip))
        pairs.append((s, t))
    return pairs


def shift(array, dx=0, dz=0, flip=False):
    return lax.ppermute(array, "seq", seq_perm(dx, dz, flip))


def source_perm(dzl=0, dy=0):
    pairs = []
    for b in range(NB):
        zl, y = b // NY, b % NY
        t = (zl + dzl) % ZL * NY + (y + dy) % NY
        for s in range(NS):
            if y % 2 == s // NC % ZH // 2:
                pairs.append((b * NS + s, t * NS + s))
    return pairs


def from_sources(array, dzl=0, dy=0):
    return lax.ppermute(array, ("batch", "seq"), source_perm(dzl, dy))


def norm_kernel(hist_ref, cand_ref, out_ref):
    for ref, first, count in ((hist_ref, 0, HIST), (cand_ref, HIST, CAND)):
        rows = ref[0].astype(F32)
        rows = rows - jnp.mean(rows, axis=-1, keepdims=True)
        spread = jnp.mean(rows * rows, axis=-1, keepdims=True)
        out_ref[first : first + count, :] = (rows * lax.rsqrt(spread + 1e-6)).astype(BF16)


def norm_rows(hist, cand):
    return pl.pallas_call(
        norm_kernel,
        out_shape=jax.ShapeDtypeStruct((ROWS, D), BF16),
        in_specs=[VM, VM],
        out_specs=VM,
        cost_estimate=pl.CostEstimate(flops=8 * ROWS * D, bytes_accessed=4 * ROWS * D, transcendentals=0),
        name="norm_rows",
    )(hist, cand)


def bias_kernel(kpos_ref, flat_ref, value_ref, later_ref, tq_ref, tk_ref, ttab_ref, ptab_ref, out_ref, col_ref, *, fresh):
    for i in range(QROWS // 128):
        col_ref[i * 128 : (i + 1) * 128, :] = jnp.transpose(jnp.broadcast_to(tq_ref[i : i + 1, :], (128, 128)))
    ttab = jnp.broadcast_to(ttab_ref[0:1, :], (128, 128))
    ptab = jnp.broadcast_to(ptab_ref[0:1, :], (128, 128))
    row = lax.broadcasted_iota(I32, (128, 128), 0)
    lane = lax.broadcasted_iota(I32, (128, 128), 1)

    def time_tile(first, j):
        gap = col_ref[pl.ds(first, 128), :] - tk_ref[j : j + 1, :]
        return jnp.take_along_axis(ttab, lax.clz(gap), axis=1)

    for i in range(QC // 128):
        for j in range(NP):
            gap = (LENGTH - kpos_ref[0] - j * HIST) - lax.broadcasted_iota(I32, (8, 128), 1)
            place = jnp.take_along_axis(ptab[0:8], lax.clz(gap), axis=1)
            out_ref[QH + i * 128 : QH + (i + 1) * 128, j * 128 : (j + 1) * 128] = time_tile(QH + i * 128, j) + place[0:1, :]

    @pl.when(later_ref[0] == 0)
    def _():
        def hist_block(i, carry):
            first = pl.multiple_of(i * 128, 128)
            for j in range(NP):
                at = kpos_ref[1] + i - j + NP - 1
                out_ref[pl.ds(first, 128), j * 128 : (j + 1) * 128] = time_tile(first, j) + value_ref[at]
            for j in range(NP):
                at = kpos_ref[1] + i - j + NP - 1

                @pl.when(flat_ref[at] == 0)
                def _():
                    gap = (at - (NP - 1)) * HIST + row - lane
                    place = jnp.take_along_axis(ptab, lax.clz(gap), axis=1)
                    tile = out_ref[pl.ds(first, 128), j * 128 : (j + 1) * 128] + place
                    out_ref[pl.ds(first, 128), j * 128 : (j + 1) * 128] = jnp.where(gap >= 0, tile, MASKED)

            return carry

        lax.fori_loop(0, NP, hist_block, 0)


def make_bias(kpos, flat, value, later, tq, tk, ttab, ptab):
    return pl.pallas_call(
        functools.partial(bias_kernel, fresh=True),
        out_shape=jax.ShapeDtypeStruct((QROWS, KEYS), F32),
        in_specs=[SM] * 4 + [VM] * 4,
        out_specs=VM,
        scratch_shapes=[pltpu.VMEM((QROWS, 128), I32)],
        compiler_params=params(20),
        cost_estimate=pl.CostEstimate(flops=2000 * QROWS * KEYS, bytes_accessed=4 * QROWS * KEYS, transcendentals=0),
        name="make_bias",
    )(kpos, flat, value, later, tq, tk, ttab, ptab)


def half_silu(half):
    return half + half * jnp.tanh(half)


def project_kernel(x_ref, tie_ref, rows_ref, wout_ref, w0, w1, w2, w3a, w3b, q_ref, kv_ref, own_ref, gate_ref, wout_out, rows, weights):
    for place in range(NP):
        rows[place * HIST : (place + 1) * HIST, :] = rows_ref[place, :HIST, :]
        rows[QH + place * CAND : QH + (place + 1) * CAND, :] = rows_ref[place, HIST:, :]
    wout_out[...] = wout_ref[...]
    depth = D // NX
    for m, part in enumerate((w0, w1, w2)):
        at = pl.multiple_of(x_ref[m] * depth, depth)
        for kind in range(4):
            weights[pl.ds(at, depth), kind * HD : (kind + 1) * HD] = part[kind]
    at = pl.multiple_of(x_ref[3] * depth, depth)
    for kind in range(4):
        weights[pl.ds(at, depth), kind * HD : (kind + 1) * HD] = (w3a, w3b)[kind // 2][kind % 2]
    mixed = jnp.dot(rows[...], weights[:, 2 * HD :], preferred_element_type=F32)
    mixed = half_silu(0.5 * mixed)
    queries, keys = mixed[:, :HD], mixed[:, HD:]
    q_ref[...] = (queries * (0.5 * HD**-0.5)).astype(BF16)
    kv_ref[:, :HD] = keys[:QH].astype(BF16)
    dots = jnp.sum(queries[QH:].astype(BF16).astype(F32) * keys[QH:].astype(BF16).astype(F32), axis=-1, keepdims=True)
    own = half_silu(dots * (0.5 * HD**-0.5)).astype(BF16).astype(F32)
    mixed = jnp.dot(rows[...], weights[:, : 2 * HD], preferred_element_type=F32)
    mixed = half_silu(0.5 * mixed).astype(BF16)
    kv_ref[:, HD:] = mixed[:QH, HD:]
    own_ref[...] = own * mixed[QH:, HD:].astype(F32)
    for place in range(NP):
        gate_ref[place, :HIST, :] = mixed[place * HIST : (place + 1) * HIST, :HD]
        gate_ref[place, HIST:, :] = mixed[QH + place * CAND : QH + (place + 1) * CAND, :HD]


def project(x_of, tie, rows, w_out, parts):
    return pl.pallas_call(
        project_kernel,
        out_shape=[
            jax.ShapeDtypeStruct((QROWS, HD), BF16),
            jax.ShapeDtypeStruct((KEYS, 2 * HD), BF16),
            jax.ShapeDtypeStruct((QC, HD), F32),
            jax.ShapeDtypeStruct((NP, ROWS, HD), BF16),
            jax.ShapeDtypeStruct(w_out.shape, BF16),
        ],
        in_specs=[SM, pl.BlockSpec(memory_space=pl.ANY)] + [VM] * 7,
        out_specs=[VM] * 5,
        scratch_shapes=[pltpu.VMEM((QROWS, D), BF16), pltpu.VMEM((D, 4 * HD), BF16)],
        compiler_params=params(32),
        cost_estimate=pl.CostEstimate(flops=2 * QROWS * D * 4 * HD, bytes_accessed=6 << 20, transcendentals=QROWS * 4 * HD),
        name="project",
    )(x_of, tie, rows, w_out, *parts)


def attend_kernel(flag_ref, tie_ref, q_ref, sums_in, *rest, fresh, last, counts):
    kvs, biases, (out_ref, sums_ref) = rest[: len(counts)], rest[len(counts) : -2], rest[-2:]
    if fresh:
        sums_ref[:QH, :] = jnp.zeros((QH, HD), F32)
        sums_ref[QH:, :] = sums_in[...]
    else:
        sums_ref[...] = sums_in[...]

    def step(n, first, count):
        bias_ref, begin = biases[counts[n][1]], counts[n][2]
        for piece in range(0, count, 256):
            at = first + piece
            half = lax.dot_general(
                q_ref[at : at + 256, :], kvs[n][:, :HD], (((1,), (1,)), ((), ())), preferred_element_type=F32
            )
            weights = half_silu(half + bias_ref[at : at + 256, begin : begin + counts[n][0]]).astype(BF16)
            sums_ref[at : at + 256, :] += jnp.dot(weights, kvs[n][:, HD:], preferred_element_type=F32)

    for n in range(len(counts)):
        step(n, QH, QC)

        @pl.when(flag_ref[counts[n][1]] == 0)
        def _():
            step(n, 0, QH)

    if last:
        for place in range(NP):
            out_ref[place, :HIST, :] = sums_ref[place * HIST : (place + 1) * HIST, :].astype(BF16)
            out_ref[place, HIST:, :] = sums_ref[QH + place * CAND : QH + (place + 1) * CAND, :].astype(BF16)
    else:
        out_ref[...] = sums_ref[...]


def attend(flags, tie, q, sums, kvs, biases, counts, fresh=False, last=False):
    keys = sum(count[0] for count in counts)
    return pl.pallas_call(
        functools.partial(attend_kernel, fresh=fresh, last=last, counts=counts),
        in_specs=[SM, pl.BlockSpec(memory_space=pl.ANY)] + [VM] * (2 + len(kvs) + len(biases)),
        out_specs=VM,
        out_shape=jax.ShapeDtypeStruct((NP, ROWS, HD), BF16) if last else jax.ShapeDtypeStruct((QROWS, HD), F32),
        scratch_shapes=[pltpu.VMEM((QROWS, HD), F32)],
        compiler_params=params(24),
        cost_estimate=pl.CostEstimate(
            flops=8 * QROWS * keys * HD, bytes_accessed=4 * QROWS * keys, transcendentals=QROWS * keys
        ),
        name="attend",
    )(flags, tie, q, sums, *kvs, *biases)


def finish_kernel(hist_ref, cand_ref, w_ref, att_ref, gate_ref, hist_out, cand_out):
    parts = [att_ref[h].astype(F32) for h in range(HEADS)]
    center = sum(jnp.sum(part, axis=-1, keepdims=True) for part in parts) * (1.0 / D)
    parts = [part - center for part in parts]
    spread = sum(jnp.sum(part * part, axis=-1, keepdims=True) for part in parts) * (1.0 / D)
    scale = lax.rsqrt(spread + 1e-6)
    parts = [(part * scale * gate_ref[h].astype(F32)).astype(BF16) for h, part in enumerate(parts)]
    total = jnp.dot(jnp.concatenate(parts, axis=1), w_ref[...], preferred_element_type=F32)
    hist_out[0] = (hist_ref[0].astype(F32) + total[:HIST]).astype(BF16)
    cand_out[0] = (cand_ref[0].astype(F32) + total[HIST:]).astype(BF16)


def finish(hist, cand, w_out, att, gate):
    return pl.pallas_call(
        finish_kernel,
        out_shape=[
            jax.ShapeDtypeStruct((1, HIST, D), BF16),
            jax.ShapeDtypeStruct((1, CAND, D), BF16),
        ],
        in_specs=[VM] * 5,
        out_specs=[VM, VM],
        compiler_params=params(24),
        cost_estimate=pl.CostEstimate(flops=2 * ROWS * D * D, bytes_accessed=4 << 20, transcendentals=0),
        name="finish",
    )(hist, cand, w_out, att, gate)


def gather_weights(w_proj, x, z, core, batch):
    depth = D // NX
    z_lo, y = batch // NY, batch % NY
    head = NC * z + core
    mine = lax.dynamic_slice(w_proj, (x * depth, head % 4 * HD), (depth, HD))
    other = from_sources(mine, dzl=1)
    pair = jnp.stack([mine, other])
    up, down, across = from_sources(pair, dy=1), from_sources(pair, dy=-1), from_sources(pair, dy=2)
    is_source = y % 2 == z // 2
    halves = []
    for f in range(2):
        source = jnp.where(y // 2 == f, pair, across)
        sink = jnp.where((y - 1) % NY // 2 == f, up, down)
        halves.append(jnp.where(is_source, source, sink))
    low = [jnp.where(z_lo == 0, half[0], half[1]) for half in halves]
    high = [jnp.where(z_lo == 0, half[1], half[0]) for half in halves]
    return jnp.stack(low + high)


def body(history, candidates, event_times, request_times, w_proj, w_out, bias_steps):
    seq, batch = lax.axis_index("seq"), lax.axis_index("batch")
    x, z, core = seq // (ZH * NC), seq // NC % ZH, seq % NC
    head = NC * z + core
    zs = [(z + off) % ZH for off in OFF]
    xs = jnp.stack([(x + off) % NX for off in OFF])

    rows = lax.all_gather(norm_rows(history, candidates), "seq", axis_index_groups=SAME_X)

    t0 = jnp.concatenate([event_times, request_times], axis=1)
    near = [t0, shift(t0, dz=1), shift(t0, dz=-1), shift(t0, dz=2)]
    t4 = jnp.concatenate([sum(jnp.where(zs[r] == j, near[r], 0) for r in range(ZH)) for j in range(ZH)], axis=0)
    other = shift(t4, flip=True)
    t8 = jnp.stack([jnp.where(core == 0, t4, other), jnp.where(core == 0, other, t4)], axis=1).reshape(NP, ROWS)
    k0 = t8[:, :HIST]
    tk = [k0, shift(k0, dx=1), shift(k0, dx=-1), shift(k0, dx=2)]
    tq = jnp.concatenate([k0, t8[:, HIST:].reshape(QC // 128, 128), jnp.zeros((6, 128), I32)], axis=0)

    w0 = gather_weights(w_proj, x, z, core, batch)
    w1, w2 = shift(w0, dx=1), shift(w0, dx=-1)
    w3a, w3b = shift(w1[:2], dx=1), shift(w2[2:], dx=-1)

    steps = 0.5 * lax.dynamic_slice(bias_steps, (0, head), (2 * LEVELS, 1))[:, 0]
    bits = 32 - jnp.arange(128, dtype=I32)
    level = jnp.arange(LEVELS, dtype=I32)
    ttab = jnp.sum(jnp.where(bits[None, :] >= 2 * level[:, None] + 1, steps[:LEVELS, None], 0.0), axis=0)
    ptab = jnp.sum(jnp.where(bits[None, :] >= level[:, None] + 1, steps[LEVELS:, None], 0.0), axis=0)
    ttab, ptab = jnp.broadcast_to(ttab, (8, 128)), jnp.broadcast_to(ptab, (8, 128))
    gap = (jnp.arange(NS + NP, dtype=I32) - (NP - 1)) * HIST
    low, top = gap - (HIST - 1), gap + (HIST - 1)
    marks = 2**level
    flat = (low >= 1) & ~jnp.any((low[:, None] < marks) & (top[:, None] >= marks), axis=-1)
    value = jnp.sum(jnp.where(low[:, None] >= marks, steps[LEVELS:], 0.0), axis=-1)
    value = jnp.where(flat, value, 0.0)
    later = (xs > x).astype(I32)
    biases = [
        make_bias(
            jnp.stack([xs[m] * KEYS, (x - xs[m]) * NP]), flat.astype(I32), value, later[m : m + 1], tq, tk[m], ttab, ptab
        )
        for m in range(NX)
    ]

    q, kv0, own, gate, w_mine = project(xs, biases[3], rows, w_out, [w0, w1, w2, w3a, w3b])
    w_full = lax.all_gather(w_mine, "batch", axis=0, tiled=True)
    kv1, kv2 = shift(kv0, dx=1), shift(kv0, dx=-1)
    part = KEYS // 2
    kv3a, kv3b = shift(kv1[:part], dx=1), shift(kv2[part:], dx=-1)
    gates = lax.all_to_all(gate, "seq", 0, 0, axis_index_groups=SAME_X)
    sums = attend(later[:1], q, q, own, [kv0], biases[:1], ((KEYS, 0, 0),), fresh=True)
    sums = attend(later[1:3], gates, q, sums, [kv1, kv2], biases[1:3], ((KEYS, 0, 0), (KEYS, 1, 0)))
    att = attend(later[3:], q, q, sums, [kv3a, kv3b], biases[3:], ((part, 0, 0), (part, 0, part)), last=True)
    atts = lax.all_to_all(att, "seq", 0, 0, axis_index_groups=SAME_X)
    return tuple(finish(history, candidates, w_full, atts, gates))


def solution(mesh):
    in_specs = (
        P("batch", "seq", None),
        P("batch", "seq", None),
        P("batch", "seq"),
        P("batch", "seq"),
        P(None, "batch"),
        P("batch", None),
        P(),
    )
    out_specs = (P("batch", "seq", None), P("batch", "seq", None))
    return jax.shard_map(body, mesh=mesh, in_specs=in_specs, out_specs=out_specs, check_vma=False)
```

```python
import functools

import jax
import jax.numpy as jnp
from jax import lax
from jax.experimental import pallas as pl
from jax.experimental.pallas import tpu as pltpu
from jax.sharding import PartitionSpec as P

F32, BF16, I32 = jnp.float32, jnp.bfloat16, jnp.int32
ZL, NY, NX, ZH, NC = 2, 4, 4, 4, 2
NB, NS = ZL * NY, NX * ZH * NC
OFF = (0, -1, 1, 2)
HEADS, HD, D = 8, 128, 1024
HIST, CAND = 128, 32
ROWS = HIST + CAND
NP = ZH * NC
QH, QC = NP * HIST, NP * CAND
QROWS = QH + QC
KEYS = NP * HIST
LENGTH = NS * HIST
LEVELS = 12
MASKED = -1e30
SAME_X = [[x * NP + p for p in range(NP)] for x in range(NX)]
VM = pl.BlockSpec(memory_space=pltpu.VMEM)
SM = pl.BlockSpec(memory_space=pltpu.SMEM)


def params(mib):
    return pltpu.CompilerParams(vmem_limit_bytes=mib << 20)


def seq_perm(dx=0, dz=0, flip=False):
    pairs = []
    for s in range(NS):
        x, z, c = s // (ZH * NC), s // NC % ZH, s % NC
        t = ((x + dx) % NX * ZH + (z + dz) % ZH) * NC + (c ^ int(flip))
        pairs.append((s, t))
    return pairs


def shift(array, dx=0, dz=0, flip=False):
    return lax.ppermute(array, "seq", seq_perm(dx, dz, flip))


def source_perm(dzl=0, dy=0):
    pairs = []
    for b in range(NB):
        zl, y = b // NY, b % NY
        t = (zl + dzl) % ZL * NY + (y + dy) % NY
        for s in range(NS):
            if y % 2 == s // NC % ZH // 2:
                pairs.append((b * NS + s, t * NS + s))
    return pairs


def from_sources(array, dzl=0, dy=0):
    return lax.ppermute(array, ("batch", "seq"), source_perm(dzl, dy))


def norm_kernel(hist_ref, cand_ref, events_ref, requests_ref, out_ref, times_ref):
    for ref, first, count in ((hist_ref, 0, HIST), (cand_ref, HIST, CAND)):
        rows = ref[0].astype(F32)
        rows = rows - jnp.mean(rows, axis=-1, keepdims=True)
        spread = jnp.mean(rows * rows, axis=-1, keepdims=True)
        out_ref[first : first + count, :] = (rows * lax.rsqrt(spread + 1e-6)).astype(BF16)
    times_ref[...] = jnp.zeros_like(times_ref)
    times_ref[:, :HIST] = events_ref[...]
    times_ref[:, HIST:ROWS] = requests_ref[...]


def norm_rows(hist, cand, events, requests):
    return pl.pallas_call(
        norm_kernel,
        out_shape=[jax.ShapeDtypeStruct((ROWS, D), BF16), jax.ShapeDtypeStruct((1, 2 * HIST), I32)],
        in_specs=[VM] * 4,
        out_specs=[VM] * 2,
        cost_estimate=pl.CostEstimate(flops=8 * ROWS * D, bytes_accessed=4 * ROWS * D, transcendentals=0),
        name="norm_rows",
    )(hist, cand, events, requests)


def prepare_kernel(tq_ref, wout_ref, col_ref, wout_out):
    for i in range(QROWS // 128):
        col_ref[i * 128 : (i + 1) * 128, :] = jnp.transpose(jnp.broadcast_to(tq_ref[i : i + 1, :], (128, 128)))
    wout_out[...] = wout_ref[...]


def prepare(tq, w_out):
    return pl.pallas_call(
        prepare_kernel,
        out_shape=[jax.ShapeDtypeStruct((QROWS, 128), I32), jax.ShapeDtypeStruct(w_out.shape, BF16)],
        in_specs=[VM] * 2,
        out_specs=[VM] * 2,
        cost_estimate=pl.CostEstimate(flops=2 << 20, bytes_accessed=1 << 20, transcendentals=0),
        name="prepare",
    )(tq, w_out)


def half_silu(half):
    return half + half * jnp.tanh(half)


def project_kernel(core_ref, *refs):
    pieces, weights = refs[:NP], refs[NP]
    q_ref, kv_ref, own_ref, gate_ref, rows = refs[NP + 1 :]
    for r in range(ZH):
        for c in range(NC):
            place = core_ref[1 + r] * NC + (core_ref[0] ^ c)
            piece = pieces[c * ZH + r]
            rows[pl.ds(pl.multiple_of(place * HIST, HIST), HIST), :] = piece[:HIST, :]
            rows[pl.ds(pl.multiple_of(QH + place * CAND, CAND), CAND), :] = piece[HIST:, :]
    mixed = jnp.dot(rows[...], weights[:, 2 * HD :], preferred_element_type=F32)
    mixed = half_silu(0.5 * mixed)
    queries, keys = mixed[:, :HD], mixed[:, HD:]
    q_ref[...] = (queries * (0.5 * HD**-0.5)).astype(BF16)
    kv_ref[:, :HD] = keys[:QH].astype(BF16)
    dots = jnp.sum(queries[QH:].astype(BF16).astype(F32) * keys[QH:].astype(BF16).astype(F32), axis=-1, keepdims=True)
    own = half_silu(dots * (0.5 * HD**-0.5)).astype(BF16).astype(F32)
    mixed = jnp.dot(rows[...], weights[:, : 2 * HD], preferred_element_type=F32)
    mixed = half_silu(0.5 * mixed).astype(BF16)
    kv_ref[:, HD:] = mixed[:QH, HD:]
    own_ref[...] = own * mixed[QH:, HD:].astype(F32)
    for place in range(NP):
        gate_ref[place, :HIST, :] = mixed[place * HIST : (place + 1) * HIST, :HD]
        gate_ref[place, HIST:, :] = mixed[QH + place * CAND : QH + (place + 1) * CAND, :HD]


def project(where, pieces, w_head):
    return pl.pallas_call(
        project_kernel,
        out_shape=[
            jax.ShapeDtypeStruct((QROWS, HD), BF16),
            jax.ShapeDtypeStruct((KEYS, 2 * HD), BF16),
            jax.ShapeDtypeStruct((QC, HD), F32),
            jax.ShapeDtypeStruct((NP, ROWS, HD), BF16),
        ],
        in_specs=[SM] + [VM] * (NP + 1),
        out_specs=[VM] * 4,
        scratch_shapes=[pltpu.VMEM((QROWS, D), BF16)],
        compiler_params=params(14),
        cost_estimate=pl.CostEstimate(flops=2 * QROWS * D * 4 * HD, bytes_accessed=6 << 20, transcendentals=QROWS * 4 * HD),
        name="project",
    )(where, *pieces, w_head)


BLOCK = 256
TILES = (QROWS // 128) * NP


def attend_kernel(flag_ref, code_ref, base_ref, apart_ref, steps_ref, tie_ref, q_ref, sums_in, col_ref, *rest, fresh, last, chunks):
    arrays = sum(len(chunk) for chunk in chunks)
    kvs, tks = list(rest[:arrays]), rest[arrays : arrays + len(chunks)]
    out_ref, sums_ref, half_ref = rest[arrays + len(chunks) :]
    if fresh:
        sums_ref[:QH, :] = jnp.zeros((QH, HD), F32)
        sums_ref[QH:, :] = sums_in[...]
    else:
        sums_ref[...] = sums_in[...]
    row = lax.broadcasted_iota(I32, (128, 128), 0)
    lane = lax.broadcasted_iota(I32, (128, 128), 1)

    def scores(n, block, slot):
        first = block * BLOCK
        begin = 0
        for kv in parts[n]:
            keys = kv.shape[0]
            half = lax.dot_general(
                q_ref[first : first + BLOCK, :], kv[:, :HD], (((1,), (1,)), ((), ())), preferred_element_type=F32
            )
            for i in range(BLOCK // 128):
                for j in range(keys // 128):
                    at = n * TILES + (block * (BLOCK // 128) + i) * NP + begin // 128 + j
                    half_ref[slot, i * 128 : (i + 1) * 128, begin + j * 128 : begin + (j + 1) * 128] = (
                        half[i * 128 : (i + 1) * 128, j * 128 : (j + 1) * 128] + base_ref[at]
                    )
            begin += keys

    def correct(n, block, slot):
        is_cand = block * BLOCK >= QH

        def tile(t, carry):
            i, j = t // NP, t % NP
            at = n * TILES + (block * (BLOCK // 128)) * NP + t
            code = code_ref[at]
            time_low, time_high, place_low, place_high = (code & 15, (code >> 4) & 15, (code >> 8) & 15, (code >> 12) & 15)

            @pl.when((time_low != time_high) | (place_low != place_high))
            def _():
                rows = pl.ds(pl.multiple_of(i * 128, 128), 128)
                columns = pl.ds(pl.multiple_of(j * 128, 128), 128)
                first = pl.multiple_of(block * BLOCK + i * 128, 128)
                value = half_ref[slot, rows, columns]
                gap = col_ref[pl.ds(first, 128), :] - tks[n][pl.ds(j, 1), :]

                def time_step(level, value):
                    return value + jnp.where(gap >= (1 << (2 * level)), steps_ref[level], 0.0)

                value = lax.fori_loop(time_low, time_high, time_step, value)
                if is_cand:
                    gap2 = (LENGTH - apart_ref[NX + n] - j * 128) - lane
                else:
                    gap2 = (apart_ref[n] + (block * (BLOCK // 128) + i - j) * 128) + row - lane

                def place_step(level, value):
                    return value + jnp.where(gap2 >= (1 << level), steps_ref[LEVELS + level], 0.0)

                value = lax.fori_loop(place_low, place_high, place_step, value)
                if not is_cand:
                    value = jnp.where(gap2 >= 0, value, MASKED)
                half_ref[slot, rows, columns] = value

            return carry

        lax.fori_loop(0, BLOCK // 128 * NP, tile, 0)

    def combine(n, block, slot):
        first = block * BLOCK
        begin = 0
        total = sums_ref[first : first + BLOCK, :]
        for kv in parts[n]:
            keys = kv.shape[0]
            weights = half_silu(half_ref[slot, :, begin : begin + keys]).astype(BF16)
            total = total + jnp.dot(weights, kv[:, HD:], preferred_element_type=F32)
            begin += keys
        sums_ref[first : first + BLOCK, :] = total

    def sweep(n, blocks):
        for k, block in enumerate(blocks):
            scores(n, block, k % 2)
            if k > 0:
                combine(n, blocks[k - 1], (k - 1) % 2)
            correct(n, block, k % 2)
        combine(n, blocks[-1], (len(blocks) - 1) % 2)

    parts = []
    for chunk in chunks:
        parts.append([kvs.pop(0) for _ in chunk])
    for n in range(len(chunks)):

        @pl.when(flag_ref[n] == 0)
        def _():
            sweep(n, list(range(QROWS // BLOCK)))

        @pl.when(flag_ref[n] != 0)
        def _():
            sweep(n, [QROWS // BLOCK - 1])

    if last:
        for place in range(NP):
            out_ref[place, :HIST, :] = sums_ref[place * HIST : (place + 1) * HIST, :].astype(BF16)
            out_ref[place, HIST:, :] = sums_ref[QH + place * CAND : QH + (place + 1) * CAND, :].astype(BF16)
    else:
        out_ref[...] = sums_ref[...]


def attend(tables, steps, tie, q, sums, col, chunks, tks, fresh=False, last=False):
    flags, codes, bases, apart = tables
    kvs = [kv for chunk in chunks for kv in chunk]
    shapes = tuple(tuple(kv.shape[0] for kv in chunk) for chunk in chunks)
    keys = sum(kv.shape[0] for kv in kvs)
    return pl.pallas_call(
        functools.partial(attend_kernel, fresh=fresh, last=last, chunks=shapes),
        in_specs=[SM] * 5 + [pl.BlockSpec(memory_space=pl.ANY)] + [VM] * (3 + len(kvs) + len(tks)),
        out_specs=VM,
        out_shape=jax.ShapeDtypeStruct((NP, ROWS, HD), BF16) if last else jax.ShapeDtypeStruct((QROWS, HD), F32),
        scratch_shapes=[pltpu.VMEM((QROWS, HD), F32), pltpu.VMEM((2, BLOCK, KEYS), F32)],
        compiler_params=params(16),
        cost_estimate=pl.CostEstimate(
            flops=16 * QROWS * keys * HD, bytes_accessed=4 * QROWS * keys, transcendentals=QROWS * keys
        ),
        name="attend",
    )(flags, codes, bases, apart, steps, tie, q, sums, col, *kvs, *tks)


def finish_kernel(hist_ref, cand_ref, w_ref, att_ref, gate_ref, hist_out, cand_out):
    parts = [att_ref[h].astype(F32) for h in range(HEADS)]
    center = sum(jnp.sum(part, axis=-1, keepdims=True) for part in parts) * (1.0 / D)
    parts = [part - center for part in parts]
    spread = sum(jnp.sum(part * part, axis=-1, keepdims=True) for part in parts) * (1.0 / D)
    scale = lax.rsqrt(spread + 1e-6)
    parts = [(part * scale * gate_ref[h].astype(F32)).astype(BF16) for h, part in enumerate(parts)]
    total = jnp.dot(jnp.concatenate(parts, axis=1), w_ref[...], preferred_element_type=F32)
    hist_out[0] = (hist_ref[0].astype(F32) + total[:HIST]).astype(BF16)
    cand_out[0] = (cand_ref[0].astype(F32) + total[HIST:]).astype(BF16)


def finish(hist, cand, w_out, att, gate):
    return pl.pallas_call(
        finish_kernel,
        out_shape=[
            jax.ShapeDtypeStruct((1, HIST, D), BF16),
            jax.ShapeDtypeStruct((1, CAND, D), BF16),
        ],
        in_specs=[VM] * 5,
        out_specs=[VM, VM],
        compiler_params=params(6),
        cost_estimate=pl.CostEstimate(flops=2 * ROWS * D * D, bytes_accessed=4 << 20, transcendentals=0),
        name="finish",
    )(hist, cand, w_out, att, gate)


def gather_weights(w_proj, z, core, batch):
    z_lo, y = batch // NY, batch % NY
    head = NC * z + core
    mine = lax.dynamic_slice(w_proj, (0, head % 4 * HD), (D, HD))
    other = from_sources(mine, dzl=1)
    pair = jnp.stack([mine, other])
    up, down, across = from_sources(pair, dy=1), from_sources(pair, dy=-1), from_sources(pair, dy=2)
    is_source = y % 2 == z // 2
    halves = []
    for f in range(2):
        source = jnp.where(y // 2 == f, pair, across)
        sink = jnp.where((y - 1) % NY // 2 == f, up, down)
        halves.append(jnp.where(is_source, source, sink))
    low = [jnp.where(z_lo == 0, half[0], half[1]) for half in halves]
    high = [jnp.where(z_lo == 0, half[1], half[0]) for half in halves]
    return jnp.concatenate(low + high, axis=1)


def body(history, candidates, event_times, request_times, w_proj, w_out, bias_steps):
    seq, batch = lax.axis_index("seq"), lax.axis_index("batch")
    x, z, core = seq // (ZH * NC), seq // NC % ZH, seq % NC
    head = NC * z + core
    zs = [(z + off) % ZH for off in OFF]
    xs = jnp.stack([(x + off) % NX for off in OFF])

    n0, t0 = norm_rows(history, candidates, event_times, request_times)
    near = [n0, shift(n0, dz=1), shift(n0, dz=-1), shift(n0, dz=2)]
    pieces = near + [shift(piece, flip=True) for piece in near]

    near = [t0, shift(t0, dz=1), shift(t0, dz=-1), shift(t0, dz=2)]
    t4 = jnp.concatenate([sum(jnp.where(zs[r] == j, near[r], 0) for r in range(ZH)) for j in range(ZH)], axis=0)
    other = shift(t4, flip=True)
    t8 = jnp.stack([jnp.where(core == 0, t4, other), jnp.where(core == 0, other, t4)], axis=1).reshape(NP, 2 * HIST)
    k0 = t8[:, :HIST]
    tks = [k0, shift(k0, dx=1), shift(k0, dx=-1), shift(k0, dx=2)]
    cand_times = t8[:, HIST:ROWS].reshape(QC // 128, 128)
    tq = jnp.concatenate([k0, cand_times, jnp.zeros((6, 128), I32)], axis=0)

    w_head = gather_weights(w_proj, z, core, batch)

    steps = 0.5 * lax.dynamic_slice(bias_steps, (0, head), (2 * LEVELS, 1))[:, 0]
    level = jnp.arange(LEVELS, dtype=I32)
    tk = jnp.stack(tks)
    first_q = jnp.concatenate([k0[:, 0], jnp.min(cand_times, axis=1)])
    last_q = jnp.concatenate([k0[:, -1], jnp.max(cand_times, axis=1)])

    def passed(gap, marks):
        return jnp.sum((gap[..., None] >= marks).astype(I32), axis=-1)

    time_low = passed(first_q[None, :, None] - tk[:, None, :, -1], 4**level)
    time_high = passed(last_q[None, :, None] - tk[:, None, :, 0], 4**level)
    blocks = jnp.arange(NP, dtype=I32)
    hist_gap = ((x - xs)[:, None, None] * NP + blocks[None, :, None] - blocks[None, None, :]) * HIST
    cand_gap = LENGTH - (xs[:, None, None] * NP + blocks[None, None, :]) * HIST
    cand_gap = jnp.broadcast_to(cand_gap, (NX, QC // 128, NP))
    place_low = passed(jnp.concatenate([hist_gap, cand_gap], axis=1) - (HIST - 1), 2**level)
    place_high = passed(jnp.concatenate([hist_gap + (HIST - 1), cand_gap], axis=1), 2**level)
    hidden = jnp.concatenate([hist_gap < 0, cand_gap < 0], axis=1)
    code = time_low | (time_high << 4) | (place_low << 8) | (place_high << 12)
    code = jnp.where(hidden, 0, code).reshape(NX, TILES)
    base = jnp.sum(jnp.where(time_low[..., None] > level, steps[:LEVELS], 0.0), axis=-1)
    base = base + jnp.sum(jnp.where(place_low[..., None] > level, steps[LEVELS:], 0.0), axis=-1)
    base = jnp.where(hidden, MASKED, base).reshape(NX, TILES)
    later = (xs > x).astype(I32)
    col, w_mine = prepare(tq, w_out)
    w_full = lax.all_gather(w_mine, "batch", axis=0, tiled=True)

    def tables(first, count):
        chosen = slice(first, first + count)
        apart = jnp.zeros((2 * NX,), I32).at[:count].set((x - xs[chosen]) * KEYS).at[NX : NX + count].set(xs[chosen] * KEYS)
        return later[chosen], code[chosen].reshape(-1), base[chosen].reshape(-1), apart

    q, kv0, own, gate = project(jnp.stack([core, *zs]), pieces, w_head)
    kv1, kv2 = shift(kv0, dx=1), shift(kv0, dx=-1)
    part = KEYS // 2
    kv3a, kv3b = shift(kv1[:part], dx=1), shift(kv2[part:], dx=-1)
    gates = lax.all_to_all(gate, "seq", 0, 0, axis_index_groups=SAME_X)
    sums = attend(tables(0, 1), steps, q, q, own, col, [[kv0]], tks[:1], fresh=True)
    sums = attend(tables(1, 2), steps, gates, q, sums, col, [[kv1], [kv2]], tks[1:3])
    att = attend(tables(3, 1), steps, q, q, sums, col, [[kv3a, kv3b]], tks[3:], last=True)
    atts = lax.all_to_all(att, "seq", 0, 0, axis_index_groups=SAME_X)
    return tuple(finish(history, candidates, w_full, atts, gates))


def solution(mesh):
    in_specs = (
        P("batch", "seq", None),
        P("batch", "seq", None),
        P("batch", "seq"),
        P("batch", "seq"),
        P(None, "batch"),
        P("batch", None),
        P(),
    )
    out_specs = (P("batch", "seq", None), P("batch", "seq", None))
    return jax.shard_map(body, mesh=mesh, in_specs=in_specs, out_specs=out_specs, check_vma=False)
```

```python
import functools

import jax
import jax.numpy as jnp
from jax import lax
from jax.experimental import pallas as pl
from jax.experimental.pallas import tpu as pltpu
from jax.sharding import PartitionSpec as P

F32, BF16, I32 = jnp.float32, jnp.bfloat16, jnp.int32
ZL, NY, NX, ZH, NC = 2, 4, 4, 4, 2
NB, NS = ZL * NY, NX * ZH * NC
OFF = (0, -1, 1, 2)
HEADS, HD, D = 8, 128, 1024
HIST, CAND = 128, 32
ROWS = HIST + CAND
NP = ZH * NC
QH, QC = NP * HIST, NP * CAND
QROWS = QH + QC
KEYS = NP * HIST
LENGTH = NS * HIST
LEVELS = 12
MASKED = -1e30
SAME_X = [[x * NP + p for p in range(NP)] for x in range(NX)]
VM = pl.BlockSpec(memory_space=pltpu.VMEM)
SM = pl.BlockSpec(memory_space=pltpu.SMEM)


def params(mib):
    return pltpu.CompilerParams(vmem_limit_bytes=mib << 20)


def seq_perm(dx=0, dz=0, flip=False):
    pairs = []
    for s in range(NS):
        x, z, c = s // (ZH * NC), s // NC % ZH, s % NC
        t = ((x + dx) % NX * ZH + (z + dz) % ZH) * NC + (c ^ int(flip))
        pairs.append((s, t))
    return pairs


def shift(array, dx=0, dz=0, flip=False):
    return lax.ppermute(array, "seq", seq_perm(dx, dz, flip))


def source_perm(dzl=0, dy=0):
    pairs = []
    for b in range(NB):
        zl, y = b // NY, b % NY
        t = (zl + dzl) % ZL * NY + (y + dy) % NY
        for s in range(NS):
            if y % 2 == s // NC % ZH // 2:
                pairs.append((b * NS + s, t * NS + s))
    return pairs


def from_sources(array, dzl=0, dy=0):
    return lax.ppermute(array, ("batch", "seq"), source_perm(dzl, dy))


def norm_kernel(hist_ref, cand_ref, events_ref, requests_ref, out_ref, times_ref):
    for ref, first, count in ((hist_ref, 0, HIST), (cand_ref, HIST, CAND)):
        rows = ref[0].astype(F32)
        rows = rows - jnp.mean(rows, axis=-1, keepdims=True)
        spread = jnp.mean(rows * rows, axis=-1, keepdims=True)
        out_ref[first : first + count, :] = (rows * lax.rsqrt(spread + 1e-6)).astype(BF16)
    times_ref[...] = jnp.zeros_like(times_ref)
    times_ref[:, :HIST] = events_ref[...]
    times_ref[:, HIST:ROWS] = requests_ref[...]


def norm_rows(hist, cand, events, requests):
    return pl.pallas_call(
        norm_kernel,
        out_shape=[jax.ShapeDtypeStruct((ROWS, D), BF16), jax.ShapeDtypeStruct((1, 2 * HIST), I32)],
        in_specs=[VM] * 4,
        out_specs=[VM] * 2,
        cost_estimate=pl.CostEstimate(flops=8 * ROWS * D, bytes_accessed=4 * ROWS * D, transcendentals=0),
        name="norm_rows",
    )(hist, cand, events, requests)


def prepare_kernel(tq_ref, col_ref):
    for i in range(QROWS // 128):
        col_ref[i * 128 : (i + 1) * 128, :] = jnp.transpose(jnp.broadcast_to(tq_ref[i : i + 1, :], (128, 128)))


def prepare(tq):
    return pl.pallas_call(
        prepare_kernel,
        out_shape=jax.ShapeDtypeStruct((QROWS, 128), I32),
        in_specs=[VM],
        out_specs=VM,
        cost_estimate=pl.CostEstimate(flops=2 << 20, bytes_accessed=1 << 20, transcendentals=0),
        name="prepare",
    )(tq)


def half_silu(half):
    return half + half * jnp.tanh(half)


def project_kernel(where_ref, *refs):
    rows_ref, (w0, w1, w2, w3a, w3b), wout_ref = refs[0], refs[1:6], refs[6]
    q_ref, kv_ref, own_ref, gate_ref, wout_out, rows, weights = refs[7:]
    wout_out[...] = wout_ref[...]
    for place in range(NP):
        rows[place * HIST : (place + 1) * HIST, :] = rows_ref[place, :HIST, :]
        rows[QH + place * CAND : QH + (place + 1) * CAND, :] = rows_ref[place, HIST:, :]
    depth = D // NX
    for m in range(NX):
        at = pl.multiple_of(where_ref[m] * depth, depth)
        for kind in range(4):
            part = (w0, w1, w2)[m][kind] if m < 3 else (w3a, w3b)[kind // 2][kind % 2]
            weights[pl.ds(at, depth), kind * HD : (kind + 1) * HD] = part
    mixed = jnp.dot(rows[...], weights[:, 2 * HD :], preferred_element_type=F32)
    mixed = half_silu(0.5 * mixed)
    queries, keys = mixed[:, :HD], mixed[:, HD:]
    q_ref[...] = (queries * (0.5 * HD**-0.5)).astype(BF16)
    kv_ref[:, :HD] = keys[:QH].astype(BF16)
    dots = jnp.sum(queries[QH:].astype(BF16).astype(F32) * keys[QH:].astype(BF16).astype(F32), axis=-1, keepdims=True)
    own = half_silu(dots * (0.5 * HD**-0.5)).astype(BF16).astype(F32)
    mixed = jnp.dot(rows[...], weights[:, : 2 * HD], preferred_element_type=F32)
    mixed = half_silu(0.5 * mixed).astype(BF16)
    kv_ref[:, HD:] = mixed[:QH, HD:]
    own_ref[...] = own * mixed[QH:, HD:].astype(F32)
    for place in range(NP):
        gate_ref[place, :HIST, :] = mixed[place * HIST : (place + 1) * HIST, :HD]
        gate_ref[place, HIST:, :] = mixed[QH + place * CAND : QH + (place + 1) * CAND, :HD]


def project(where, rows, parts, w_out):
    return pl.pallas_call(
        project_kernel,
        out_shape=[
            jax.ShapeDtypeStruct((QROWS, HD), BF16),
            jax.ShapeDtypeStruct((KEYS, 2 * HD), BF16),
            jax.ShapeDtypeStruct((QC, HD), F32),
            jax.ShapeDtypeStruct((NP, ROWS, HD), BF16),
            jax.ShapeDtypeStruct(w_out.shape, BF16),
        ],
        in_specs=[SM] + [VM] * 7,
        out_specs=[VM] * 5,
        scratch_shapes=[pltpu.VMEM((QROWS, D), BF16), pltpu.VMEM((D, 4 * HD), BF16)],
        compiler_params=params(16),
        cost_estimate=pl.CostEstimate(flops=2 * QROWS * D * 4 * HD, bytes_accessed=6 << 20, transcendentals=QROWS * 4 * HD),
        name="project",
    )(where, rows, *parts, w_out)


BLOCK = 256
TILES = (QROWS // 128) * NP
STEPS = QROWS // BLOCK
STEP_TILES = TILES // STEPS


def attend_kernel(flag_ref, count_ref, work_ref, base_ref, apart_ref, steps_ref, tie_ref, q_ref, sums_in, col_ref, *rest, fresh, last, chunks):
    arrays = sum(len(chunk) for chunk in chunks)
    kvs, tks = list(rest[:arrays]), rest[arrays : arrays + len(chunks)]
    out_ref, sums_ref, half_ref = rest[arrays + len(chunks) :]
    if fresh:
        sums_ref[:QH, :] = jnp.zeros((QH, HD), F32)
        sums_ref[QH:, :] = sums_in[...]
    else:
        sums_ref[...] = sums_in[...]
    row = lax.broadcasted_iota(I32, (128, 128), 0)
    lane = lax.broadcasted_iota(I32, (128, 128), 1)

    def scores(n, block, slot):
        first = block * BLOCK
        begin = 0
        for kv in parts[n]:
            keys = kv.shape[0]
            half = lax.dot_general(
                q_ref[first : first + BLOCK, :], kv[:, :HD], (((1,), (1,)), ((), ())), preferred_element_type=F32
            )
            for i in range(BLOCK // 128):
                for j in range(keys // 128):
                    at = n * TILES + (block * (BLOCK // 128) + i) * NP + begin // 128 + j
                    half_ref[slot, i * 128 : (i + 1) * 128, begin + j * 128 : begin + (j + 1) * 128] = (
                        half[i * 128 : (i + 1) * 128, j * 128 : (j + 1) * 128] + base_ref[at]
                    )
            begin += keys

    def correct(n, block, slot):
        is_cand = block * BLOCK >= QH

        def tile(k, carry):
            code = work_ref[n * TILES + block * STEP_TILES + k]
            i, j = (code >> 3) & 1, code & 7
            time_low, time_high, place_low, place_high = [(code >> bit) & 15 for bit in (4, 8, 12, 16)]
            if True:
                rows = pl.ds(pl.multiple_of(i * 128, 128), 128)
                columns = pl.ds(pl.multiple_of(j * 128, 128), 128)
                first = pl.multiple_of(block * BLOCK + i * 128, 128)
                value = half_ref[slot, rows, columns]
                gap = col_ref[pl.ds(first, 128), :] - tks[n][pl.ds(j, 1), :]

                def time_step(level, value):
                    return value + jnp.where(gap >= (1 << (2 * level)), steps_ref[level], 0.0)

                value = lax.fori_loop(time_low, time_high, time_step, value)
                if is_cand:
                    gap2 = (LENGTH - apart_ref[NX + n] - j * 128) - lane
                else:
                    gap2 = (apart_ref[n] + (block * (BLOCK // 128) + i - j) * 128) + row - lane

                def place_step(level, value):
                    return value + jnp.where(gap2 >= (1 << level), steps_ref[LEVELS + level], 0.0)

                value = lax.fori_loop(place_low, place_high, place_step, value)
                if not is_cand:
                    value = jnp.where(gap2 >= 0, value, MASKED)
                half_ref[slot, rows, columns] = value

            return carry

        lax.fori_loop(0, count_ref[n * STEPS + block], tile, 0)

    def combine(n, block, slot):
        first = block * BLOCK
        begin = 0
        total = sums_ref[first : first + BLOCK, :]
        for kv in parts[n]:
            keys = kv.shape[0]
            weights = half_silu(half_ref[slot, :, begin : begin + keys]).astype(BF16)
            total = total + jnp.dot(weights, kv[:, HD:], preferred_element_type=F32)
            begin += keys
        sums_ref[first : first + BLOCK, :] = total

    def sweep(n, blocks):
        for k, block in enumerate(blocks):
            scores(n, block, k % 2)
            if k > 0:
                combine(n, blocks[k - 1], (k - 1) % 2)
            correct(n, block, k % 2)
        combine(n, blocks[-1], (len(blocks) - 1) % 2)

    parts = []
    for chunk in chunks:
        parts.append([kvs.pop(0) for _ in chunk])
    for n in range(len(chunks)):

        @pl.when(flag_ref[n] == 0)
        def _():
            sweep(n, list(range(QROWS // BLOCK)))

        @pl.when(flag_ref[n] != 0)
        def _():
            sweep(n, [QROWS // BLOCK - 1])

    if last:
        for place in range(NP):
            out_ref[place, :HIST, :] = sums_ref[place * HIST : (place + 1) * HIST, :].astype(BF16)
            out_ref[place, HIST:, :] = sums_ref[QH + place * CAND : QH + (place + 1) * CAND, :].astype(BF16)
    else:
        out_ref[...] = sums_ref[...]


def attend(tables, steps, tie, q, sums, col, chunks, tks, fresh=False, last=False):
    flags, counts, works, bases, apart = tables
    kvs = [kv for chunk in chunks for kv in chunk]
    shapes = tuple(tuple(kv.shape[0] for kv in chunk) for chunk in chunks)
    keys = sum(kv.shape[0] for kv in kvs)
    return pl.pallas_call(
        functools.partial(attend_kernel, fresh=fresh, last=last, chunks=shapes),
        in_specs=[SM] * 6 + [pl.BlockSpec(memory_space=pl.ANY)] + [VM] * (3 + len(kvs) + len(tks)),
        out_specs=VM,
        out_shape=jax.ShapeDtypeStruct((NP, ROWS, HD), BF16) if last else jax.ShapeDtypeStruct((QROWS, HD), F32),
        scratch_shapes=[pltpu.VMEM((QROWS, HD), F32), pltpu.VMEM((2, BLOCK, KEYS), F32)],
        compiler_params=params(16),
        cost_estimate=pl.CostEstimate(
            flops=16 * QROWS * keys * HD, bytes_accessed=4 * QROWS * keys, transcendentals=QROWS * keys
        ),
        name="attend",
    )(flags, counts, works, bases, apart, steps, tie, q, sums, col, *kvs, *tks)


def finish_kernel(hist_ref, cand_ref, w_ref, att_ref, gate_ref, hist_out, cand_out):
    parts = [att_ref[h].astype(F32) for h in range(HEADS)]
    center = sum(jnp.sum(part, axis=-1, keepdims=True) for part in parts) * (1.0 / D)
    parts = [part - center for part in parts]
    spread = sum(jnp.sum(part * part, axis=-1, keepdims=True) for part in parts) * (1.0 / D)
    scale = lax.rsqrt(spread + 1e-6)
    parts = [(part * scale * gate_ref[h].astype(F32)).astype(BF16) for h, part in enumerate(parts)]
    total = jnp.dot(jnp.concatenate(parts, axis=1), w_ref[...], preferred_element_type=F32)
    hist_out[0] = (hist_ref[0].astype(F32) + total[:HIST]).astype(BF16)
    cand_out[0] = (cand_ref[0].astype(F32) + total[HIST:]).astype(BF16)


def finish(hist, cand, w_out, att, gate):
    return pl.pallas_call(
        finish_kernel,
        out_shape=[
            jax.ShapeDtypeStruct((1, HIST, D), BF16),
            jax.ShapeDtypeStruct((1, CAND, D), BF16),
        ],
        in_specs=[VM] * 5,
        out_specs=[VM, VM],
        compiler_params=params(6),
        cost_estimate=pl.CostEstimate(flops=2 * ROWS * D * D, bytes_accessed=4 << 20, transcendentals=0),
        name="finish",
    )(hist, cand, w_out, att, gate)


def gather_weights(w_proj, x, z, core, batch):
    depth = D // NX
    z_lo, y = batch // NY, batch % NY
    head = NC * z + core
    mine = lax.dynamic_slice(w_proj, (x * depth, head % 4 * HD), (depth, HD))
    other = from_sources(mine, dzl=1)
    pair = jnp.stack([mine, other])
    up, down, across = from_sources(pair, dy=1), from_sources(pair, dy=-1), from_sources(pair, dy=2)
    is_source = y % 2 == z // 2
    halves = []
    for f in range(2):
        source = jnp.where(y // 2 == f, pair, across)
        sink = jnp.where((y - 1) % NY // 2 == f, up, down)
        halves.append(jnp.where(is_source, source, sink))
    low = [jnp.where(z_lo == 0, half[0], half[1]) for half in halves]
    high = [jnp.where(z_lo == 0, half[1], half[0]) for half in halves]
    return jnp.stack(low + high)


def body(history, candidates, event_times, request_times, w_proj, w_out, bias_steps):
    seq, batch = lax.axis_index("seq"), lax.axis_index("batch")
    x, z, core = seq // (ZH * NC), seq // NC % ZH, seq % NC
    head = NC * z + core
    xs = jnp.stack([(x + off) % NX for off in OFF])

    n0, t0 = norm_rows(history, candidates, event_times, request_times)
    rows = lax.all_gather(n0, "seq", axis_index_groups=SAME_X)

    bits = [seq >> bit & 1 for bit in range(5)]
    times = t0
    for bit in range(5):
        if bit == 3:
            t8, times = times, times[:, :HIST]
        other = lax.ppermute(times, "seq", [(s, s ^ (1 << bit)) for s in range(NS)])
        first = bits[bit] == 0
        times = jnp.concatenate([jnp.where(first, times, other), jnp.where(first, other, times)], axis=0)
    k0 = t8[:, :HIST]
    by_x = times.reshape(NX, NP, HIST)
    tks = [sum(jnp.where(xs[m] == j, by_x[j], 0) for j in range(NX)) for m in range(NX)]
    cand_times = t8[:, HIST:ROWS].reshape(QC // 128, 128)
    tq = jnp.concatenate([k0, cand_times, jnp.zeros((6, 128), I32)], axis=0)

    w0 = gather_weights(w_proj, x, z, core, batch)
    w1, w2 = shift(w0, dx=1), shift(w0, dx=-1)
    w_parts = [w0, w1, w2, shift(w1[:2], dx=1), shift(w2[2:], dx=-1)]

    steps = 0.5 * lax.dynamic_slice(bias_steps, (0, head), (2 * LEVELS, 1))[:, 0]
    level = jnp.arange(LEVELS, dtype=I32)
    tk = jnp.stack(tks)
    first_q = jnp.concatenate([k0[:, 0], jnp.min(cand_times, axis=1)])
    last_q = jnp.concatenate([k0[:, -1], jnp.max(cand_times, axis=1)])

    def passed(gap, marks):
        return jnp.sum((gap[..., None] >= marks).astype(I32), axis=-1)

    time_low = passed(first_q[None, :, None] - tk[:, None, :, -1], 4**level)
    time_high = passed(last_q[None, :, None] - tk[:, None, :, 0], 4**level)
    blocks = jnp.arange(NP, dtype=I32)
    hist_gap = ((x - xs)[:, None, None] * NP + blocks[None, :, None] - blocks[None, None, :]) * HIST
    cand_gap = LENGTH - (xs[:, None, None] * NP + blocks[None, None, :]) * HIST
    cand_gap = jnp.broadcast_to(cand_gap, (NX, QC // 128, NP))
    place_low = passed(jnp.concatenate([hist_gap, cand_gap], axis=1) - (HIST - 1), 2**level)
    place_high = passed(jnp.concatenate([hist_gap + (HIST - 1), cand_gap], axis=1), 2**level)
    hidden = jnp.concatenate([hist_gap < 0, cand_gap < 0], axis=1)
    code = time_low | (time_high << 4) | (place_low << 8) | (place_high << 12)
    mixed = ~hidden & ((time_low != time_high) | (place_low != place_high))
    number = jnp.arange(STEP_TILES, dtype=I32)
    code = (code << 4 | number.reshape(BLOCK // 128, NP)[jnp.arange(QROWS // 128) % (BLOCK // 128)]).reshape(NX, STEPS, STEP_TILES)
    mixed = mixed.reshape(NX, STEPS, STEP_TILES)
    rank = jnp.sum(jnp.where(number[None, :] < number[:, None], mixed[..., None, :].astype(I32), 0), axis=-1)
    spot = mixed[..., None] & (rank[..., None] == number)
    works = jnp.sum(jnp.where(spot, code[..., None], 0), axis=-2).reshape(NX, TILES)
    counts = jnp.sum(mixed.astype(I32), axis=-1)
    base = jnp.sum(jnp.where(time_low[..., None] > level, steps[:LEVELS], 0.0), axis=-1)
    base = base + jnp.sum(jnp.where(place_low[..., None] > level, steps[LEVELS:], 0.0), axis=-1)
    base = jnp.where(hidden, MASKED, base).reshape(NX, TILES)
    later = (xs > x).astype(I32)
    col = prepare(tq)

    def tables(first, count):
        chosen = slice(first, first + count)
        apart = jnp.concatenate([jnp.roll((x - xs) * KEYS, -first), jnp.roll(xs * KEYS, -first)])
        return later[chosen], counts[chosen].reshape(-1), works[chosen].reshape(-1), base[chosen].reshape(-1), apart

    q, kv0, own, gate, w_mine = project(xs, rows, w_parts, w_out)
    w_full = lax.all_gather(w_mine, "batch", axis=0, tiled=True)
    kv1, kv2 = shift(kv0, dx=1), shift(kv0, dx=-1)
    part = KEYS // 2
    kv3a, kv3b = shift(kv1[:part], dx=1), shift(kv2[part:], dx=-1)
    gates = lax.all_to_all(gate, "seq", 0, 0, axis_index_groups=SAME_X)
    sums = attend(tables(0, 1), steps, q, q, own, col, [[kv0]], tks[:1], fresh=True)
    sums = attend(tables(1, 2), steps, gates, q, sums, col, [[kv1], [kv2]], tks[1:3])
    att = attend(tables(3, 1), steps, q, q, sums, col, [[kv3a, kv3b]], tks[3:], last=True)
    atts = lax.all_to_all(att, "seq", 0, 0, axis_index_groups=SAME_X)
    return tuple(finish(history, candidates, w_full, atts, gates))


def solution(mesh):
    in_specs = (
        P("batch", "seq", None),
        P("batch", "seq", None),
        P("batch", "seq"),
        P("batch", "seq"),
        P(None, "batch"),
        P("batch", None),
        P(),
    )
    out_specs = (P("batch", "seq", None), P("batch", "seq", None))
    return jax.shard_map(body, mesh=mesh, in_specs=in_specs, out_specs=out_specs, check_vma=False)
```

```python
import functools

import jax
import jax.numpy as jnp
from jax import lax
from jax.experimental import pallas as pl
from jax.experimental.pallas import tpu as pltpu
from jax.sharding import PartitionSpec as P

F32, BF16, I32 = jnp.float32, jnp.bfloat16, jnp.int32
ZL, NY, NX, ZH, NC = 2, 4, 4, 4, 2
NB, NS = ZL * NY, NX * ZH * NC
OFF = (0, -1, 1, 2)
HEADS, HD, D = 8, 128, 1024
HIST, CAND = 128, 32
ROWS = HIST + CAND
NP = ZH * NC
QH, QC = NP * HIST, NP * CAND
QROWS = QH + QC
KEYS = NP * HIST
LENGTH = NS * HIST
LEVELS = 12
MASKED = -1e30
SAME_X = [[x * NP + p for p in range(NP)] for x in range(NX)]
VM = pl.BlockSpec(memory_space=pltpu.VMEM)
SM = pl.BlockSpec(memory_space=pltpu.SMEM)
HBM = pl.BlockSpec(memory_space=pl.ANY)
DEPTH = D // NX


def params(mib):
    return pltpu.CompilerParams(vmem_limit_bytes=mib << 20)


def position():
    seq = lax.axis_index("seq")
    return seq // (ZH * NC), seq // NC % ZH, seq % NC


def seq_perm(dx=0, dz=0, flip=False):
    pairs = []
    for s in range(NS):
        x, z, c = s // (ZH * NC), s // NC % ZH, s % NC
        t = ((x + dx) % NX * ZH + (z + dz) % ZH) * NC + (c ^ int(flip))
        pairs.append((s, t))
    return pairs


def shift(array, dx=0, dz=0, flip=False):
    return lax.ppermute(array, "seq", seq_perm(dx, dz, flip))


def norm_kernel(hist_ref, cand_ref, events_ref, requests_ref, proj_ref, out_ref, times_ref, shards_ref, part_ref, sem):
    x, z, core = position()
    column = pl.multiple_of((NC * z + core) % 4 * HD, HD)
    copy = pltpu.make_async_copy(
        proj_ref.at[pl.ds(pl.multiple_of(x * DEPTH, DEPTH), DEPTH), pl.ds(column, HD)], part_ref, sem
    )
    copy.start()
    for ref, first, count in ((hist_ref, 0, HIST), (cand_ref, HIST, CAND)):
        rows = ref[0].astype(F32)
        rows = rows - jnp.mean(rows, axis=-1, keepdims=True)
        spread = jnp.mean(rows * rows, axis=-1, keepdims=True)
        out_ref[first : first + count, :] = (rows * lax.rsqrt(spread + 1e-6)).astype(BF16)
    times_ref[...] = jnp.zeros_like(times_ref)
    times_ref[:, :HIST] = events_ref[...]
    times_ref[:, HIST:ROWS] = requests_ref[...]
    copy.wait()
    for b in range(NB):
        shards_ref[b] = part_ref[...]


def norm_rows(hist, cand, events, requests, w_proj):
    return pl.pallas_call(
        norm_kernel,
        out_shape=[
            jax.ShapeDtypeStruct((ROWS, D), BF16),
            jax.ShapeDtypeStruct((1, 2 * HIST), I32),
            jax.ShapeDtypeStruct((NB, DEPTH, HD), BF16),
        ],
        in_specs=[VM] * 4 + [HBM],
        out_specs=[VM] * 3,
        scratch_shapes=[pltpu.VMEM((DEPTH, HD), BF16), pltpu.SemaphoreType.DMA(())],
        cost_estimate=pl.CostEstimate(flops=8 * ROWS * D, bytes_accessed=4 * ROWS * D, transcendentals=0),
        name="norm_rows",
    )(hist, cand, events, requests, w_proj)


def merge_kernel(mine_ref, other_ref, wout_ref, *rest, bit):
    out_ref, wout_out = rest[-2:]
    count = mine_ref.shape[0]
    first = lax.axis_index("seq") >> bit & 1 == 0
    out_ref[:count] = jnp.where(first, mine_ref[...], other_ref[...])
    out_ref[count:] = jnp.where(first, other_ref[...], mine_ref[...])
    wout_out[...] = wout_ref[...]


def merge(mine, other, bit, w_out, ties):
    return pl.pallas_call(
        functools.partial(merge_kernel, bit=bit),
        out_shape=[
            jax.ShapeDtypeStruct((2 * mine.shape[0], mine.shape[1]), mine.dtype),
            jax.ShapeDtypeStruct(w_out.shape, w_out.dtype),
        ],
        in_specs=[VM] * 3 + [HBM] * len(ties),
        out_specs=[VM] * 2,
        cost_estimate=pl.CostEstimate(flops=1 << 12, bytes_accessed=1 << 16, transcendentals=0),
        name="merge",
    )(mine, other, w_out, *ties)


def prepare_kernel(tq_ref, col_ref):
    for i in range(QROWS // 128):
        col_ref[i * 128 : (i + 1) * 128, :] = jnp.transpose(jnp.broadcast_to(tq_ref[i : i + 1, :], (128, 128)))


def prepare(tq):
    return pl.pallas_call(
        prepare_kernel,
        out_shape=jax.ShapeDtypeStruct((QROWS, 128), I32),
        in_specs=[VM],
        out_specs=VM,
        cost_estimate=pl.CostEstimate(flops=2 << 20, bytes_accessed=1 << 20, transcendentals=0),
        name="prepare",
    )(tq)


def half_silu(half):
    return half + half * jnp.tanh(half)


HALF = NP // 2


HALF = NP // 2


def project_kernel(rows_ref, *refs):
    parts, (qh_ref, qc_ref, kv_ref, own_ref, gate_ref, rows, weights, sems) = refs[:NX], refs[NX:]
    x = position()[0]
    hist, cand = HALF * HIST, HALF * CAND
    copies, fetches = [], []
    for m in range(NX):
        at = pl.multiple_of((x + OFF[m]) % NX * DEPTH, DEPTH)
        for kind in range(4):
            block = weights.at[pl.ds(at, DEPTH), kind * HD : (kind + 1) * HD]
            fetches.append(pltpu.make_async_copy(parts[m].at[kind], block, sems.at[2 + m, kind]))
            fetches[-1].start()
    for place in range(NP):
        step, at = place // HALF, place % HALF
        copies.append(
            (
                pltpu.make_async_copy(
                    rows_ref.at[place, :HIST, :], rows.at[step, at * HIST : (at + 1) * HIST, :], sems.at[0, place]
                ),
                pltpu.make_async_copy(
                    rows_ref.at[place, HIST:, :],
                    rows.at[step, hist + at * CAND : hist + (at + 1) * CAND, :],
                    sems.at[1, place],
                ),
            )
        )
        for copy in copies[-1]:
            copy.start()
    for fetch in fetches:
        fetch.wait()
    for step in range(NP // HALF):
        for pair in copies[step * HALF : (step + 1) * HALF]:
            for copy in pair:
                copy.wait()
        mixed = jnp.dot(rows[step], weights[:, 2 * HD :], preferred_element_type=F32)
        mixed = half_silu(0.5 * mixed)
        queries, keys = mixed[:, :HD], mixed[:, HD:]
        scaled = (queries * (0.5 * HD**-0.5)).astype(BF16)
        hists, cands = slice(step * hist, (step + 1) * hist), slice(step * cand, (step + 1) * cand)
        qh_ref[hists, :] = scaled[:hist]
        qc_ref[cands, :] = scaled[hist:]
        kv_ref[hists, :HD] = keys[:hist].astype(BF16)
        dots = queries[hist:].astype(BF16).astype(F32) * keys[hist:].astype(BF16).astype(F32)
        dots = jnp.sum(dots, axis=-1, keepdims=True)
        own = half_silu(dots * (0.5 * HD**-0.5)).astype(BF16).astype(F32)
        mixed = jnp.dot(rows[step], weights[:, : 2 * HD], preferred_element_type=F32)
        mixed = half_silu(0.5 * mixed).astype(BF16)
        kv_ref[hists, HD:] = mixed[:hist, HD:]
        own_ref[cands, :] = own * mixed[hist:, HD:].astype(F32)
        for at in range(HALF):
            place = step * HALF + at
            gate_ref[place, :HIST, :] = mixed[at * HIST : (at + 1) * HIST, :HD]
            gate_ref[place, HIST:, :] = mixed[hist + at * CAND : hist + (at + 1) * CAND, :HD]


def project(rows, parts):
    return pl.pallas_call(
        project_kernel,
        in_specs=[HBM] * (1 + NX),
        out_specs=[VM] * 5,
        scratch_shapes=[
            pltpu.VMEM((NP // HALF, HALF * ROWS, D), BF16),
            pltpu.VMEM((D, 4 * HD), BF16),
            pltpu.SemaphoreType.DMA((2 + NX, NP)),
        ],
        out_shape=[
            jax.ShapeDtypeStruct((QH, HD), BF16),
            jax.ShapeDtypeStruct((QC, HD), BF16),
            jax.ShapeDtypeStruct((KEYS, 2 * HD), BF16),
            jax.ShapeDtypeStruct((QC, HD), F32),
            jax.ShapeDtypeStruct((NP, ROWS, HD), BF16),
        ],
        compiler_params=params(56),
        cost_estimate=pl.CostEstimate(flops=2 * QROWS * D * 4 * HD, bytes_accessed=6 << 20, transcendentals=QROWS * 4 * HD),
        name="project",
    )(rows, *parts)


BLOCK = 256
TILES = (QROWS // 128) * NP
STEPS = QROWS // BLOCK
STEP_TILES = TILES // STEPS


def attend_kernel(count_ref, work_ref, base_ref, steps_ref, qh_ref, qc_ref, sums_in, col_ref, *rest, fresh, last, chunks, start):
    arrays = sum(len(chunk) for chunk in chunks)
    gate_ref = rest[-4]
    kvs, tks = list(rest[:arrays]), rest[arrays : arrays + len(chunks)]
    out_ref, sums_ref, half_ref = rest[-3:]
    if fresh:
        sums_ref[:QH, :] = jnp.zeros((QH, HD), F32)
        sums_ref[QH:, :] = sums_in[...]
    else:
        sums_ref[...] = sums_in[...]
    row = lax.broadcasted_iota(I32, (128, 128), 0)
    lane = lax.broadcasted_iota(I32, (128, 128), 1)
    x = position()[0]
    froms = [(x + OFF[start + n]) % NX for n in range(len(chunks))]

    def scores(n, block, slot):
        first = block * BLOCK
        begin = 0
        for kv in parts[n]:
            keys = kv.shape[0]
            queries = qc_ref[first - QH : first - QH + BLOCK, :] if first >= QH else qh_ref[first : first + BLOCK, :]
            half = lax.dot_general(
                queries, kv[:, :HD], (((1,), (1,)), ((), ())), preferred_element_type=F32
            )
            for i in range(BLOCK // 128):
                for j in range(keys // 128):
                    at = (start + n) * TILES + (block * (BLOCK // 128) + i) * NP + begin // 128 + j
                    half_ref[slot, i * 128 : (i + 1) * 128, begin + j * 128 : begin + (j + 1) * 128] = (
                        half[i * 128 : (i + 1) * 128, j * 128 : (j + 1) * 128] + base_ref[at]
                    )
            begin += keys

    def correct(n, block, slot):
        is_cand = block * BLOCK >= QH

        def tile(k, carry):
            code = work_ref[(start + n) * TILES + block * STEP_TILES + k]
            i, j = (code >> 3) & 1, code & 7
            time_low, time_high, place_low, place_high = [(code >> bit) & 15 for bit in (4, 8, 12, 16)]
            if True:
                rows = pl.ds(pl.multiple_of(i * 128, 128), 128)
                columns = pl.ds(pl.multiple_of(j * 128, 128), 128)
                first = pl.multiple_of(block * BLOCK + i * 128, 128)
                value = half_ref[slot, rows, columns]
                gap = col_ref[pl.ds(first, 128), :] - tks[n][pl.ds(j, 1), :]

                def time_step(level, value):
                    return value + jnp.where(gap >= (1 << (2 * level)), steps_ref[level], 0.0)

                value = lax.fori_loop(time_low, time_high, time_step, value)
                if is_cand:
                    gap2 = (LENGTH - froms[n] * KEYS - j * 128) - lane
                else:
                    gap2 = ((x - froms[n]) * KEYS + (block * (BLOCK // 128) + i - j) * 128) + row - lane

                def place_step(level, value):
                    return value + jnp.where(gap2 >= (1 << level), steps_ref[LEVELS + level], 0.0)

                value = lax.fori_loop(place_low, place_high, place_step, value)
                if not is_cand:
                    value = jnp.where(gap2 >= 0, value, MASKED)
                half_ref[slot, rows, columns] = value

            return carry

        lax.fori_loop(0, count_ref[(start + n) * STEPS + block], tile, 0)

    def combine(n, block, slot):
        first = block * BLOCK
        begin = 0
        total = sums_ref[first : first + BLOCK, :]
        for kv in parts[n]:
            keys = kv.shape[0]
            weights = half_silu(half_ref[slot, :, begin : begin + keys]).astype(BF16)
            total = total + jnp.dot(weights, kv[:, HD:], preferred_element_type=F32)
            begin += keys
        sums_ref[first : first + BLOCK, :] = total

    def sweep(n, blocks):
        for k, block in enumerate(blocks):
            scores(n, block, k % 2)
            if k > 0:
                combine(n, blocks[k - 1], (k - 1) % 2)
            correct(n, block, k % 2)
        combine(n, blocks[-1], (len(blocks) - 1) % 2)

    parts = []
    for chunk in chunks:
        parts.append([kvs.pop(0) for _ in chunk])
    for n in range(len(chunks)):

        @pl.when(froms[n] <= x)
        def _():
            sweep(n, list(range(QROWS // BLOCK)))

        @pl.when(froms[n] > x)
        def _():
            sweep(n, [QROWS // BLOCK - 1])

    if last:
        for place in range(NP):
            out_ref[place, :HIST, :HD] = sums_ref[place * HIST : (place + 1) * HIST, :].astype(BF16)
            out_ref[place, HIST:, :HD] = sums_ref[QH + place * CAND : QH + (place + 1) * CAND, :].astype(BF16)
            out_ref[place, :, HD:] = gate_ref[place]
    else:
        out_ref[...] = sums_ref[...]


def attend(tables, queries, sums, col, chunks, tks, start, gates=None):
    fresh, last = start == 0, gates is not None
    gates = [gates] if last else []
    kvs = [kv for chunk in chunks for kv in chunk]
    shapes = tuple(tuple(kv.shape[0] for kv in chunk) for chunk in chunks)
    keys = sum(kv.shape[0] for kv in kvs)
    return pl.pallas_call(
        functools.partial(attend_kernel, fresh=fresh, last=last, chunks=shapes, start=start),
        in_specs=[SM] * 4 + [VM] * (4 + len(kvs) + len(tks) + len(gates)),
        out_specs=VM,
        out_shape=jax.ShapeDtypeStruct((NP, ROWS, 2 * HD), BF16) if last else jax.ShapeDtypeStruct((QROWS, HD), F32),
        scratch_shapes=[pltpu.VMEM((QROWS, HD), F32), pltpu.VMEM((2, BLOCK, KEYS), F32)],
        compiler_params=params(16),
        cost_estimate=pl.CostEstimate(
            flops=16 * QROWS * keys * HD, bytes_accessed=4 * QROWS * keys, transcendentals=QROWS * keys
        ),
        name="attend",
    )(*tables, *queries, sums, col, *kvs, *tks, *gates)


def finish_kernel(hist_ref, cand_ref, pair_ref, w_hbm, hist_out, cand_out, w_ref, sem):
    copy = pltpu.make_async_copy(w_hbm, w_ref, sem)
    copy.start()
    parts = [pair_ref[h, :, :HD].astype(F32) for h in range(HEADS)]
    center = sum(jnp.sum(part, axis=-1, keepdims=True) for part in parts) * (1.0 / D)
    parts = [part - center for part in parts]
    spread = sum(jnp.sum(part * part, axis=-1, keepdims=True) for part in parts) * (1.0 / D)
    scale = lax.rsqrt(spread + 1e-6)
    parts = [(part * scale * pair_ref[h, :, HD:].astype(F32)).astype(BF16) for h, part in enumerate(parts)]
    copy.wait()
    total = jnp.dot(jnp.concatenate(parts, axis=1), w_ref[...], preferred_element_type=F32)
    hist_out[0] = (hist_ref[0].astype(F32) + total[:HIST]).astype(BF16)
    cand_out[0] = (cand_ref[0].astype(F32) + total[HIST:]).astype(BF16)


def finish(hist, cand, w_out, pairs):
    return pl.pallas_call(
        finish_kernel,
        out_shape=[
            jax.ShapeDtypeStruct((1, HIST, D), BF16),
            jax.ShapeDtypeStruct((1, CAND, D), BF16),
        ],
        in_specs=[VM] * 3 + [HBM],
        out_specs=[VM, VM],
        scratch_shapes=[pltpu.VMEM((D, D), BF16), pltpu.SemaphoreType.DMA(())],
        compiler_params=params(56),
        cost_estimate=pl.CostEstimate(flops=2 * ROWS * D * D, bytes_accessed=4 << 20, transcendentals=0),
        name="finish",
    )(hist, cand, pairs, w_out)


def gather_weights(shards, z):
    shards = lax.all_to_all(shards, "batch", 0, 0)
    return lax.dynamic_index_in_dim(shards.reshape(4, 2, DEPTH, HD), z // 2, axis=1, keepdims=False)


def body(history, candidates, event_times, request_times, w_proj, w_out, bias_steps):
    seq = lax.axis_index("seq")
    x, z, core = position()
    head = NC * z + core
    xs = jnp.stack([(x + off) % NX for off in OFF])

    n0, t0, shards = norm_rows(history, candidates, event_times, request_times, w_proj)
    rows = lax.all_gather(n0, "seq", axis_index_groups=SAME_X)

    w0 = gather_weights(shards, z)
    w_parts = [w0, shift(w0, dx=1), shift(w0, dx=-1), shift(w0, dx=2)]

    times = t0
    order = (3, 4, 0, 1, 2)
    for bit in order:
        other = lax.ppermute(times, "seq", [(s, s ^ (1 << bit)) for s in range(NS)])
        if bit == order[-2]:
            times, w_mine = merge(times, other, bit, w_out, w_parts[1:])
            w_full = lax.all_gather(w_mine, "batch", axis=0, tiled=True)
        else:
            first = seq >> bit & 1 == 0
            times = jnp.concatenate([jnp.where(first, times, other), jnp.where(first, other, times)], axis=0)
    times = times.reshape(ZH, NC, NX, 2 * HIST).transpose(2, 0, 1, 3).reshape(NX, NP, 2 * HIST)
    t8 = jnp.sum(jnp.where((x == jnp.arange(NX))[:, None, None], times, 0), axis=0)
    k0 = t8[:, :HIST]
    tks = [jnp.sum(jnp.where((xs[m] == jnp.arange(NX))[:, None, None], times[..., :HIST], 0), axis=0) for m in range(NX)]
    cand_times = t8[:, HIST:ROWS].reshape(QC // 128, 128)

    qh, qc, kv0, own, gates = project(rows, w_parts)

    steps = 0.5 * lax.dynamic_slice(bias_steps, (0, head), (2 * LEVELS, 1))[:, 0]
    level = jnp.arange(LEVELS, dtype=I32)
    tie = (kv0[0, 0] * 0).astype(I32)
    tk = jnp.stack(tks) + tie
    tq = jnp.concatenate([k0, cand_times, jnp.zeros((6, 128), I32)], axis=0) + tie
    first_q = jnp.concatenate([k0[:, 0], jnp.min(cand_times, axis=1)]) + tie
    last_q = jnp.concatenate([k0[:, -1], jnp.max(cand_times, axis=1)]) + tie

    def passed(gap, marks):
        return jnp.sum((gap[..., None] >= marks).astype(I32), axis=-1)

    time_low = passed(first_q[None, :, None] - tk[:, None, :, -1], 4**level)
    time_high = passed(last_q[None, :, None] - tk[:, None, :, 0], 4**level)
    blocks = jnp.arange(NP, dtype=I32)
    hist_gap = ((x - xs)[:, None, None] * NP + blocks[None, :, None] - blocks[None, None, :]) * HIST
    cand_gap = LENGTH - (xs[:, None, None] * NP + blocks[None, None, :]) * HIST
    cand_gap = jnp.broadcast_to(cand_gap, (NX, QC // 128, NP))
    place_low = passed(jnp.concatenate([hist_gap, cand_gap], axis=1) - (HIST - 1), 2**level)
    place_high = passed(jnp.concatenate([hist_gap + (HIST - 1), cand_gap], axis=1), 2**level)
    hidden = jnp.concatenate([hist_gap < 0, cand_gap < 0], axis=1)
    code = time_low | (time_high << 4) | (place_low << 8) | (place_high << 12)
    mixed = ~hidden & ((time_low != time_high) | (place_low != place_high))
    number = jnp.arange(STEP_TILES, dtype=I32)
    code = (code << 4 | number.reshape(BLOCK // 128, NP)[jnp.arange(QROWS // 128) % (BLOCK // 128)]).reshape(NX, STEPS, STEP_TILES)
    mixed = mixed.reshape(NX, STEPS, STEP_TILES)
    rank = jnp.sum(jnp.where(number[None, :] < number[:, None], mixed[..., None, :].astype(I32), 0), axis=-1)
    spot = mixed[..., None] & (rank[..., None] == number)
    works = jnp.sum(jnp.where(spot, code[..., None], 0), axis=-2).reshape(NX, TILES)
    counts = jnp.sum(mixed.astype(I32), axis=-1)
    base = jnp.sum(jnp.where(time_low[..., None] > level, steps[:LEVELS], 0.0), axis=-1)
    base = base + jnp.sum(jnp.where(place_low[..., None] > level, steps[LEVELS:], 0.0), axis=-1)
    base = jnp.where(hidden, MASKED, base).reshape(NX, TILES)
    col = prepare(tq)
    tables = (counts.reshape(-1), works.reshape(-1), base.reshape(-1), steps)

    queries = (qh, qc)
    kv1, kv2 = shift(kv0, dx=1), shift(kv0, dx=-1)
    part = KEYS // 2
    kv3a, kv3b = shift(kv1[:part], dx=1), shift(kv2[part:], dx=-1)
    sums = attend(tables, queries, own, col, [[kv0]], tks[:1], 0)
    sums = attend(tables, queries, sums, col, [[kv1], [kv2]], tks[1:3], 1)
    att = attend(tables, queries, sums, col, [[kv3a, kv3b]], tks[3:], 3, gates)
    atts = lax.all_to_all(att, "seq", 0, 0, axis_index_groups=SAME_X)
    return tuple(finish(history, candidates, w_full, atts))


def solution(mesh):
    in_specs = (
        P("batch", "seq", None),
        P("batch", "seq", None),
        P("batch", "seq"),
        P("batch", "seq"),
        P(None, "batch"),
        P("batch", None),
        P(),
    )
    out_specs = (P("batch", "seq", None), P("batch", "seq", None))
    return jax.shard_map(body, mesh=mesh, in_specs=in_specs, out_specs=out_specs, check_vma=False)
```

```python
import functools

import jax
import jax.numpy as jnp
from jax import lax
from jax.experimental import pallas as pl
from jax.experimental.pallas import tpu as pltpu
from jax.sharding import PartitionSpec as P

F32, BF16, I32 = jnp.float32, jnp.bfloat16, jnp.int32
ZL, NY, NX, ZH, NC = 2, 4, 4, 4, 2
NB, NS = ZL * NY, NX * ZH * NC
OFF = (0, -1, 1, 2)
HEADS, HD, D = 8, 128, 1024
HIST, CAND = 128, 32
ROWS = HIST + CAND
NP = ZH * NC
QH, QC = NP * HIST, NP * CAND
QROWS = QH + QC
KEYS = NP * HIST
LENGTH = NS * HIST
LEVELS = 12
MASKED = -1e30
SAME_X = [[x * NP + p for p in range(NP)] for x in range(NX)]
VM = pl.BlockSpec(memory_space=pltpu.VMEM)
SM = pl.BlockSpec(memory_space=pltpu.SMEM)
HBM = pl.BlockSpec(memory_space=pl.ANY)
DEPTH = D // NX


def params(mib):
    return pltpu.CompilerParams(vmem_limit_bytes=mib << 20)


def position():
    seq = lax.axis_index("seq")
    return seq // (ZH * NC), seq // NC % ZH, seq % NC


def seq_perm(dx=0, dz=0, flip=False):
    pairs = []
    for s in range(NS):
        x, z, c = s // (ZH * NC), s // NC % ZH, s % NC
        t = ((x + dx) % NX * ZH + (z + dz) % ZH) * NC + (c ^ int(flip))
        pairs.append((s, t))
    return pairs


def shift(array, dx=0, dz=0, flip=False):
    return lax.ppermute(array, "seq", seq_perm(dx, dz, flip))


def norm_kernel(hist_ref, cand_ref, events_ref, requests_ref, proj_ref, out_ref, times_ref, shards_ref, part_ref, sem):
    x, z, core = position()
    column = pl.multiple_of((NC * z + core) % 4 * HD, HD)
    copy = pltpu.make_async_copy(
        proj_ref.at[pl.ds(pl.multiple_of(x * DEPTH, DEPTH), DEPTH), pl.ds(column, HD)], part_ref, sem
    )
    copy.start()
    for ref, first, count in ((hist_ref, 0, HIST), (cand_ref, HIST, CAND)):
        rows = ref[0].astype(F32)
        rows = rows - jnp.mean(rows, axis=-1, keepdims=True)
        spread = jnp.mean(rows * rows, axis=-1, keepdims=True)
        out_ref[first : first + count, :] = (rows * lax.rsqrt(spread + 1e-6)).astype(BF16)
    times_ref[...] = jnp.zeros_like(times_ref)
    times_ref[:, :HIST] = events_ref[...]
    times_ref[:, HIST:ROWS] = requests_ref[...]
    copy.wait()
    for b in range(NB):
        shards_ref[b] = part_ref[...]


def norm_rows(hist, cand, events, requests, w_proj):
    return pl.pallas_call(
        norm_kernel,
        out_shape=[
            jax.ShapeDtypeStruct((ROWS, D), BF16),
            jax.ShapeDtypeStruct((1, 2 * HIST), I32),
            jax.ShapeDtypeStruct((NB, DEPTH, HD), BF16),
        ],
        in_specs=[VM] * 4 + [HBM],
        out_specs=[VM] * 3,
        scratch_shapes=[pltpu.VMEM((DEPTH, HD), BF16), pltpu.SemaphoreType.DMA(())],
        compiler_params=params(6),
        cost_estimate=pl.CostEstimate(flops=8 * ROWS * D, bytes_accessed=4 * ROWS * D, transcendentals=0),
        name="norm_rows",
    )(hist, cand, events, requests, w_proj)


def merge_kernel(mine_ref, other_ref, wout_ref, *rest, bit):
    out_ref, wout_out = rest[-2:]
    count = mine_ref.shape[0]
    first = lax.axis_index("seq") >> bit & 1 == 0
    out_ref[:count] = jnp.where(first, mine_ref[...], other_ref[...])
    out_ref[count:] = jnp.where(first, other_ref[...], mine_ref[...])
    wout_out[...] = wout_ref[...]


def merge(mine, other, bit, w_out, ties):
    return pl.pallas_call(
        functools.partial(merge_kernel, bit=bit),
        out_shape=[
            jax.ShapeDtypeStruct((2 * mine.shape[0], mine.shape[1]), mine.dtype),
            jax.ShapeDtypeStruct(w_out.shape, w_out.dtype),
        ],
        in_specs=[VM] * (3 + len(ties)),
        out_specs=[VM] * 2,
        compiler_params=params(6),
        cost_estimate=pl.CostEstimate(flops=1 << 12, bytes_accessed=1 << 16, transcendentals=0),
        name="merge",
    )(mine, other, w_out, *ties)


def prepare_kernel(tq_ref, col_ref):
    for i in range(QROWS // 128):
        col_ref[i * 128 : (i + 1) * 128, :] = jnp.transpose(jnp.broadcast_to(tq_ref[i : i + 1, :], (128, 128)))


def prepare(tq):
    return pl.pallas_call(
        prepare_kernel,
        out_shape=jax.ShapeDtypeStruct((QROWS, 128), I32),
        in_specs=[VM],
        out_specs=VM,
        compiler_params=params(4),
        cost_estimate=pl.CostEstimate(flops=2 << 20, bytes_accessed=1 << 20, transcendentals=0),
        name="prepare",
    )(tq)


def half_silu(half):
    return half + half * jnp.tanh(half)


HALF = NP // 2


HALF = NP // 2


def project_kernel(rows_ref, *refs):
    parts, (qh_ref, qc_ref, kv_ref, own_ref, gate_ref, rows, weights, sems) = refs[:NX], refs[NX:]
    x = position()[0]
    hist, cand = HALF * HIST, HALF * CAND
    copies = []
    for place in range(NP):
        step, at = place // HALF, place % HALF
        copies.append(
            (
                pltpu.make_async_copy(
                    rows_ref.at[place, :HIST, :], rows.at[step, at * HIST : (at + 1) * HIST, :], sems.at[0, place]
                ),
                pltpu.make_async_copy(
                    rows_ref.at[place, HIST:, :],
                    rows.at[step, hist + at * CAND : hist + (at + 1) * CAND, :],
                    sems.at[1, place],
                ),
            )
        )
        for copy in copies[-1]:
            copy.start()
    for m in range(NX):
        at = pl.multiple_of((x + OFF[m]) % NX * DEPTH, DEPTH)
        for kind in range(4):
            weights[pl.ds(at, DEPTH), kind * HD : (kind + 1) * HD] = parts[m][kind]
    for step in range(NP // HALF):
        for pair in copies[step * HALF : (step + 1) * HALF]:
            for copy in pair:
                copy.wait()
        mixed = jnp.dot(rows[step], weights[:, 2 * HD :], preferred_element_type=F32)
        mixed = half_silu(0.5 * mixed)
        queries, keys = mixed[:, :HD], mixed[:, HD:]
        scaled = (queries * (0.5 * HD**-0.5)).astype(BF16)
        hists, cands = slice(step * hist, (step + 1) * hist), slice(step * cand, (step + 1) * cand)
        qh_ref[hists, :] = scaled[:hist]
        qc_ref[cands, :] = scaled[hist:]
        kv_ref[hists, :HD] = keys[:hist].astype(BF16)
        dots = queries[hist:].astype(BF16).astype(F32) * keys[hist:].astype(BF16).astype(F32)
        dots = jnp.sum(dots, axis=-1, keepdims=True)
        own = half_silu(dots * (0.5 * HD**-0.5)).astype(BF16).astype(F32)
        mixed = jnp.dot(rows[step], weights[:, : 2 * HD], preferred_element_type=F32)
        mixed = half_silu(0.5 * mixed).astype(BF16)
        kv_ref[hists, HD:] = mixed[:hist, HD:]
        own_ref[cands, :] = own * mixed[hist:, HD:].astype(F32)
        for at in range(HALF):
            place = step * HALF + at
            gate_ref[place, :HIST, :] = mixed[at * HIST : (at + 1) * HIST, :HD]
            gate_ref[place, HIST:, :] = mixed[hist + at * CAND : hist + (at + 1) * CAND, :HD]


def project(rows, parts):
    return pl.pallas_call(
        project_kernel,
        in_specs=[HBM] + [VM] * NX,
        out_specs=[VM] * 5,
        scratch_shapes=[
            pltpu.VMEM((NP // HALF, HALF * ROWS, D), BF16),
            pltpu.VMEM((D, 4 * HD), BF16),
            pltpu.SemaphoreType.DMA((2, NP)),
        ],
        out_shape=[
            jax.ShapeDtypeStruct((QH, HD), BF16),
            jax.ShapeDtypeStruct((QC, HD), BF16),
            jax.ShapeDtypeStruct((KEYS, 2 * HD), BF16),
            jax.ShapeDtypeStruct((QC, HD), F32),
            jax.ShapeDtypeStruct((NP, ROWS, HD), BF16),
        ],
        compiler_params=params(50),
        cost_estimate=pl.CostEstimate(flops=2 * QROWS * D * 4 * HD, bytes_accessed=6 << 20, transcendentals=QROWS * 4 * HD),
        name="project",
    )(rows, *parts)


BLOCK = 256
TILES = (QROWS // 128) * NP
STEPS = QROWS // BLOCK
STEP_TILES = TILES // STEPS


def attend_kernel(count_ref, work_ref, base_ref, steps_ref, qh_ref, qc_ref, sums_in, col_ref, *rest, fresh, last, chunks, start):
    arrays = sum(len(chunk) for chunk in chunks)
    gate_ref = rest[-4]
    kvs, tks = list(rest[:arrays]), rest[arrays : arrays + len(chunks)]
    out_ref, sums_ref, half_ref = rest[-3:]
    if fresh:
        sums_ref[:QH, :] = jnp.zeros((QH, HD), F32)
        sums_ref[QH:, :] = sums_in[...]
    else:
        sums_ref[...] = sums_in[...]
    row = lax.broadcasted_iota(I32, (128, 128), 0)
    lane = lax.broadcasted_iota(I32, (128, 128), 1)
    x = position()[0]
    froms = [(x + OFF[start + n]) % NX for n in range(len(chunks))]

    def scores(n, block, slot):
        first = block * BLOCK
        begin = 0
        for kv in parts[n]:
            keys = kv.shape[0]
            queries = qc_ref[first - QH : first - QH + BLOCK, :] if first >= QH else qh_ref[first : first + BLOCK, :]
            half = lax.dot_general(
                queries, kv[:, :HD], (((1,), (1,)), ((), ())), preferred_element_type=F32
            )
            for i in range(BLOCK // 128):
                for j in range(keys // 128):
                    at = (start + n) * TILES + (block * (BLOCK // 128) + i) * NP + begin // 128 + j
                    half_ref[slot, i * 128 : (i + 1) * 128, begin + j * 128 : begin + (j + 1) * 128] = (
                        half[i * 128 : (i + 1) * 128, j * 128 : (j + 1) * 128] + base_ref[at]
                    )
            begin += keys

    def correct(n, block, slot):
        is_cand = block * BLOCK >= QH

        def tile(k, carry):
            code = work_ref[(start + n) * TILES + block * STEP_TILES + k]
            i, j = (code >> 3) & 1, code & 7
            time_low, time_high, place_low, place_high = [(code >> bit) & 15 for bit in (4, 8, 12, 16)]
            if True:
                rows = pl.ds(pl.multiple_of(i * 128, 128), 128)
                columns = pl.ds(pl.multiple_of(j * 128, 128), 128)
                first = pl.multiple_of(block * BLOCK + i * 128, 128)
                value = half_ref[slot, rows, columns]
                gap = col_ref[pl.ds(first, 128), :] - tks[n][pl.ds(j, 1), :]

                def time_step(level, value):
                    return value + jnp.where(gap >= (1 << (2 * level)), steps_ref[level], 0.0)

                value = lax.fori_loop(time_low, time_high, time_step, value)
                if is_cand:
                    gap2 = (LENGTH - froms[n] * KEYS - j * 128) - lane
                else:
                    gap2 = ((x - froms[n]) * KEYS + (block * (BLOCK // 128) + i - j) * 128) + row - lane

                def place_step(level, value):
                    return value + jnp.where(gap2 >= (1 << level), steps_ref[LEVELS + level], 0.0)

                value = lax.fori_loop(place_low, place_high, place_step, value)
                if not is_cand:
                    value = jnp.where(gap2 >= 0, value, MASKED)
                half_ref[slot, rows, columns] = value

            return carry

        lax.fori_loop(0, count_ref[(start + n) * STEPS + block], tile, 0)

    def combine(n, block, slot):
        first = block * BLOCK
        begin = 0
        total = sums_ref[first : first + BLOCK, :]
        for kv in parts[n]:
            keys = kv.shape[0]
            weights = half_silu(half_ref[slot, :, begin : begin + keys]).astype(BF16)
            total = total + jnp.dot(weights, kv[:, HD:], preferred_element_type=F32)
            begin += keys
        sums_ref[first : first + BLOCK, :] = total

    def sweep(n, blocks):
        for k, block in enumerate(blocks):
            scores(n, block, k % 2)
            if k > 0:
                combine(n, blocks[k - 1], (k - 1) % 2)
            correct(n, block, k % 2)
        combine(n, blocks[-1], (len(blocks) - 1) % 2)

    parts = []
    for chunk in chunks:
        parts.append([kvs.pop(0) for _ in chunk])
    for n in range(len(chunks)):

        @pl.when(froms[n] <= x)
        def _():
            sweep(n, list(range(QROWS // BLOCK)))

        @pl.when(froms[n] > x)
        def _():
            sweep(n, [QROWS // BLOCK - 1])

    if last:
        for place in range(NP):
            out_ref[place, :HIST, :HD] = sums_ref[place * HIST : (place + 1) * HIST, :].astype(BF16)
            out_ref[place, HIST:, :HD] = sums_ref[QH + place * CAND : QH + (place + 1) * CAND, :].astype(BF16)
            out_ref[place, :, HD:] = gate_ref[place]
    else:
        out_ref[...] = sums_ref[...]


def attend(tables, queries, sums, col, chunks, tks, start, gates=None):
    fresh, last = start == 0, gates is not None
    gates = [gates] if last else []
    kvs = [kv for chunk in chunks for kv in chunk]
    shapes = tuple(tuple(kv.shape[0] for kv in chunk) for chunk in chunks)
    keys = sum(kv.shape[0] for kv in kvs)
    return pl.pallas_call(
        functools.partial(attend_kernel, fresh=fresh, last=last, chunks=shapes, start=start),
        in_specs=[SM] * 4 + [VM] * (4 + len(kvs) + len(tks) + len(gates)),
        out_specs=VM,
        out_shape=jax.ShapeDtypeStruct((NP, ROWS, 2 * HD), BF16) if last else jax.ShapeDtypeStruct((QROWS, HD), F32),
        scratch_shapes=[pltpu.VMEM((QROWS, HD), F32), pltpu.VMEM((2, BLOCK, KEYS), F32)],
        compiler_params=params(16),
        cost_estimate=pl.CostEstimate(
            flops=16 * QROWS * keys * HD, bytes_accessed=4 * QROWS * keys, transcendentals=QROWS * keys
        ),
        name="attend",
    )(*tables, *queries, sums, col, *kvs, *tks, *gates)


def finish_kernel(hist_ref, cand_ref, pair_ref, w_hbm, hist_out, cand_out, w_ref, sem):
    copy = pltpu.make_async_copy(w_hbm, w_ref, sem)
    copy.start()
    parts = [pair_ref[h, :, :HD].astype(F32) for h in range(HEADS)]
    center = sum(jnp.sum(part, axis=-1, keepdims=True) for part in parts) * (1.0 / D)
    parts = [part - center for part in parts]
    spread = sum(jnp.sum(part * part, axis=-1, keepdims=True) for part in parts) * (1.0 / D)
    scale = lax.rsqrt(spread + 1e-6)
    parts = [(part * scale * pair_ref[h, :, HD:].astype(F32)).astype(BF16) for h, part in enumerate(parts)]
    copy.wait()
    total = jnp.dot(jnp.concatenate(parts, axis=1), w_ref[...], preferred_element_type=F32)
    hist_out[0] = (hist_ref[0].astype(F32) + total[:HIST]).astype(BF16)
    cand_out[0] = (cand_ref[0].astype(F32) + total[HIST:]).astype(BF16)


def finish(hist, cand, w_out, pairs):
    return pl.pallas_call(
        finish_kernel,
        out_shape=[
            jax.ShapeDtypeStruct((1, HIST, D), BF16),
            jax.ShapeDtypeStruct((1, CAND, D), BF16),
        ],
        in_specs=[VM] * 3 + [HBM],
        out_specs=[VM, VM],
        scratch_shapes=[pltpu.VMEM((D, D), BF16), pltpu.SemaphoreType.DMA(())],
        compiler_params=params(12),
        cost_estimate=pl.CostEstimate(flops=2 * ROWS * D * D, bytes_accessed=4 << 20, transcendentals=0),
        name="finish",
    )(hist, cand, pairs, w_out)


def gather_weights(shards, z):
    shards = lax.all_to_all(shards, "batch", 0, 0)
    return lax.dynamic_index_in_dim(shards.reshape(4, 2, DEPTH, HD), z // 2, axis=1, keepdims=False)


def body(history, candidates, event_times, request_times, w_proj, w_out, bias_steps):
    seq = lax.axis_index("seq")
    x, z, core = position()
    head = NC * z + core
    xs = jnp.stack([(x + off) % NX for off in OFF])

    n0, t0, shards = norm_rows(history, candidates, event_times, request_times, w_proj)
    rows = lax.all_gather(n0, "seq", axis_index_groups=SAME_X)

    w0 = gather_weights(shards, z)
    w_parts = [w0, shift(w0, dx=1), shift(w0, dx=-1), shift(w0, dx=2)]

    times = t0
    order = (3, 4, 0, 1, 2)
    for bit in order:
        other = lax.ppermute(times, "seq", [(s, s ^ (1 << bit)) for s in range(NS)])
        if bit == order[-2]:
            times, w_mine = merge(times, other, bit, w_out, w_parts[1:])
            w_full = lax.all_gather(w_mine, "batch", axis=0, tiled=True)
        else:
            first = seq >> bit & 1 == 0
            times = jnp.concatenate([jnp.where(first, times, other), jnp.where(first, other, times)], axis=0)
    times = times.reshape(ZH, NC, NX, 2 * HIST).transpose(2, 0, 1, 3).reshape(NX, NP, 2 * HIST)
    t8 = jnp.sum(jnp.where((x == jnp.arange(NX))[:, None, None], times, 0), axis=0)
    k0 = t8[:, :HIST]
    tks = [jnp.sum(jnp.where((xs[m] == jnp.arange(NX))[:, None, None], times[..., :HIST], 0), axis=0) for m in range(NX)]
    cand_times = t8[:, HIST:ROWS].reshape(QC // 128, 128)

    qh, qc, kv0, own, gates = project(rows, w_parts)

    steps = 0.5 * lax.dynamic_slice(bias_steps, (0, head), (2 * LEVELS, 1))[:, 0]
    level = jnp.arange(LEVELS, dtype=I32)
    tie = (kv0[0, 0] * 0).astype(I32)
    tk = jnp.stack(tks) + tie
    tq = jnp.concatenate([k0, cand_times, jnp.zeros((6, 128), I32)], axis=0) + tie
    first_q = jnp.concatenate([k0[:, 0], jnp.min(cand_times, axis=1)]) + tie
    last_q = jnp.concatenate([k0[:, -1], jnp.max(cand_times, axis=1)]) + tie

    def passed(gap, marks):
        return jnp.sum((gap[..., None] >= marks).astype(I32), axis=-1)

    time_low = passed(first_q[None, :, None] - tk[:, None, :, -1], 4**level)
    time_high = passed(last_q[None, :, None] - tk[:, None, :, 0], 4**level)
    blocks = jnp.arange(NP, dtype=I32)
    hist_gap = ((x - xs)[:, None, None] * NP + blocks[None, :, None] - blocks[None, None, :]) * HIST
    cand_gap = LENGTH - (xs[:, None, None] * NP + blocks[None, None, :]) * HIST
    cand_gap = jnp.broadcast_to(cand_gap, (NX, QC // 128, NP))
    place_low = passed(jnp.concatenate([hist_gap, cand_gap], axis=1) - (HIST - 1), 2**level)
    place_high = passed(jnp.concatenate([hist_gap + (HIST - 1), cand_gap], axis=1), 2**level)
    hidden = jnp.concatenate([hist_gap < 0, cand_gap < 0], axis=1)
    code = time_low | (time_high << 4) | (place_low << 8) | (place_high << 12)
    mixed = ~hidden & ((time_low != time_high) | (place_low != place_high))
    number = jnp.arange(STEP_TILES, dtype=I32)
    code = (code << 4 | number.reshape(BLOCK // 128, NP)[jnp.arange(QROWS // 128) % (BLOCK // 128)]).reshape(NX, STEPS, STEP_TILES)
    mixed = mixed.reshape(NX, STEPS, STEP_TILES)
    rank = jnp.sum(jnp.where(number[None, :] < number[:, None], mixed[..., None, :].astype(I32), 0), axis=-1)
    spot = mixed[..., None] & (rank[..., None] == number)
    works = jnp.sum(jnp.where(spot, code[..., None], 0), axis=-2).reshape(NX, TILES)
    counts = jnp.sum(mixed.astype(I32), axis=-1)
    base = jnp.sum(jnp.where(time_low[..., None] > level, steps[:LEVELS], 0.0), axis=-1)
    base = base + jnp.sum(jnp.where(place_low[..., None] > level, steps[LEVELS:], 0.0), axis=-1)
    base = jnp.where(hidden, MASKED, base).reshape(NX, TILES)
    col = prepare(tq)
    tables = (counts.reshape(-1), works.reshape(-1), base.reshape(-1), steps)

    queries = (qh, qc)
    kv1, kv2 = shift(kv0, dx=1), shift(kv0, dx=-1)
    part = KEYS // 2
    kv3a, kv3b = shift(kv1[:part], dx=1), shift(kv2[part:], dx=-1)
    sums = attend(tables, queries, own, col, [[kv0]], tks[:1], 0)
    sums = attend(tables, queries, sums, col, [[kv1], [kv2]], tks[1:3], 1)
    att = attend(tables, queries, sums, col, [[kv3a, kv3b]], tks[3:], 3, gates)
    atts = lax.all_to_all(att, "seq", 0, 0, axis_index_groups=SAME_X)
    return tuple(finish(history, candidates, w_full, atts))


def solution(mesh):
    in_specs = (
        P("batch", "seq", None),
        P("batch", "seq", None),
        P("batch", "seq"),
        P("batch", "seq"),
        P(None, "batch"),
        P("batch", None),
        P(),
    )
    out_specs = (P("batch", "seq", None), P("batch", "seq", None))
    return jax.shard_map(body, mesh=mesh, in_specs=in_specs, out_specs=out_specs, check_vma=False)
```

```python
import functools

import jax
import jax.numpy as jnp
from jax import lax
from jax.experimental import pallas as pl
from jax.experimental.pallas import tpu as pltpu
from jax.sharding import PartitionSpec as P

F32, BF16, I32 = jnp.float32, jnp.bfloat16, jnp.int32
ZL, NY, NX, ZH, NC = 2, 4, 4, 4, 2
NB, NS = ZL * NY, NX * ZH * NC
OFF = (0, -1, 1, 2)
HEADS, HD, D = 8, 128, 1024
HIST, CAND = 128, 32
ROWS = HIST + CAND
NP = ZH * NC
QH, QC = NP * HIST, NP * CAND
QROWS = QH + QC
KEYS = NP * HIST
LENGTH = NS * HIST
LEVELS = 12
MASKED = -1e30
SAME_X = [[x * NP + p for p in range(NP)] for x in range(NX)]
VM = pl.BlockSpec(memory_space=pltpu.VMEM)
SM = pl.BlockSpec(memory_space=pltpu.SMEM)
HBM = pl.BlockSpec(memory_space=pl.ANY)
DEPTH = D // NX


def params(mib):
    return pltpu.CompilerParams(vmem_limit_bytes=mib << 20)


def position():
    seq = lax.axis_index("seq")
    return seq // (ZH * NC), seq // NC % ZH, seq % NC


def seq_perm(dx=0, dz=0, flip=False):
    pairs = []
    for s in range(NS):
        x, z, c = s // (ZH * NC), s // NC % ZH, s % NC
        t = ((x + dx) % NX * ZH + (z + dz) % ZH) * NC + (c ^ int(flip))
        pairs.append((s, t))
    return pairs


def shift(array, dx=0, dz=0, flip=False):
    return lax.ppermute(array, "seq", seq_perm(dx, dz, flip))


def norm_kernel(hist_ref, cand_ref, events_ref, requests_ref, proj_ref, out_ref, times_ref, shards_ref, part_ref, sem):
    x, z, core = position()
    column = pl.multiple_of((NC * z + core) % 4 * HD, HD)
    copy = pltpu.make_async_copy(
        proj_ref.at[pl.ds(pl.multiple_of(x * DEPTH, DEPTH), DEPTH), pl.ds(column, HD)], part_ref, sem
    )
    copy.start()
    for ref, first, count in ((hist_ref, 0, HIST), (cand_ref, HIST, CAND)):
        rows = ref[0].astype(F32)
        rows = rows - jnp.mean(rows, axis=-1, keepdims=True)
        spread = jnp.mean(rows * rows, axis=-1, keepdims=True)
        out_ref[first : first + count, :] = (rows * lax.rsqrt(spread + 1e-6)).astype(BF16)
    times_ref[...] = jnp.zeros_like(times_ref)
    times_ref[:, :HIST] = events_ref[...]
    times_ref[:, HIST:ROWS] = requests_ref[...]
    copy.wait()
    for b in range(NB):
        shards_ref[b] = part_ref[...]


def norm_rows(hist, cand, events, requests, w_proj):
    return pl.pallas_call(
        norm_kernel,
        out_shape=[
            jax.ShapeDtypeStruct((ROWS, D), BF16),
            jax.ShapeDtypeStruct((1, 2 * HIST), I32),
            jax.ShapeDtypeStruct((NB, DEPTH, HD), BF16),
        ],
        in_specs=[VM] * 4 + [HBM],
        out_specs=[VM] * 3,
        scratch_shapes=[pltpu.VMEM((DEPTH, HD), BF16), pltpu.SemaphoreType.DMA(())],
        cost_estimate=pl.CostEstimate(flops=8 * ROWS * D, bytes_accessed=4 * ROWS * D, transcendentals=0),
        name="norm_rows",
    )(hist, cand, events, requests, w_proj)


def merge_kernel(mine_ref, other_ref, wout_ref, *rest, bit):
    out_ref, wout_out = rest[-2:]
    count = mine_ref.shape[0]
    first = lax.axis_index("seq") >> bit & 1 == 0
    out_ref[:count] = jnp.where(first, mine_ref[...], other_ref[...])
    out_ref[count:] = jnp.where(first, other_ref[...], mine_ref[...])
    half = wout_out.shape[0]
    wout_out[...] = wout_ref[pl.ds(pl.multiple_of(position()[2] * half, half), half), :]


def merge(mine, other, bit, w_out, ties):
    return pl.pallas_call(
        functools.partial(merge_kernel, bit=bit),
        out_shape=[
            jax.ShapeDtypeStruct((2 * mine.shape[0], mine.shape[1]), mine.dtype),
            jax.ShapeDtypeStruct((w_out.shape[0] // NC, D), w_out.dtype),
        ],
        in_specs=[VM] * (3 + len(ties)),
        out_specs=[VM] * 2,
        compiler_params=params(6),
        cost_estimate=pl.CostEstimate(flops=1 << 12, bytes_accessed=1 << 16, transcendentals=0),
        name="merge",
    )(mine, other, w_out, *ties)


def prepare_kernel(tq_ref, col_ref):
    for i in range(QROWS // 128):
        col_ref[i * 128 : (i + 1) * 128, :] = jnp.transpose(jnp.broadcast_to(tq_ref[i : i + 1, :], (128, 128)))


def prepare(tq):
    return pl.pallas_call(
        prepare_kernel,
        out_shape=jax.ShapeDtypeStruct((QROWS, 128), I32),
        in_specs=[VM],
        out_specs=VM,
        compiler_params=params(4),
        cost_estimate=pl.CostEstimate(flops=2 << 20, bytes_accessed=1 << 20, transcendentals=0),
        name="prepare",
    )(tq)


def half_silu(half):
    return half + half * jnp.tanh(half)


HALF = NP // 2


HALF = NP // 2


def project_kernel(rows_ref, *refs):
    parts, (qh_ref, qc_ref, kv_ref, own_ref, gate_ref, rows, weights, sems) = refs[:NX], refs[NX:]
    x = position()[0]
    hist, cand = HALF * HIST, HALF * CAND
    copies = []
    for place in range(NP):
        step, at = place // HALF, place % HALF
        copies.append(
            (
                pltpu.make_async_copy(
                    rows_ref.at[place, :HIST, :], rows.at[step, at * HIST : (at + 1) * HIST, :], sems.at[0, place]
                ),
                pltpu.make_async_copy(
                    rows_ref.at[place, HIST:, :],
                    rows.at[step, hist + at * CAND : hist + (at + 1) * CAND, :],
                    sems.at[1, place],
                ),
            )
        )
        for copy in copies[-1]:
            copy.start()
    for m in range(NX):
        at = pl.multiple_of((x + OFF[m]) % NX * DEPTH, DEPTH)
        for kind in range(4):
            weights[pl.ds(at, DEPTH), kind * HD : (kind + 1) * HD] = parts[m][kind]
    for step in range(NP // HALF):
        for pair in copies[step * HALF : (step + 1) * HALF]:
            for copy in pair:
                copy.wait()
        mixed = jnp.dot(rows[step], weights[:, 2 * HD :], preferred_element_type=F32)
        mixed = half_silu(0.5 * mixed)
        queries, keys = mixed[:, :HD], mixed[:, HD:]
        scaled = (queries * (0.5 * HD**-0.5)).astype(BF16)
        hists, cands = slice(step * hist, (step + 1) * hist), slice(step * cand, (step + 1) * cand)
        qh_ref[hists, :] = scaled[:hist]
        qc_ref[cands, :] = scaled[hist:]
        kv_ref[hists, :HD] = keys[:hist].astype(BF16)
        dots = queries[hist:].astype(BF16).astype(F32) * keys[hist:].astype(BF16).astype(F32)
        dots = jnp.sum(dots, axis=-1, keepdims=True)
        own = half_silu(dots * (0.5 * HD**-0.5)).astype(BF16).astype(F32)
        mixed = jnp.dot(rows[step], weights[:, : 2 * HD], preferred_element_type=F32)
        mixed = half_silu(0.5 * mixed).astype(BF16)
        kv_ref[hists, HD:] = mixed[:hist, HD:]
        own_ref[cands, :] = own * mixed[hist:, HD:].astype(F32)
        for at in range(HALF):
            place = step * HALF + at
            gate_ref[place, :HIST, :] = mixed[at * HIST : (at + 1) * HIST, :HD]
            gate_ref[place, HIST:, :] = mixed[hist + at * CAND : hist + (at + 1) * CAND, :HD]


def project(rows, parts):
    return pl.pallas_call(
        project_kernel,
        in_specs=[HBM] + [VM] * NX,
        out_specs=[VM] * 5,
        scratch_shapes=[
            pltpu.VMEM((NP // HALF, HALF * ROWS, D), BF16),
            pltpu.VMEM((D, 4 * HD), BF16),
            pltpu.SemaphoreType.DMA((2, NP)),
        ],
        out_shape=[
            jax.ShapeDtypeStruct((QH, HD), BF16),
            jax.ShapeDtypeStruct((QC, HD), BF16),
            jax.ShapeDtypeStruct((KEYS, 2 * HD), BF16),
            jax.ShapeDtypeStruct((QC, HD), F32),
            jax.ShapeDtypeStruct((NP, ROWS, HD), BF16),
        ],
        compiler_params=params(50),
        cost_estimate=pl.CostEstimate(flops=2 * QROWS * D * 4 * HD, bytes_accessed=6 << 20, transcendentals=QROWS * 4 * HD),
        name="project",
    )(rows, *parts)


BLOCK = 256
TILES = (QROWS // 128) * NP
STEPS = QROWS // BLOCK
STEP_TILES = TILES // STEPS


def attend_kernel(count_ref, work_ref, base_ref, steps_ref, qh_ref, qc_ref, sums_in, col_ref, *rest, fresh, last, chunks, start):
    arrays = sum(len(chunk) for chunk in chunks)
    gate_ref = rest[-4]
    kvs, tks = list(rest[:arrays]), rest[arrays : arrays + len(chunks)]
    out_ref, sums_ref, half_ref = rest[-3:]
    if fresh:
        sums_ref[:QH, :] = jnp.zeros((QH, HD), F32)
        sums_ref[QH:, :] = sums_in[...]
    else:
        sums_ref[...] = sums_in[...]
    row = lax.broadcasted_iota(I32, (128, 128), 0)
    lane = lax.broadcasted_iota(I32, (128, 128), 1)
    x = position()[0]
    froms = [(x + OFF[start + n]) % NX for n in range(len(chunks))]

    def scores(n, block, slot):
        first = block * BLOCK
        begin = 0
        for kv in parts[n]:
            keys = kv.shape[0]
            queries = qc_ref[first - QH : first - QH + BLOCK, :] if first >= QH else qh_ref[first : first + BLOCK, :]
            half = lax.dot_general(
                queries, kv[:, :HD], (((1,), (1,)), ((), ())), preferred_element_type=F32
            )
            for i in range(BLOCK // 128):
                for j in range(keys // 128):
                    at = (start + n) * TILES + (block * (BLOCK // 128) + i) * NP + begin // 128 + j
                    half_ref[slot, i * 128 : (i + 1) * 128, begin + j * 128 : begin + (j + 1) * 128] = (
                        half[i * 128 : (i + 1) * 128, j * 128 : (j + 1) * 128] + base_ref[at]
                    )
            begin += keys

    def correct(n, block, slot):
        is_cand = block * BLOCK >= QH

        def tile(k, carry):
            code = work_ref[(start + n) * TILES + block * STEP_TILES + k]
            i, j = (code >> 3) & 1, code & 7
            time_low, time_high, place_low, place_high = [(code >> bit) & 15 for bit in (4, 8, 12, 16)]
            if True:
                rows = pl.ds(pl.multiple_of(i * 128, 128), 128)
                columns = pl.ds(pl.multiple_of(j * 128, 128), 128)
                first = pl.multiple_of(block * BLOCK + i * 128, 128)
                value = half_ref[slot, rows, columns]
                gap = col_ref[pl.ds(first, 128), :] - tks[n][pl.ds(j, 1), :]

                def time_step(level, value):
                    return value + jnp.where(gap >= (1 << (2 * level)), steps_ref[level], 0.0)

                value = lax.fori_loop(time_low, time_high, time_step, value)
                if is_cand:
                    gap2 = (LENGTH - froms[n] * KEYS - j * 128) - lane
                else:
                    gap2 = ((x - froms[n]) * KEYS + (block * (BLOCK // 128) + i - j) * 128) + row - lane

                def place_step(level, value):
                    return value + jnp.where(gap2 >= (1 << level), steps_ref[LEVELS + level], 0.0)

                value = lax.fori_loop(place_low, place_high, place_step, value)
                if not is_cand:
                    value = jnp.where(gap2 >= 0, value, MASKED)
                half_ref[slot, rows, columns] = value

            return carry

        lax.fori_loop(0, count_ref[(start + n) * STEPS + block], tile, 0)

    def combine(n, block, slot):
        first = block * BLOCK
        begin = 0
        total = sums_ref[first : first + BLOCK, :]
        for kv in parts[n]:
            keys = kv.shape[0]
            weights = half_silu(half_ref[slot, :, begin : begin + keys]).astype(BF16)
            total = total + jnp.dot(weights, kv[:, HD:], preferred_element_type=F32)
            begin += keys
        sums_ref[first : first + BLOCK, :] = total

    def sweep(n, blocks):
        for k, block in enumerate(blocks):
            scores(n, block, k % 2)
            if k > 0:
                combine(n, blocks[k - 1], (k - 1) % 2)
            correct(n, block, k % 2)
        combine(n, blocks[-1], (len(blocks) - 1) % 2)

    parts = []
    for chunk in chunks:
        parts.append([kvs.pop(0) for _ in chunk])
    for n in range(len(chunks)):

        @pl.when(froms[n] <= x)
        def _():
            sweep(n, list(range(QROWS // BLOCK)))

        @pl.when(froms[n] > x)
        def _():
            sweep(n, [QROWS // BLOCK - 1])

    if last:
        for place in range(NP):
            out_ref[place, :HIST, :HD] = sums_ref[place * HIST : (place + 1) * HIST, :].astype(BF16)
            out_ref[place, HIST:, :HD] = sums_ref[QH + place * CAND : QH + (place + 1) * CAND, :].astype(BF16)
            out_ref[place, :, HD:] = gate_ref[place]
    else:
        out_ref[...] = sums_ref[...]


def attend(tables, queries, sums, col, chunks, tks, start, gates=None):
    fresh, last = start == 0, gates is not None
    gates = [gates] if last else []
    kvs = [kv for chunk in chunks for kv in chunk]
    shapes = tuple(tuple(kv.shape[0] for kv in chunk) for chunk in chunks)
    keys = sum(kv.shape[0] for kv in kvs)
    return pl.pallas_call(
        functools.partial(attend_kernel, fresh=fresh, last=last, chunks=shapes, start=start),
        in_specs=[SM] * 4 + [VM] * (4 + len(kvs) + len(tks) + len(gates)),
        out_specs=VM,
        out_shape=jax.ShapeDtypeStruct((NP, ROWS, 2 * HD), BF16) if last else jax.ShapeDtypeStruct((QROWS, HD), F32),
        scratch_shapes=[pltpu.VMEM((QROWS, HD), F32), pltpu.VMEM((2, BLOCK, KEYS), F32)],
        compiler_params=params(16),
        cost_estimate=pl.CostEstimate(
            flops=16 * QROWS * keys * HD, bytes_accessed=4 * QROWS * keys, transcendentals=QROWS * keys
        ),
        name="attend",
    )(*tables, *queries, sums, col, *kvs, *tks, *gates)


def finish_kernel(hist_ref, cand_ref, pair_ref, mine_ref, other_ref, hist_out, cand_out, w_ref, sems):
    core = position()[2]
    copies = [
        pltpu.make_async_copy(mine_ref, w_ref.at[:, core], sems.at[0]),
        pltpu.make_async_copy(other_ref, w_ref.at[:, 1 - core], sems.at[1]),
    ]
    for copy in copies:
        copy.start()
    parts = [pair_ref[h, :, :HD].astype(F32) for h in range(HEADS)]
    center = sum(jnp.sum(part, axis=-1, keepdims=True) for part in parts) * (1.0 / D)
    parts = [part - center for part in parts]
    spread = sum(jnp.sum(part * part, axis=-1, keepdims=True) for part in parts) * (1.0 / D)
    scale = lax.rsqrt(spread + 1e-6)
    parts = [(part * scale * pair_ref[h, :, HD:].astype(F32)).astype(BF16) for h, part in enumerate(parts)]
    for copy in copies:
        copy.wait()
    total = jnp.dot(jnp.concatenate(parts, axis=1), w_ref[...].reshape(D, D), preferred_element_type=F32)
    hist_out[0] = (hist_ref[0].astype(F32) + total[:HIST]).astype(BF16)
    cand_out[0] = (cand_ref[0].astype(F32) + total[HIST:]).astype(BF16)


def finish(hist, cand, mine, other, pairs):
    return pl.pallas_call(
        finish_kernel,
        out_shape=[
            jax.ShapeDtypeStruct((1, HIST, D), BF16),
            jax.ShapeDtypeStruct((1, CAND, D), BF16),
        ],
        in_specs=[VM] * 3 + [HBM] * 2,
        out_specs=[VM, VM],
        scratch_shapes=[pltpu.VMEM((NB, NC, D // NB // NC, D), BF16), pltpu.SemaphoreType.DMA((2,))],
        compiler_params=params(12),
        cost_estimate=pl.CostEstimate(flops=2 * ROWS * D * D, bytes_accessed=4 << 20, transcendentals=0),
        name="finish",
    )(hist, cand, pairs, mine, other)


def gather_weights(shards, z):
    shards = lax.all_to_all(shards, "batch", 0, 0)
    return lax.dynamic_index_in_dim(shards.reshape(4, 2, DEPTH, HD), z // 2, axis=1, keepdims=False)


def body(history, candidates, event_times, request_times, w_proj, w_out, bias_steps):
    seq = lax.axis_index("seq")
    x, z, core = position()
    head = NC * z + core
    xs = jnp.stack([(x + off) % NX for off in OFF])

    n0, t0, shards = norm_rows(history, candidates, event_times, request_times, w_proj)
    rows = lax.all_gather(n0, "seq", axis_index_groups=SAME_X)

    w0 = gather_weights(shards, z)
    w_parts = [w0, shift(w0, dx=1), shift(w0, dx=-1), shift(w0, dx=2)]

    times = t0
    order = (3, 4, 0, 1, 2)
    for bit in order:
        other = lax.ppermute(times, "seq", [(s, s ^ (1 << bit)) for s in range(NS)])
        if bit == order[-2]:
            times, w_mine = merge(times, other, bit, w_out, w_parts[1:])
            w_half = lax.all_gather(w_mine, "batch")
            w_other = shift(w_half, flip=True)
        else:
            first = seq >> bit & 1 == 0
            times = jnp.concatenate([jnp.where(first, times, other), jnp.where(first, other, times)], axis=0)
    times = times.reshape(ZH, NC, NX, 2 * HIST).transpose(2, 0, 1, 3).reshape(NX, NP, 2 * HIST)
    t8 = jnp.sum(jnp.where((x == jnp.arange(NX))[:, None, None], times, 0), axis=0)
    k0 = t8[:, :HIST]
    tks = [jnp.sum(jnp.where((xs[m] == jnp.arange(NX))[:, None, None], times[..., :HIST], 0), axis=0) for m in range(NX)]
    cand_times = t8[:, HIST:ROWS].reshape(QC // 128, 128)

    qh, qc, kv0, own, gates = project(rows, w_parts)

    steps = 0.5 * lax.dynamic_slice(bias_steps, (0, head), (2 * LEVELS, 1))[:, 0]
    level = jnp.arange(LEVELS, dtype=I32)
    tie = (kv0[0, 0] * 0).astype(I32)
    tk = jnp.stack(tks) + tie
    tq = jnp.concatenate([k0, cand_times, jnp.zeros((6, 128), I32)], axis=0) + tie
    first_q = jnp.concatenate([k0[:, 0], jnp.min(cand_times, axis=1)]) + tie
    last_q = jnp.concatenate([k0[:, -1], jnp.max(cand_times, axis=1)]) + tie

    def passed(gap, marks):
        return jnp.sum((gap[..., None] >= marks).astype(I32), axis=-1)

    time_low = passed(first_q[None, :, None] - tk[:, None, :, -1], 4**level)
    time_high = passed(last_q[None, :, None] - tk[:, None, :, 0], 4**level)
    blocks = jnp.arange(NP, dtype=I32)
    hist_gap = ((x - xs)[:, None, None] * NP + blocks[None, :, None] - blocks[None, None, :]) * HIST
    cand_gap = LENGTH - (xs[:, None, None] * NP + blocks[None, None, :]) * HIST
    cand_gap = jnp.broadcast_to(cand_gap, (NX, QC // 128, NP))
    place_low = passed(jnp.concatenate([hist_gap, cand_gap], axis=1) - (HIST - 1), 2**level)
    place_high = passed(jnp.concatenate([hist_gap + (HIST - 1), cand_gap], axis=1), 2**level)
    hidden = jnp.concatenate([hist_gap < 0, cand_gap < 0], axis=1)
    code = time_low | (time_high << 4) | (place_low << 8) | (place_high << 12)
    mixed = ~hidden & ((time_low != time_high) | (place_low != place_high))
    number = jnp.arange(STEP_TILES, dtype=I32)
    code = (code << 4 | number.reshape(BLOCK // 128, NP)[jnp.arange(QROWS // 128) % (BLOCK // 128)]).reshape(NX, STEPS, STEP_TILES)
    mixed = mixed.reshape(NX, STEPS, STEP_TILES)
    rank = jnp.sum(jnp.where(number[None, :] < number[:, None], mixed[..., None, :].astype(I32), 0), axis=-1)
    spot = mixed[..., None] & (rank[..., None] == number)
    works = jnp.sum(jnp.where(spot, code[..., None], 0), axis=-2).reshape(NX, TILES)
    counts = jnp.sum(mixed.astype(I32), axis=-1)
    base = jnp.sum(jnp.where(time_low[..., None] > level, steps[:LEVELS], 0.0), axis=-1)
    base = base + jnp.sum(jnp.where(place_low[..., None] > level, steps[LEVELS:], 0.0), axis=-1)
    base = jnp.where(hidden, MASKED, base).reshape(NX, TILES)
    col = prepare(tq)
    tables = (counts.reshape(-1), works.reshape(-1), base.reshape(-1), steps)

    queries = (qh, qc)
    kv1, kv2 = shift(kv0, dx=1), shift(kv0, dx=-1)
    part = KEYS // 2
    kv3a, kv3b = shift(kv1[:part], dx=1), shift(kv2[part:], dx=-1)
    sums = attend(tables, queries, own, col, [[kv0]], tks[:1], 0)
    sums = attend(tables, queries, sums, col, [[kv1], [kv2]], tks[1:3], 1)
    att = attend(tables, queries, sums, col, [[kv3a, kv3b]], tks[3:], 3, gates)
    atts = lax.all_to_all(att, "seq", 0, 0, axis_index_groups=SAME_X)
    return tuple(finish(history, candidates, w_half, w_other, atts))


def solution(mesh):
    in_specs = (
        P("batch", "seq", None),
        P("batch", "seq", None),
        P("batch", "seq"),
        P("batch", "seq"),
        P(None, "batch"),
        P("batch", None),
        P(),
    )
    out_specs = (P("batch", "seq", None), P("batch", "seq", None))
    return jax.shard_map(body, mesh=mesh, in_specs=in_specs, out_specs=out_specs, check_vma=False)
```

```python
import functools

import jax
import jax.numpy as jnp
from jax import lax
from jax.experimental import pallas as pl
from jax.experimental.pallas import tpu as pltpu
from jax.sharding import PartitionSpec as P

F32, BF16, I32 = jnp.float32, jnp.bfloat16, jnp.int32
ZL, NY, NX, ZH, NC = 2, 4, 4, 4, 2
NB, NS = ZL * NY, NX * ZH * NC
OFF = (0, -1, 1, 2)
HEADS, HD, D = 8, 128, 1024
HIST, CAND = 128, 32
ROWS = HIST + CAND
NP = ZH * NC
QH, QC = NP * HIST, NP * CAND
QROWS = QH + QC
KEYS = NP * HIST
LENGTH = NS * HIST
LEVELS = 12
MASKED = -1e30
SAME_X = [[x * NP + p for p in range(NP)] for x in range(NX)]
VM = pl.BlockSpec(memory_space=pltpu.VMEM)
SM = pl.BlockSpec(memory_space=pltpu.SMEM)
HBM = pl.BlockSpec(memory_space=pl.ANY)
DEPTH = D // NX


def params(mib):
    return pltpu.CompilerParams(vmem_limit_bytes=mib << 20)


def position():
    seq = lax.axis_index("seq")
    return seq // (ZH * NC), seq // NC % ZH, seq % NC


def seq_perm(dx=0, dz=0, flip=False):
    pairs = []
    for s in range(NS):
        x, z, c = s // (ZH * NC), s // NC % ZH, s % NC
        t = ((x + dx) % NX * ZH + (z + dz) % ZH) * NC + (c ^ int(flip))
        pairs.append((s, t))
    return pairs


def shift(array, dx=0, dz=0, flip=False):
    return lax.ppermute(array, "seq", seq_perm(dx, dz, flip))


def norm_kernel(hist_ref, cand_ref, events_ref, requests_ref, proj_ref, out_ref, times_ref, shards_ref, part_ref, sem):
    x, z, core = position()
    column = pl.multiple_of((NC * z + core) % 4 * HD, HD)
    copy = pltpu.make_async_copy(
        proj_ref.at[pl.ds(pl.multiple_of(x * DEPTH, DEPTH), DEPTH), pl.ds(column, HD)], part_ref, sem
    )
    copy.start()
    for ref, first, count in ((hist_ref, 0, HIST), (cand_ref, HIST, CAND)):
        rows = ref[0].astype(F32)
        rows = rows - jnp.mean(rows, axis=-1, keepdims=True)
        spread = jnp.mean(rows * rows, axis=-1, keepdims=True)
        out_ref[first : first + count, :] = (rows * lax.rsqrt(spread + 1e-6)).astype(BF16)
    times_ref[...] = jnp.zeros_like(times_ref)
    times_ref[:, :HIST] = events_ref[...]
    times_ref[:, HIST:ROWS] = requests_ref[...]
    copy.wait()
    for b in range(NB):
        shards_ref[b] = part_ref[...]


def norm_rows(hist, cand, events, requests, w_proj):
    return pl.pallas_call(
        norm_kernel,
        out_shape=[
            jax.ShapeDtypeStruct((ROWS, D), BF16),
            jax.ShapeDtypeStruct((1, 2 * HIST), I32),
            jax.ShapeDtypeStruct((NB, DEPTH, HD), BF16),
        ],
        in_specs=[VM] * 4 + [HBM],
        out_specs=[VM] * 3,
        scratch_shapes=[pltpu.VMEM((DEPTH, HD), BF16), pltpu.SemaphoreType.DMA(())],
        cost_estimate=pl.CostEstimate(flops=8 * ROWS * D, bytes_accessed=4 * ROWS * D, transcendentals=0),
        name="norm_rows",
    )(hist, cand, events, requests, w_proj)


def merge_kernel(mine_ref, other_ref, wout_ref, *rest, bit):
    out_ref, wout_out = rest[-2:]
    count = mine_ref.shape[0]
    first = lax.axis_index("seq") >> bit & 1 == 0
    out_ref[:count] = jnp.where(first, mine_ref[...], other_ref[...])
    out_ref[count:] = jnp.where(first, other_ref[...], mine_ref[...])
    half = wout_out.shape[0]
    wout_out[...] = wout_ref[pl.ds(pl.multiple_of(position()[2] * half, half), half), :]


def merge(mine, other, bit, w_out, ties):
    return pl.pallas_call(
        functools.partial(merge_kernel, bit=bit),
        out_shape=[
            jax.ShapeDtypeStruct((2 * mine.shape[0], mine.shape[1]), mine.dtype),
            jax.ShapeDtypeStruct((w_out.shape[0] // NC, D), w_out.dtype),
        ],
        in_specs=[VM] * (3 + len(ties)),
        out_specs=[VM] * 2,
        compiler_params=params(6),
        cost_estimate=pl.CostEstimate(flops=1 << 12, bytes_accessed=1 << 16, transcendentals=0),
        name="merge",
    )(mine, other, w_out, *ties)


def prepare_kernel(tq_ref, col_ref):
    for i in range(QROWS // 128):
        col_ref[i * 128 : (i + 1) * 128, :] = jnp.transpose(jnp.broadcast_to(tq_ref[i : i + 1, :], (128, 128)))


def prepare(tq):
    return pl.pallas_call(
        prepare_kernel,
        out_shape=jax.ShapeDtypeStruct((QROWS, 128), I32),
        in_specs=[VM],
        out_specs=VM,
        compiler_params=params(4),
        cost_estimate=pl.CostEstimate(flops=2 << 20, bytes_accessed=1 << 20, transcendentals=0),
        name="prepare",
    )(tq)


def half_silu(half):
    return half + half * jnp.tanh(half)


HALF = NP // 2


HALF = NP // 2


def project_kernel(rows_ref, *refs):
    parts, (qh_ref, qc_ref, kv_ref, own_ref, gate_ref, rows, weights, sems) = refs[:NX], refs[NX:]
    x = position()[0]
    hist, cand = HALF * HIST, HALF * CAND
    copies = []
    for place in range(NP):
        step, at = place // HALF, place % HALF
        copies.append(
            (
                pltpu.make_async_copy(
                    rows_ref.at[place, :HIST, :], rows.at[step, at * HIST : (at + 1) * HIST, :], sems.at[0, place]
                ),
                pltpu.make_async_copy(
                    rows_ref.at[place, HIST:, :],
                    rows.at[step, hist + at * CAND : hist + (at + 1) * CAND, :],
                    sems.at[1, place],
                ),
            )
        )
        for copy in copies[-1]:
            copy.start()
    for m in range(NX):
        at = pl.multiple_of((x + OFF[m]) % NX * DEPTH, DEPTH)
        for kind in range(4):
            weights[pl.ds(at, DEPTH), kind * HD : (kind + 1) * HD] = parts[m][kind]
    for step in range(NP // HALF):
        for pair in copies[step * HALF : (step + 1) * HALF]:
            for copy in pair:
                copy.wait()
        mixed = jnp.dot(rows[step], weights[:, 2 * HD :], preferred_element_type=F32)
        mixed = half_silu(0.5 * mixed)
        queries, keys = mixed[:, :HD], mixed[:, HD:]
        scaled = (queries * (0.5 * HD**-0.5)).astype(BF16)
        hists, cands = slice(step * hist, (step + 1) * hist), slice(step * cand, (step + 1) * cand)
        qh_ref[hists, :] = scaled[:hist]
        qc_ref[cands, :] = scaled[hist:]
        kv_ref[hists, :HD] = keys[:hist].astype(BF16)
        dots = queries[hist:].astype(BF16).astype(F32) * keys[hist:].astype(BF16).astype(F32)
        dots = jnp.sum(dots, axis=-1, keepdims=True)
        own = half_silu(dots * (0.5 * HD**-0.5)).astype(BF16).astype(F32)
        mixed = jnp.dot(rows[step], weights[:, : 2 * HD], preferred_element_type=F32)
        mixed = half_silu(0.5 * mixed).astype(BF16)
        kv_ref[hists, HD:] = mixed[:hist, HD:]
        own_ref[cands, :] = own * mixed[hist:, HD:].astype(F32)
        for at in range(HALF):
            place = step * HALF + at
            gate_ref[place, :HIST, :] = mixed[at * HIST : (at + 1) * HIST, :HD]
            gate_ref[place, HIST:, :] = mixed[hist + at * CAND : hist + (at + 1) * CAND, :HD]


def project(rows, parts):
    return pl.pallas_call(
        project_kernel,
        in_specs=[HBM] + [VM] * NX,
        out_specs=[VM] * 5,
        scratch_shapes=[
            pltpu.VMEM((NP // HALF, HALF * ROWS, D), BF16),
            pltpu.VMEM((D, 4 * HD), BF16),
            pltpu.SemaphoreType.DMA((2, NP)),
        ],
        out_shape=[
            jax.ShapeDtypeStruct((QH, HD), BF16),
            jax.ShapeDtypeStruct((QC, HD), BF16),
            jax.ShapeDtypeStruct((KEYS, 2 * HD), BF16),
            jax.ShapeDtypeStruct((QC, HD), F32),
            jax.ShapeDtypeStruct((NP, ROWS, HD), BF16),
        ],
        compiler_params=params(50),
        cost_estimate=pl.CostEstimate(flops=2 * QROWS * D * 4 * HD, bytes_accessed=6 << 20, transcendentals=QROWS * 4 * HD),
        name="project",
    )(rows, *parts)


BLOCK = 256
TILES = (QROWS // 128) * NP
STEPS = QROWS // BLOCK
STEP_TILES = TILES // STEPS


def attend_kernel(count_ref, work_ref, base_ref, steps_ref, qh_ref, qc_ref, sums_in, col_ref, *rest, fresh, last, chunks, start):
    arrays = sum(len(chunk) for chunk in chunks)
    gate_ref = rest[-4]
    kvs, tks = list(rest[:arrays]), rest[arrays : arrays + len(chunks)]
    out_ref, sums_ref, half_ref = rest[-3:]
    if fresh:
        sums_ref[:QH, :] = jnp.zeros((QH, HD), F32)
        sums_ref[QH:, :] = sums_in[...]
    else:
        sums_ref[...] = sums_in[...]
    row = lax.broadcasted_iota(I32, (128, 128), 0)
    lane = lax.broadcasted_iota(I32, (128, 128), 1)
    x = position()[0]
    froms = [(x + OFF[start + n]) % NX for n in range(len(chunks))]

    def scores(n, block, slot):
        first = block * BLOCK
        begin = 0
        for kv in parts[n]:
            keys = kv.shape[0]
            queries = qc_ref[first - QH : first - QH + BLOCK, :] if first >= QH else qh_ref[first : first + BLOCK, :]
            half = lax.dot_general(
                queries, kv[:, :HD], (((1,), (1,)), ((), ())), preferred_element_type=F32
            )
            for i in range(BLOCK // 128):
                for j in range(keys // 128):
                    at = (start + n) * TILES + (block * (BLOCK // 128) + i) * NP + begin // 128 + j
                    half_ref[slot, i * 128 : (i + 1) * 128, begin + j * 128 : begin + (j + 1) * 128] = (
                        half[i * 128 : (i + 1) * 128, j * 128 : (j + 1) * 128] + base_ref[at]
                    )
            begin += keys

    def correct(n, block, slot):
        is_cand = block * BLOCK >= QH

        def tile(k, carry):
            code = work_ref[(start + n) * TILES + block * STEP_TILES + k]
            i, j = (code >> 3) & 1, code & 7
            time_low, time_high, place_low, place_high = [(code >> bit) & 15 for bit in (4, 8, 12, 16)]
            if True:
                rows = pl.ds(pl.multiple_of(i * 128, 128), 128)
                columns = pl.ds(pl.multiple_of(j * 128, 128), 128)
                first = pl.multiple_of(block * BLOCK + i * 128, 128)
                value = half_ref[slot, rows, columns]
                gap = col_ref[pl.ds(first, 128), :] - tks[n][pl.ds(j, 1), :]

                def time_step(level, value):
                    return value + jnp.where(gap >= (1 << (2 * level)), steps_ref[level], 0.0)

                value = lax.fori_loop(time_low, time_high, time_step, value)
                if is_cand:
                    gap2 = (LENGTH - froms[n] * KEYS - j * 128) - lane
                else:
                    gap2 = ((x - froms[n]) * KEYS + (block * (BLOCK // 128) + i - j) * 128) + row - lane

                def place_step(level, value):
                    return value + jnp.where(gap2 >= (1 << level), steps_ref[LEVELS + level], 0.0)

                value = lax.fori_loop(place_low, place_high, place_step, value)
                if not is_cand:
                    value = jnp.where(gap2 >= 0, value, MASKED)
                half_ref[slot, rows, columns] = value

            return carry

        lax.fori_loop(0, count_ref[(start + n) * STEPS + block], tile, 0)

    def combine(n, block, slot):
        first = block * BLOCK
        begin = 0
        total = sums_ref[first : first + BLOCK, :]
        for kv in parts[n]:
            keys = kv.shape[0]
            weights = half_silu(half_ref[slot, :, begin : begin + keys]).astype(BF16)
            total = total + jnp.dot(weights, kv[:, HD:], preferred_element_type=F32)
            begin += keys
        sums_ref[first : first + BLOCK, :] = total

    def sweep(n, blocks):
        for k, block in enumerate(blocks):
            scores(n, block, k % 2)
            if k > 0:
                combine(n, blocks[k - 1], (k - 1) % 2)
            correct(n, block, k % 2)
        combine(n, blocks[-1], (len(blocks) - 1) % 2)

    parts = []
    for chunk in chunks:
        parts.append([kvs.pop(0) for _ in chunk])
    for n in range(len(chunks)):

        @pl.when(froms[n] <= x)
        def _():
            sweep(n, list(range(QROWS // BLOCK)))

        @pl.when(froms[n] > x)
        def _():
            sweep(n, [QROWS // BLOCK - 1])

    if last:
        for place in range(NP):
            out_ref[place, :HIST, :HD] = sums_ref[place * HIST : (place + 1) * HIST, :].astype(BF16)
            out_ref[place, HIST:, :HD] = sums_ref[QH + place * CAND : QH + (place + 1) * CAND, :].astype(BF16)
            out_ref[place, :, HD:] = gate_ref[place]
    else:
        out_ref[...] = sums_ref[...]


def attend(tables, queries, sums, col, chunks, tks, start, gates=None):
    fresh, last = start == 0, gates is not None
    gates = [gates] if last else []
    kvs = [kv for chunk in chunks for kv in chunk]
    shapes = tuple(tuple(kv.shape[0] for kv in chunk) for chunk in chunks)
    keys = sum(kv.shape[0] for kv in kvs)
    return pl.pallas_call(
        functools.partial(attend_kernel, fresh=fresh, last=last, chunks=shapes, start=start),
        in_specs=[SM] * 4 + [VM] * (4 + len(kvs) + len(tks) + len(gates)),
        out_specs=VM,
        out_shape=jax.ShapeDtypeStruct((NP, ROWS, 2 * HD), BF16) if last else jax.ShapeDtypeStruct((QROWS, HD), F32),
        scratch_shapes=[pltpu.VMEM((QROWS, HD), F32), pltpu.VMEM((2, BLOCK, KEYS), F32)],
        compiler_params=params(16),
        cost_estimate=pl.CostEstimate(
            flops=16 * QROWS * keys * HD, bytes_accessed=4 * QROWS * keys, transcendentals=QROWS * keys
        ),
        name="attend",
    )(*tables, *queries, sums, col, *kvs, *tks, *gates)


def finish_kernel(hist_ref, cand_ref, pair_ref, mine_ref, other_ref, hist_out, cand_out, w_ref, sems):
    core = position()[2]
    copies = [
        pltpu.make_async_copy(mine_ref, w_ref.at[:, core], sems.at[0]),
        pltpu.make_async_copy(other_ref, w_ref.at[:, 1 - core], sems.at[1]),
    ]
    for copy in copies:
        copy.start()
    parts = [pair_ref[h, :, :HD].astype(F32) for h in range(HEADS)]
    center = sum(jnp.sum(part, axis=-1, keepdims=True) for part in parts) * (1.0 / D)
    parts = [part - center for part in parts]
    spread = sum(jnp.sum(part * part, axis=-1, keepdims=True) for part in parts) * (1.0 / D)
    scale = lax.rsqrt(spread + 1e-6)
    parts = [(part * scale * pair_ref[h, :, HD:].astype(F32)).astype(BF16) for h, part in enumerate(parts)]
    for copy in copies:
        copy.wait()
    total = jnp.dot(jnp.concatenate(parts, axis=1), w_ref[...].reshape(D, D), preferred_element_type=F32)
    hist_out[0] = (hist_ref[0].astype(F32) + total[:HIST]).astype(BF16)
    cand_out[0] = (cand_ref[0].astype(F32) + total[HIST:]).astype(BF16)


def finish(hist, cand, mine, other, pairs):
    return pl.pallas_call(
        finish_kernel,
        out_shape=[
            jax.ShapeDtypeStruct((1, HIST, D), BF16),
            jax.ShapeDtypeStruct((1, CAND, D), BF16),
        ],
        in_specs=[VM] * 3 + [HBM] * 2,
        out_specs=[VM, VM],
        scratch_shapes=[pltpu.VMEM((NB, NC, D // NB // NC, D), BF16), pltpu.SemaphoreType.DMA((2,))],
        compiler_params=params(12),
        cost_estimate=pl.CostEstimate(flops=2 * ROWS * D * D, bytes_accessed=4 << 20, transcendentals=0),
        name="finish",
    )(hist, cand, pairs, mine, other)


def gather_weights(shards, z):
    shards = lax.all_to_all(shards, "batch", 0, 0)
    return lax.dynamic_index_in_dim(shards.reshape(4, 2, DEPTH, HD), z // 2, axis=1, keepdims=False)


def body(history, candidates, event_times, request_times, w_proj, w_out, bias_steps):
    seq = lax.axis_index("seq")
    x, z, core = position()
    head = NC * z + core
    xs = jnp.stack([(x + off) % NX for off in OFF])

    n0, t0, shards = norm_rows(history, candidates, event_times, request_times, w_proj)
    rows = lax.all_gather(n0, "seq", axis_index_groups=SAME_X)

    w0 = gather_weights(shards, z)
    w_parts = [w0, shift(w0, dx=1), shift(w0, dx=-1), shift(w0, dx=2)]

    times = t0
    order = (3, 4, 0, 1, 2)
    for bit in order:
        other = lax.ppermute(times, "seq", [(s, s ^ (1 << bit)) for s in range(NS)])
        if bit == order[-2]:
            times, w_mine = merge(times, other, bit, w_out, w_parts[1:])
            w_half = lax.all_gather(w_mine, "batch")
            w_other = shift(w_half, flip=True)
        else:
            first = seq >> bit & 1 == 0
            times = jnp.concatenate([jnp.where(first, times, other), jnp.where(first, other, times)], axis=0)
    times = times.reshape(ZH, NC, NX, 2 * HIST).transpose(2, 0, 1, 3).reshape(NX, NP, 2 * HIST)
    t8 = jnp.sum(jnp.where((x == jnp.arange(NX))[:, None, None], times, 0), axis=0)
    k0 = t8[:, :HIST]
    tks = [jnp.sum(jnp.where((xs[m] == jnp.arange(NX))[:, None, None], times[..., :HIST], 0), axis=0) for m in range(NX)]
    cand_times = t8[:, HIST:ROWS].reshape(QC // 128, 128)

    qh, qc, kv0, own, gates = project(rows, w_parts)

    steps = 0.5 * lax.dynamic_slice(bias_steps, (0, head), (2 * LEVELS, 1))[:, 0]
    level = jnp.arange(LEVELS, dtype=I32)
    tk = jnp.stack(tks)
    tq = jnp.concatenate([k0, cand_times, jnp.zeros((6, 128), I32)], axis=0)
    first_q = jnp.concatenate([k0[:, 0], jnp.min(cand_times, axis=1)])
    last_q = jnp.concatenate([k0[:, -1], jnp.max(cand_times, axis=1)])

    def passed(gap, marks):
        return jnp.sum((gap[..., None] >= marks).astype(I32), axis=-1)

    time_low = passed(first_q[None, :, None] - tk[:, None, :, -1], 4**level)
    time_high = passed(last_q[None, :, None] - tk[:, None, :, 0], 4**level)
    blocks = jnp.arange(NP, dtype=I32)
    hist_gap = ((x - xs)[:, None, None] * NP + blocks[None, :, None] - blocks[None, None, :]) * HIST
    cand_gap = LENGTH - (xs[:, None, None] * NP + blocks[None, None, :]) * HIST
    cand_gap = jnp.broadcast_to(cand_gap, (NX, QC // 128, NP))
    place_low = passed(jnp.concatenate([hist_gap, cand_gap], axis=1) - (HIST - 1), 2**level)
    place_high = passed(jnp.concatenate([hist_gap + (HIST - 1), cand_gap], axis=1), 2**level)
    hidden = jnp.concatenate([hist_gap < 0, cand_gap < 0], axis=1)
    code = time_low | (time_high << 4) | (place_low << 8) | (place_high << 12)
    mixed = ~hidden & ((time_low != time_high) | (place_low != place_high))
    number = jnp.arange(STEP_TILES, dtype=I32)
    code = (code << 4 | number.reshape(BLOCK // 128, NP)[jnp.arange(QROWS // 128) % (BLOCK // 128)]).reshape(NX, STEPS, STEP_TILES)
    mixed = mixed.reshape(NX, STEPS, STEP_TILES)
    rank = jnp.sum(jnp.where(number[None, :] < number[:, None], mixed[..., None, :].astype(I32), 0), axis=-1)
    spot = mixed[..., None] & (rank[..., None] == number)
    works = jnp.sum(jnp.where(spot, code[..., None], 0), axis=-2).reshape(NX, TILES)
    counts = jnp.sum(mixed.astype(I32), axis=-1)
    base = jnp.sum(jnp.where(time_low[..., None] > level, steps[:LEVELS], 0.0), axis=-1)
    base = base + jnp.sum(jnp.where(place_low[..., None] > level, steps[LEVELS:], 0.0), axis=-1)
    base = jnp.where(hidden, MASKED, base).reshape(NX, TILES)
    col = prepare(tq)
    tables = (counts.reshape(-1), works.reshape(-1), base.reshape(-1), steps)

    queries = (qh, qc)
    kv1, kv2 = shift(kv0, dx=1), shift(kv0, dx=-1)
    part = KEYS // 2
    kv3a, kv3b = shift(kv1[:part], dx=1), shift(kv2[part:], dx=-1)
    sums = attend(tables, queries, own, col, [[kv0]], tks[:1], 0)
    sums = attend(tables, queries, sums, col, [[kv1], [kv2]], tks[1:3], 1)
    att = attend(tables, queries, sums, col, [[kv3a, kv3b]], tks[3:], 3, gates)
    atts = lax.all_to_all(att, "seq", 0, 0, axis_index_groups=SAME_X)
    return tuple(finish(history, candidates, w_half, w_other, atts))


def solution(mesh):
    in_specs = (
        P("batch", "seq", None),
        P("batch", "seq", None),
        P("batch", "seq"),
        P("batch", "seq"),
        P(None, "batch"),
        P("batch", None),
        P(),
    )
    out_specs = (P("batch", "seq", None), P("batch", "seq", None))
    return jax.shard_map(body, mesh=mesh, in_specs=in_specs, out_specs=out_specs, check_vma=False)
```

```python
import functools

import jax
import jax.numpy as jnp
from jax import lax
from jax.experimental import pallas as pl
from jax.experimental.pallas import tpu as pltpu
from jax.sharding import PartitionSpec as P

F32, BF16, I32 = jnp.float32, jnp.bfloat16, jnp.int32
ZL, NY, NX, ZH, NC = 2, 4, 4, 4, 2
NB, NS = ZL * NY, NX * ZH * NC
OFF = (0, -1, 1, 2)
HEADS, HD, D = 8, 128, 1024
HIST, CAND = 128, 32
ROWS = HIST + CAND
NP = ZH * NC
QH, QC = NP * HIST, NP * CAND
QROWS = QH + QC
KEYS = NP * HIST
LENGTH = NS * HIST
LEVELS = 12
MASKED = -1e30
SAME_X = [[x * NP + p for p in range(NP)] for x in range(NX)]
VM = pl.BlockSpec(memory_space=pltpu.VMEM)
SM = pl.BlockSpec(memory_space=pltpu.SMEM)
HBM = pl.BlockSpec(memory_space=pl.ANY)
DEPTH = D // NX


def params(mib):
    return pltpu.CompilerParams(vmem_limit_bytes=mib << 20)


def position():
    seq = lax.axis_index("seq")
    return seq // (ZH * NC), seq // NC % ZH, seq % NC


def seq_perm(dx=0, dz=0, flip=False):
    pairs = []
    for s in range(NS):
        x, z, c = s // (ZH * NC), s // NC % ZH, s % NC
        t = ((x + dx) % NX * ZH + (z + dz) % ZH) * NC + (c ^ int(flip))
        pairs.append((s, t))
    return pairs


def shift(array, dx=0, dz=0, flip=False):
    return lax.ppermute(array, "seq", seq_perm(dx, dz, flip))


def norm_kernel(hist_ref, cand_ref, events_ref, requests_ref, out_ref, times_ref):
    for ref, first, count in ((hist_ref, 0, HIST), (cand_ref, HIST, CAND)):
        rows = ref[0].astype(F32)
        rows = rows - jnp.mean(rows, axis=-1, keepdims=True)
        spread = jnp.mean(rows * rows, axis=-1, keepdims=True)
        out_ref[first : first + count, :] = (rows * lax.rsqrt(spread + 1e-6)).astype(BF16)
    times_ref[...] = jnp.zeros_like(times_ref)
    times_ref[:, :HIST] = events_ref[...]
    times_ref[:, HIST:ROWS] = requests_ref[...]


def norm_rows(hist, cand, events, requests):
    return pl.pallas_call(
        norm_kernel,
        out_shape=[jax.ShapeDtypeStruct((ROWS, D), BF16), jax.ShapeDtypeStruct((1, 2 * HIST), I32)],
        in_specs=[VM] * 4,
        out_specs=[VM] * 2,
        cost_estimate=pl.CostEstimate(flops=8 * ROWS * D, bytes_accessed=4 * ROWS * D, transcendentals=0),
        name="norm_rows",
    )(hist, cand, events, requests)


def shards_kernel(tie_ref, proj_ref, shards_ref, part_ref, sem):
    x, z, core = position()
    column = pl.multiple_of((NC * z + core) % 4 * HD, HD)
    copy = pltpu.make_async_copy(
        proj_ref.at[pl.ds(pl.multiple_of(x * DEPTH, DEPTH), DEPTH), pl.ds(column, HD)], part_ref, sem
    )
    copy.start()
    copy.wait()
    for b in range(NB):
        shards_ref[b] = part_ref[...]


def make_shards(tie, w_proj):
    return pl.pallas_call(
        shards_kernel,
        out_shape=jax.ShapeDtypeStruct((NB, DEPTH, HD), BF16),
        in_specs=[HBM] * 2,
        out_specs=VM,
        scratch_shapes=[pltpu.VMEM((DEPTH, HD), BF16), pltpu.SemaphoreType.DMA(())],
        cost_estimate=pl.CostEstimate(flops=1 << 10, bytes_accessed=1 << 19, transcendentals=0),
        name="make_shards",
    )(tie, w_proj)


def merge_kernel(mine_ref, other_ref, wout_ref, *rest, bit):
    out_ref, wout_out = rest[-2:]
    count = mine_ref.shape[0]
    first = lax.axis_index("seq") >> bit & 1 == 0
    out_ref[:count] = jnp.where(first, mine_ref[...], other_ref[...])
    out_ref[count:] = jnp.where(first, other_ref[...], mine_ref[...])
    half = wout_out.shape[0]
    wout_out[...] = wout_ref[pl.ds(pl.multiple_of(position()[2] * half, half), half), :]


def merge(mine, other, bit, w_out, ties):
    return pl.pallas_call(
        functools.partial(merge_kernel, bit=bit),
        out_shape=[
            jax.ShapeDtypeStruct((2 * mine.shape[0], mine.shape[1]), mine.dtype),
            jax.ShapeDtypeStruct((w_out.shape[0] // NC, D), w_out.dtype),
        ],
        in_specs=[VM] * (3 + len(ties)),
        out_specs=[VM] * 2,
        compiler_params=params(6),
        cost_estimate=pl.CostEstimate(flops=1 << 12, bytes_accessed=1 << 16, transcendentals=0),
        name="merge",
    )(mine, other, w_out, *ties)


def prepare_kernel(tq_ref, col_ref):
    for i in range(QROWS // 128):
        col_ref[i * 128 : (i + 1) * 128, :] = jnp.transpose(jnp.broadcast_to(tq_ref[i : i + 1, :], (128, 128)))


def prepare(tq):
    return pl.pallas_call(
        prepare_kernel,
        out_shape=jax.ShapeDtypeStruct((QROWS, 128), I32),
        in_specs=[VM],
        out_specs=VM,
        compiler_params=params(4),
        cost_estimate=pl.CostEstimate(flops=2 << 20, bytes_accessed=1 << 20, transcendentals=0),
        name="prepare",
    )(tq)


def half_silu(half):
    return half + half * jnp.tanh(half)


HALF = NP // 2


HALF = NP // 2


def project_kernel(rows_ref, *refs):
    parts, (qh_ref, qc_ref, kv_ref, own_ref, gate_ref, rows, weights, sems) = refs[:NX], refs[NX:]
    x = position()[0]
    hist, cand = HALF * HIST, HALF * CAND
    copies = []
    for place in range(NP):
        step, at = place // HALF, place % HALF
        copies.append(
            (
                pltpu.make_async_copy(
                    rows_ref.at[place, :HIST, :], rows.at[step, at * HIST : (at + 1) * HIST, :], sems.at[0, place]
                ),
                pltpu.make_async_copy(
                    rows_ref.at[place, HIST:, :],
                    rows.at[step, hist + at * CAND : hist + (at + 1) * CAND, :],
                    sems.at[1, place],
                ),
            )
        )
        for copy in copies[-1]:
            copy.start()
    for m in range(NX):
        at = pl.multiple_of((x + OFF[m]) % NX * DEPTH, DEPTH)
        for kind in range(4):
            weights[pl.ds(at, DEPTH), kind * HD : (kind + 1) * HD] = parts[m][kind]
    for step in range(NP // HALF):
        for pair in copies[step * HALF : (step + 1) * HALF]:
            for copy in pair:
                copy.wait()
        mixed = jnp.dot(rows[step], weights[:, 2 * HD :], preferred_element_type=F32)
        mixed = half_silu(0.5 * mixed)
        queries, keys = mixed[:, :HD], mixed[:, HD:]
        scaled = (queries * (0.5 * HD**-0.5)).astype(BF16)
        hists, cands = slice(step * hist, (step + 1) * hist), slice(step * cand, (step + 1) * cand)
        qh_ref[hists, :] = scaled[:hist]
        qc_ref[cands, :] = scaled[hist:]
        kv_ref[hists, :HD] = keys[:hist].astype(BF16)
        dots = queries[hist:].astype(BF16).astype(F32) * keys[hist:].astype(BF16).astype(F32)
        dots = jnp.sum(dots, axis=-1, keepdims=True)
        own = half_silu(dots * (0.5 * HD**-0.5)).astype(BF16).astype(F32)
        mixed = jnp.dot(rows[step], weights[:, : 2 * HD], preferred_element_type=F32)
        mixed = half_silu(0.5 * mixed).astype(BF16)
        kv_ref[hists, HD:] = mixed[:hist, HD:]
        own_ref[cands, :] = own * mixed[hist:, HD:].astype(F32)
        for at in range(HALF):
            place = step * HALF + at
            gate_ref[place, :HIST, :] = mixed[at * HIST : (at + 1) * HIST, :HD]
            gate_ref[place, HIST:, :] = mixed[hist + at * CAND : hist + (at + 1) * CAND, :HD]


def project(rows, parts):
    return pl.pallas_call(
        project_kernel,
        in_specs=[HBM] + [VM] * NX,
        out_specs=[VM] * 5,
        scratch_shapes=[
            pltpu.VMEM((NP // HALF, HALF * ROWS, D), BF16),
            pltpu.VMEM((D, 4 * HD), BF16),
            pltpu.SemaphoreType.DMA((2, NP)),
        ],
        out_shape=[
            jax.ShapeDtypeStruct((QH, HD), BF16),
            jax.ShapeDtypeStruct((QC, HD), BF16),
            jax.ShapeDtypeStruct((KEYS, 2 * HD), BF16),
            jax.ShapeDtypeStruct((QC, HD), F32),
            jax.ShapeDtypeStruct((NP, ROWS, HD), BF16),
        ],
        compiler_params=params(50),
        cost_estimate=pl.CostEstimate(flops=2 * QROWS * D * 4 * HD, bytes_accessed=6 << 20, transcendentals=QROWS * 4 * HD),
        name="project",
    )(rows, *parts)


BLOCK = 256
TILES = (QROWS // 128) * NP
STEPS = QROWS // BLOCK
STEP_TILES = TILES // STEPS


def attend_kernel(count_ref, work_ref, base_ref, steps_ref, qh_ref, qc_ref, sums_in, col_ref, *rest, fresh, last, chunks, start):
    arrays = sum(len(chunk) for chunk in chunks)
    gate_ref = rest[-4]
    kvs, tks = list(rest[:arrays]), rest[arrays : arrays + len(chunks)]
    out_ref, sums_ref, half_ref = rest[-3:]
    if fresh:
        sums_ref[:QH, :] = jnp.zeros((QH, HD), F32)
        sums_ref[QH:, :] = sums_in[...]
    else:
        sums_ref[...] = sums_in[...]
    row = lax.broadcasted_iota(I32, (128, 128), 0)
    lane = lax.broadcasted_iota(I32, (128, 128), 1)
    x = position()[0]
    froms = [(x + OFF[start + n]) % NX for n in range(len(chunks))]

    def scores(n, block, slot):
        first = block * BLOCK
        begin = 0
        for kv in parts[n]:
            keys = kv.shape[0]
            queries = qc_ref[first - QH : first - QH + BLOCK, :] if first >= QH else qh_ref[first : first + BLOCK, :]
            half = lax.dot_general(
                queries, kv[:, :HD], (((1,), (1,)), ((), ())), preferred_element_type=F32
            )
            for i in range(BLOCK // 128):
                for j in range(keys // 128):
                    at = (start + n) * TILES + (block * (BLOCK // 128) + i) * NP + begin // 128 + j
                    half_ref[slot, i * 128 : (i + 1) * 128, begin + j * 128 : begin + (j + 1) * 128] = (
                        half[i * 128 : (i + 1) * 128, j * 128 : (j + 1) * 128] + base_ref[at]
                    )
            begin += keys

    def correct(n, block, slot):
        is_cand = block * BLOCK >= QH

        def tile(k, carry):
            code = work_ref[(start + n) * TILES + block * STEP_TILES + k]
            i, j = (code >> 3) & 1, code & 7
            time_low, time_high, place_low, place_high = [(code >> bit) & 15 for bit in (4, 8, 12, 16)]
            if True:
                rows = pl.ds(pl.multiple_of(i * 128, 128), 128)
                columns = pl.ds(pl.multiple_of(j * 128, 128), 128)
                first = pl.multiple_of(block * BLOCK + i * 128, 128)
                value = half_ref[slot, rows, columns]
                gap = col_ref[pl.ds(first, 128), :] - tks[n][pl.ds(j, 1), :]

                def time_step(level, value):
                    return value + jnp.where(gap >= (1 << (2 * level)), steps_ref[level], 0.0)

                value = lax.fori_loop(time_low, time_high, time_step, value)
                if is_cand:
                    gap2 = (LENGTH - froms[n] * KEYS - j * 128) - lane
                else:
                    gap2 = ((x - froms[n]) * KEYS + (block * (BLOCK // 128) + i - j) * 128) + row - lane

                def place_step(level, value):
                    return value + jnp.where(gap2 >= (1 << level), steps_ref[LEVELS + level], 0.0)

                value = lax.fori_loop(place_low, place_high, place_step, value)
                if not is_cand:
                    value = jnp.where(gap2 >= 0, value, MASKED)
                half_ref[slot, rows, columns] = value

            return carry

        lax.fori_loop(0, count_ref[(start + n) * STEPS + block], tile, 0)

    def combine(n, block, slot):
        first = block * BLOCK
        begin = 0
        total = sums_ref[first : first + BLOCK, :]
        for kv in parts[n]:
            keys = kv.shape[0]
            weights = half_silu(half_ref[slot, :, begin : begin + keys]).astype(BF16)
            total = total + jnp.dot(weights, kv[:, HD:], preferred_element_type=F32)
            begin += keys
        sums_ref[first : first + BLOCK, :] = total

    def sweep(n, blocks):
        for k, block in enumerate(blocks):
            scores(n, block, k % 2)
            if k > 0:
                combine(n, blocks[k - 1], (k - 1) % 2)
            correct(n, block, k % 2)
        combine(n, blocks[-1], (len(blocks) - 1) % 2)

    parts = []
    for chunk in chunks:
        parts.append([kvs.pop(0) for _ in chunk])
    for n in range(len(chunks)):

        @pl.when(froms[n] <= x)
        def _():
            sweep(n, list(range(QROWS // BLOCK)))

        @pl.when(froms[n] > x)
        def _():
            sweep(n, [QROWS // BLOCK - 1])

    if last:
        for place in range(NP):
            out_ref[place, :HIST, :HD] = sums_ref[place * HIST : (place + 1) * HIST, :].astype(BF16)
            out_ref[place, HIST:, :HD] = sums_ref[QH + place * CAND : QH + (place + 1) * CAND, :].astype(BF16)
            out_ref[place, :, HD:] = gate_ref[place]
    else:
        out_ref[...] = sums_ref[...]


def attend(tables, queries, sums, col, chunks, tks, start, gates=None):
    fresh, last = start == 0, gates is not None
    gates = [gates] if last else []
    kvs = [kv for chunk in chunks for kv in chunk]
    shapes = tuple(tuple(kv.shape[0] for kv in chunk) for chunk in chunks)
    keys = sum(kv.shape[0] for kv in kvs)
    return pl.pallas_call(
        functools.partial(attend_kernel, fresh=fresh, last=last, chunks=shapes, start=start),
        in_specs=[SM] * 4 + [VM] * (4 + len(kvs) + len(tks) + len(gates)),
        out_specs=VM,
        out_shape=jax.ShapeDtypeStruct((NP, ROWS, 2 * HD), BF16) if last else jax.ShapeDtypeStruct((QROWS, HD), F32),
        scratch_shapes=[pltpu.VMEM((QROWS, HD), F32), pltpu.VMEM((2, BLOCK, KEYS), F32)],
        compiler_params=params(16),
        cost_estimate=pl.CostEstimate(
            flops=16 * QROWS * keys * HD, bytes_accessed=4 * QROWS * keys, transcendentals=QROWS * keys
        ),
        name="attend",
    )(*tables, *queries, sums, col, *kvs, *tks, *gates)


def finish_kernel(hist_ref, cand_ref, pair_ref, mine_ref, other_ref, hist_out, cand_out, w_ref, sems):
    core = position()[2]
    copies = [
        pltpu.make_async_copy(mine_ref, w_ref.at[:, core], sems.at[0]),
        pltpu.make_async_copy(other_ref, w_ref.at[:, 1 - core], sems.at[1]),
    ]
    for copy in copies:
        copy.start()
    parts = [pair_ref[h, :, :HD].astype(F32) for h in range(HEADS)]
    center = sum(jnp.sum(part, axis=-1, keepdims=True) for part in parts) * (1.0 / D)
    parts = [part - center for part in parts]
    spread = sum(jnp.sum(part * part, axis=-1, keepdims=True) for part in parts) * (1.0 / D)
    scale = lax.rsqrt(spread + 1e-6)
    parts = [(part * scale * pair_ref[h, :, HD:].astype(F32)).astype(BF16) for h, part in enumerate(parts)]
    for copy in copies:
        copy.wait()
    total = jnp.dot(jnp.concatenate(parts, axis=1), w_ref[...].reshape(D, D), preferred_element_type=F32)
    hist_out[0] = (hist_ref[0].astype(F32) + total[:HIST]).astype(BF16)
    cand_out[0] = (cand_ref[0].astype(F32) + total[HIST:]).astype(BF16)


def finish(hist, cand, mine, other, pairs):
    return pl.pallas_call(
        finish_kernel,
        out_shape=[
            jax.ShapeDtypeStruct((1, HIST, D), BF16),
            jax.ShapeDtypeStruct((1, CAND, D), BF16),
        ],
        in_specs=[VM] * 3 + [HBM] * 2,
        out_specs=[VM, VM],
        scratch_shapes=[pltpu.VMEM((NB, NC, D // NB // NC, D), BF16), pltpu.SemaphoreType.DMA((2,))],
        compiler_params=params(12),
        cost_estimate=pl.CostEstimate(flops=2 * ROWS * D * D, bytes_accessed=4 << 20, transcendentals=0),
        name="finish",
    )(hist, cand, pairs, mine, other)


def gather_weights(shards, z):
    shards = lax.all_to_all(shards, "batch", 0, 0)
    return lax.dynamic_index_in_dim(shards.reshape(4, 2, DEPTH, HD), z // 2, axis=1, keepdims=False)


def body(history, candidates, event_times, request_times, w_proj, w_out, bias_steps):
    seq = lax.axis_index("seq")
    x, z, core = position()
    head = NC * z + core
    xs = jnp.stack([(x + off) % NX for off in OFF])

    n0, t0 = norm_rows(history, candidates, event_times, request_times)
    rows = lax.all_gather(n0, "seq", axis_index_groups=SAME_X)

    w0 = gather_weights(make_shards(t0, w_proj), z)
    w_parts = [w0, shift(w0, dx=1), shift(w0, dx=-1), shift(w0, dx=2)]

    times = t0
    order = (3, 4, 0, 1, 2)
    for bit in order:
        other = lax.ppermute(times, "seq", [(s, s ^ (1 << bit)) for s in range(NS)])
        if bit == order[-2]:
            times, w_mine = merge(times, other, bit, w_out, w_parts[1:])
            w_half = lax.all_gather(w_mine, "batch")
            w_other = shift(w_half, flip=True)
        else:
            first = seq >> bit & 1 == 0
            times = jnp.concatenate([jnp.where(first, times, other), jnp.where(first, other, times)], axis=0)
    times = times.reshape(ZH, NC, NX, 2 * HIST).transpose(2, 0, 1, 3).reshape(NX, NP, 2 * HIST)
    t8 = jnp.sum(jnp.where((x == jnp.arange(NX))[:, None, None], times, 0), axis=0)
    k0 = t8[:, :HIST]
    tks = [jnp.sum(jnp.where((xs[m] == jnp.arange(NX))[:, None, None], times[..., :HIST], 0), axis=0) for m in range(NX)]
    cand_times = t8[:, HIST:ROWS].reshape(QC // 128, 128)

    qh, qc, kv0, own, gates = project(rows, w_parts)

    steps = 0.5 * lax.dynamic_slice(bias_steps, (0, head), (2 * LEVELS, 1))[:, 0]
    level = jnp.arange(LEVELS, dtype=I32)
    tie = (kv0[0, 0] * 0).astype(I32)
    tk = jnp.stack(tks) + tie
    tq = jnp.concatenate([k0, cand_times, jnp.zeros((6, 128), I32)], axis=0) + tie
    first_q = jnp.concatenate([k0[:, 0], jnp.min(cand_times, axis=1)]) + tie
    last_q = jnp.concatenate([k0[:, -1], jnp.max(cand_times, axis=1)]) + tie

    def passed(gap, marks):
        return jnp.sum((gap[..., None] >= marks).astype(I32), axis=-1)

    time_low = passed(first_q[None, :, None] - tk[:, None, :, -1], 4**level)
    time_high = passed(last_q[None, :, None] - tk[:, None, :, 0], 4**level)
    blocks = jnp.arange(NP, dtype=I32)
    hist_gap = ((x - xs)[:, None, None] * NP + blocks[None, :, None] - blocks[None, None, :]) * HIST
    cand_gap = LENGTH - (xs[:, None, None] * NP + blocks[None, None, :]) * HIST
    cand_gap = jnp.broadcast_to(cand_gap, (NX, QC // 128, NP))
    place_low = passed(jnp.concatenate([hist_gap, cand_gap], axis=1) - (HIST - 1), 2**level)
    place_high = passed(jnp.concatenate([hist_gap + (HIST - 1), cand_gap], axis=1), 2**level)
    hidden = jnp.concatenate([hist_gap < 0, cand_gap < 0], axis=1)
    code = time_low | (time_high << 4) | (place_low << 8) | (place_high << 12)
    mixed = ~hidden & ((time_low != time_high) | (place_low != place_high))
    number = jnp.arange(STEP_TILES, dtype=I32)
    code = (code << 4 | number.reshape(BLOCK // 128, NP)[jnp.arange(QROWS // 128) % (BLOCK // 128)]).reshape(NX, STEPS, STEP_TILES)
    mixed = mixed.reshape(NX, STEPS, STEP_TILES)
    rank = jnp.sum(jnp.where(number[None, :] < number[:, None], mixed[..., None, :].astype(I32), 0), axis=-1)
    spot = mixed[..., None] & (rank[..., None] == number)
    works = jnp.sum(jnp.where(spot, code[..., None], 0), axis=-2).reshape(NX, TILES)
    counts = jnp.sum(mixed.astype(I32), axis=-1)
    base = jnp.sum(jnp.where(time_low[..., None] > level, steps[:LEVELS], 0.0), axis=-1)
    base = base + jnp.sum(jnp.where(place_low[..., None] > level, steps[LEVELS:], 0.0), axis=-1)
    base = jnp.where(hidden, MASKED, base).reshape(NX, TILES)
    col = prepare(tq)
    tables = (counts.reshape(-1), works.reshape(-1), base.reshape(-1), steps)

    queries = (qh, qc)
    kv1, kv2 = shift(kv0, dx=1), shift(kv0, dx=-1)
    part = KEYS // 2
    kv3a, kv3b = shift(kv1[:part], dx=1), shift(kv2[part:], dx=-1)
    sums = attend(tables, queries, own, col, [[kv0]], tks[:1], 0)
    sums = attend(tables, queries, sums, col, [[kv1], [kv2]], tks[1:3], 1)
    att = attend(tables, queries, sums, col, [[kv3a, kv3b]], tks[3:], 3, gates)
    atts = lax.all_to_all(att, "seq", 0, 0, axis_index_groups=SAME_X)
    return tuple(finish(history, candidates, w_half, w_other, atts))


def solution(mesh):
    in_specs = (
        P("batch", "seq", None),
        P("batch", "seq", None),
        P("batch", "seq"),
        P("batch", "seq"),
        P(None, "batch"),
        P("batch", None),
        P(),
    )
    out_specs = (P("batch", "seq", None), P("batch", "seq", None))
    return jax.shard_map(body, mesh=mesh, in_specs=in_specs, out_specs=out_specs, check_vma=False)
```
